32 devices in a mesh: dp: 8 (over z, x), chan: 4 (over y, core).
Axes of the slice: x: 2, y: 2, z: 4, core: 2. Of those that a mesh axis runs over, the one named last changes fastest.
Arguments:
- x_maps: bfloat16 [64, 16, 16, 256], P('dp', None, None, 'chan'), may hold values from -6 to 6
- timesteps: int32 [64], P('dp'), may hold values from 0 to 999
- counts: int32 [8], P('dp'), may hold values from 2 to 8, as said below
- emb_table: bfloat16 [1000, 512], replicated, may hold values from -5 to 5
- w_first: bfloat16 [3, 3, 256, 256], P(None, None, None, 'chan'), may hold values from -0.125 to 0.125
- w_second: bfloat16 [3, 3, 256, 256], P(None, None, None, 'chan'), may hold values from -0.125 to 0.125
- w_embed: bfloat16 [512, 256], P(None, 'chan'), may hold values from -0.25 to 0.25
- w_qkv: bfloat16 [256, 3, 256], P(None, None, 'chan'), may hold values from -0.375 to 0.375
- w_out: bfloat16 [256, 256], P(None, 'chan'), may hold values from -1.5 to 1.5
- gain_one: bfloat16 [256], P('chan'), may hold values from 0.099609375 to 1.8984375
- shift_one: bfloat16 [256], P('chan'), may hold values from -3 to 3
- gain_two: bfloat16 [256], P('chan'), may hold values from 0.099609375 to 1.8984375
- shift_two: bfloat16 [256], P('chan'), may hold values from -3 to 3
- gain_three: bfloat16 [256], P('chan'), may hold values from 0.099609375 to 1.8984375
- shift_three: bfloat16 [256], P('chan'), may hold values from -3 to 3
- cotangent: bfloat16 [64, 16, 16, 256], P('dp', None, None, 'chan'), may hold values from -6 to 6
Outputs:
- y_maps: bfloat16 [64, 16, 16, 256], P('dp', None, None, 'chan')
- d_maps: bfloat16 [64, 16, 16, 256], P('dp', None, None, 'chan')
- d_table: float32 [1000, 512], replicated
- d_first: float32 [3, 3, 256, 256], P(None, None, None, 'chan')
- d_second: float32 [3, 3, 256, 256], P(None, None, None, 'chan')
- d_embed: float32 [512, 256], P(None, 'chan')
- d_qkv: float32 [256, 3, 256], P(None, None, 'chan')
- d_out: float32 [256, 256], P(None, 'chan')
- d_gain_one: float32 [256], P('chan')
- d_shift_one: float32 [256], P('chan')
- d_gain_two: float32 [256], P('chan')
- d_shift_two: float32 [256], P('chan')
- d_gain_three: float32 [256], P('chan')
- d_shift_three: float32 [256], P('chan')
The draws below stay inside these ranges and needn't reach their ends.
Inputs may be any that keep to these rules, and one draw needn't show every extreme that they name: `counts`: slots of an index of dp at or beyond its count are unused; one index of dp has a full count of 8, another the least count.
All inputs are finite; a program needn't handle non-finite values.
Results may differ from the reference program's by a relative error of at most 0.04.
Values may be sent and summed in bfloat16 or wider, within the bound.
A program may use at most 128 MiB of HBM per device.

```python
import jax
import jax.numpy as jnp
from jax import lax

C = 256
EMB = 512
TSTEPS = 1000
GROUPS = 32
SIDE = 16
CAP = 8
MAPS = 64
N_DP = 8


def draw_counts(key, part):
    key = jax.random.fold_in(key, 11)
    first, second, third = jax.random.split(key, 3)
    least = max(CAP // 4, 1)
    values = jax.random.randint(first, (N_DP,), least, CAP + 1)
    top = jax.random.randint(second, (), 0, N_DP)
    offset = jax.random.randint(third, (), 1, max(N_DP, 2))
    bottom = (top + offset) % N_DP
    places = jnp.arange(N_DP)
    values = jnp.where(places == bottom, least, values)
    values = jnp.where(places == top, CAP, values)
    return values.astype(jnp.int32)


def touch_ends(entries, stream_key, low, top_value):
    shape = entries.shape
    place = [jax.random.randint(jax.random.fold_in(stream_key, axis), (), 0, shape[axis]) for axis in range(len(shape))]
    entries = entries.at[tuple(place)].set(low)
    longest = shape.index(max(shape))
    place[longest] = (place[longest] + 1) % shape[longest]
    return entries.at[tuple(place)].set(top_value)


def shard_levels(own_key, shape, cuts, low, top_value):
    factor_of, own = 1.0, jax.random.fold_in(own_key, 6)
    for axis_at, blocks in cuts:
        draws = jnp.exp(jax.random.uniform(jax.random.fold_in(own, axis_at), (blocks,), jnp.float32, low / len(cuts), top_value / len(cuts)))
        factor_of = factor_of * jnp.repeat(draws, shape[axis_at] // blocks).reshape([-1 if axis == axis_at else 1 for axis in range(len(shape))])
    return factor_of


def normal_values(stream_key, shape, scale, most, pieces=(), held_as=jnp.bfloat16):
    array = jax.random.normal(stream_key, shape, jnp.float32) * scale
    if len(pieces) > 0:
        array = shard_levels(stream_key, shape, pieces, -0.22, 0.18) * array
    return jnp.clip(array, min=-most, max=most).astype(held_as)


def setup_inputs(seed: int = 0) -> dict:
    arg_keys = jax.random.split(jax.random.key(seed), 17)
    x_maps = normal_values(arg_keys[0], (MAPS, SIDE, SIDE, C), 1.0, 6.0, ((0, 8), (3, 4)))
    timesteps = touch_ends(jax.random.randint(arg_keys[1], (MAPS,), 0, TSTEPS), jax.random.fold_in(arg_keys[1], 1), 0, TSTEPS - 1).astype(jnp.int32)
    counts = draw_counts(jax.random.fold_in(arg_keys[16], 71), 0)
    emb_table = normal_values(arg_keys[3], (TSTEPS, EMB), 1.0, 5.0)
    w_first = normal_values(arg_keys[4], (3, 3, C, C), (9 * C) ** -0.5, 0.125, ((3, 4),))
    w_second = normal_values(arg_keys[5], (3, 3, C, C), (9 * C) ** -0.5, 0.125, ((3, 4),))
    w_embed = normal_values(arg_keys[6], (EMB, C), EMB ** -0.5, 0.25, ((1, 4),))
    w_qkv = normal_values(arg_keys[7], (C, 3, C), C ** -0.5, 0.375, ((2, 4),))
    w_out = normal_values(arg_keys[8], (C, C), (C // 16) ** -0.5, 1.5, ((1, 4),))
    gain_one = jnp.clip(1.0 + 0.18 * jax.random.normal(arg_keys[9], (C,), jnp.float32), 0.099609375, 1.8984375).astype(jnp.bfloat16)
    shift_one = normal_values(arg_keys[10], (C,), 0.5, 3.0, ((0, 4),))
    gain_two = jnp.clip(1.0 + 0.18 * jax.random.normal(arg_keys[11], (C,), jnp.float32), 0.099609375, 1.8984375).astype(jnp.bfloat16)
    shift_two = normal_values(arg_keys[12], (C,), 0.5, 3.0, ((0, 4),))
    gain_three = jnp.clip(1.0 + 0.18 * jax.random.normal(arg_keys[13], (C,), jnp.float32), 0.099609375, 1.8984375).astype(jnp.bfloat16)
    shift_three = normal_values(arg_keys[14], (C,), 0.5, 3.0, ((0, 4),))
    cotangent = normal_values(arg_keys[15], (MAPS, SIDE, SIDE, C), 1.0, 6.0, ((0, 8), (3, 4)))
    return {"x_maps": x_maps, "timesteps": timesteps, "counts": counts, "emb_table": emb_table, "w_first": w_first, "w_second": w_second, "w_embed": w_embed, "w_qkv": w_qkv, "w_out": w_out, "gain_one": gain_one, "shift_one": shift_one, "gain_two": gain_two, "shift_two": shift_two, "gain_three": gain_three, "shift_three": shift_three, "cotangent": cotangent}


@jax.custom_vjp
def low(v):
    return lax.optimization_barrier(v.astype(jnp.bfloat16)).astype(jnp.float32)

@jax.custom_vjp
def low_back(v):
    return v

def low_keep(v):
    return (low(v), None)

def low_pass(kept, grad):
    return (grad,)

def back_keep(v):
    return (v, None)

def back_low(kept, grad):
    return (low(grad),)
low.defvjp(low_keep, low_pass)
low_back.defvjp(back_keep, back_low)
HIGH = lax.Precision.HIGHEST
EPS = 1e-06

def group_norm(values, gain, shift):
    count = values.shape[0]
    width = values.shape[-1]
    grouped = values.reshape(count, SIDE * SIDE, GROUPS, width // GROUPS)
    center = lax.optimization_barrier(jnp.mean(grouped, axis=(1, 3), keepdims=True))
    spread = lax.optimization_barrier(jnp.mean(jnp.square(grouped - center), axis=(1, 3), keepdims=True))
    normed = ((grouped - center) * lax.rsqrt(spread + EPS)).reshape(values.shape)
    return normed * gain + shift

def conv_same(inputs, weight):
    return lax.conv_general_dilated(inputs, weight, (1, 1), 'SAME', dimension_numbers=('NHWC', 'HWIO', 'NHWC'), precision=HIGH)

def block_forward(x_block, t_block, live_block, params):
    table, w_first, w_second, w_embed, w_qkv, w_out, gain_one, shift_one, gain_two, shift_two, gain_three, shift_three = params
    count = x_block.shape[0]
    temb = jnp.take(table, t_block, axis=0)
    act_one = low(jax.nn.silu(group_norm(x_block, gain_one, shift_one)))
    hidden_one = low_back(conv_same(act_one, w_first))
    embed = low_back(jnp.dot(low(jax.nn.silu(temb)), w_embed, precision=HIGH))
    hsum = hidden_one + embed[:, None, None, :]
    act_two = low(jax.nn.silu(group_norm(hsum, gain_two, shift_two)))
    hidden_two = low_back(conv_same(act_two, w_second))
    resid = x_block + hidden_two
    act_three = low(group_norm(resid, gain_three, shift_three)).reshape(count, SIDE * SIDE, C)
    proj = jnp.einsum('npc,cjd->jnpd', act_three, w_qkv, precision=HIGH)
    proj = low_back(low(proj))
    scores = low_back(jnp.einsum('nqd,nkd->nqk', proj[0], proj[1], precision=HIGH)) * C ** (-0.5)
    probs = jax.nn.softmax(scores, axis=-1)
    mixed = jnp.einsum('nqk,nkd->nqd', low(probs), proj[2], precision=HIGH)
    mixed = low_back(low(mixed))
    outcome = jnp.einsum('npc,cd->npd', mixed, w_out, precision=HIGH).reshape(x_block.shape)
    return (resid + outcome) * live_block[:, None, None, None]

def reference(x_maps, timesteps, counts, emb_table, w_first, w_second, w_embed, w_qkv, w_out, gain_one, shift_one, gain_two, shift_two, gain_three, shift_three, cotangent):
    slots = jnp.arange(MAPS, dtype=jnp.int32)
    live = (slots % CAP < jnp.take(counts, slots // CAP)).astype(jnp.float32)
    floats = [v.astype(jnp.float32) for v in (x_maps, emb_table, w_first, w_second, w_embed, w_qkv, w_out, gain_one, shift_one, gain_two, shift_two, gain_three, shift_three)]
    t_groups = timesteps.reshape(N_DP, CAP)
    live_groups = live.reshape(N_DP, CAP)

    def forward(x_all, *params):
        x_groups = x_all.reshape((N_DP, CAP) + x_all.shape[1:])
        step = jax.checkpoint(lambda items: block_forward(items[0], items[1], items[2], params))
        result = lax.map(step, (x_groups, t_groups, live_groups))
        return result.reshape(x_all.shape)
    out, pull = jax.vjp(forward, *floats)
    grads = pull(cotangent.astype(jnp.float32))
    return (out.astype(jnp.bfloat16), grads[0].astype(jnp.bfloat16), grads[1], grads[2], grads[3], grads[4], grads[5], grads[6], grads[7], grads[8], grads[9], grads[10], grads[11], grads[12])
```

```python
import functools
from types import SimpleNamespace

import jax
import jax.numpy as jnp
from jax import lax
from jax.experimental import pallas as pl
from jax.experimental.pallas import tpu as pltpu
from jax.sharding import PartitionSpec as P

F32 = jnp.float32
BF = jnp.bfloat16
MESH = pl.DeviceIdType.MESH
EPS = 1e-06
GROUPS = 32
CHAN = 4
ROWS = 256
C = 256
SL = C // CHAN
GAP = 16
STEP = ROWS + GAP
TALL = 2 * ROWS + GAP
CH = 32
COUNT = ROWS * (C // GROUPS)


def dot(a, b):
    return jnp.dot(a, b, preferred_element_type=F32)


def dot_nt(a, b):
    return lax.dot_general(a, b, (((1,), (1,)), ((), ())), preferred_element_type=F32)


def sigmoid(u):
    return 0.5 * jnp.tanh(0.5 * u) + 0.5


def fold(v):
    return v.reshape(v.shape[0] // 8, 8, v.shape[1]).sum(axis=0)


def group_total(rows, bd):
    at = lax.broadcasted_iota(jnp.int32, (8, C), 0)
    stack = jnp.zeros((8, C), F32)
    for i, row in enumerate(rows):
        stack = jnp.where(at == i, row, stack)
    high = stack.astype(BF).astype(F32)
    rest = stack - high
    mid = rest.astype(BF).astype(F32)
    parts = jnp.concatenate([high, mid, rest - mid, jnp.zeros((8, C), F32)], axis=0)
    total = dot(parts.astype(BF), bd)
    total = total[0:8] + total[8:16] + total[16:24]
    return [total[i : i + 1] for i in range(len(rows))]


def chunk_at(i):
    return pl.multiple_of(i * CH, CH)


def passes(body, carry=None):
    carry = (0, 0) if carry is None else carry

    def step(i, held):
        return tuple(body(m, chunk_at(i), held[m]) for m in range(2))

    return lax.fori_loop(0, ROWS // CH, step, carry)


def zero_pair():
    return (jnp.zeros((8, C), F32), jnp.zeros((8, C), F32))


def col(v):
    return jnp.sum(v, axis=0, keepdims=True)


def write_shift(dst, m, at, value, forward):
    place = lax.broadcasted_iota(jnp.int32, (CH, C), 0) % 16
    before = jnp.where(place == 0, 0.0, pltpu.roll(value, 1, 0))
    after = jnp.where(place == 15, 0.0, pltpu.roll(value, CH - 1, 0))
    first, last = (before, after) if forward else (after, before)
    rows = pl.ds(pl.multiple_of(at + (GAP + m * STEP), 16), CH)
    dst[rows, 0:C] = first.astype(BF)
    dst[rows, C : 2 * C] = value.astype(BF)
    dst[rows, 2 * C : 3 * C] = last.astype(BF)


def norm_forward(load, n_ref, gain, shift, bd, emit):
    def sums(m, at, held):
        return held + fold(load(m, at))

    total = passes(sums, zero_pair())
    mean = group_total([col(t) for t in total], bd)
    mean = [v * (1.0 / COUNT) for v in mean]

    def squares(m, at, held):
        d = load(m, at) - mean[m]
        return held + fold(d * d)

    total = passes(squares, zero_pair())
    var = group_total([col(t) for t in total], bd)
    rstd = [lax.rsqrt(v * (1.0 / COUNT) + EPS) for v in var]

    def last(m, at, held):
        n = (load(m, at) - mean[m]) * rstd[m]
        n_ref[pl.ds(pl.multiple_of(at + m * ROWS, CH), CH), :] = n
        emit(m, at, n * gain + shift)
        return held

    passes(last)
    return rstd


def norm_back(d_ref, n_ref, gain, shift, rstd, bd, active, e_ref, e_at, emit):
    def rows(m, at):
        return pl.ds(pl.multiple_of(at + m * STEP, 16), CH)

    def first(m, at, held):
        d = d_ref[rows(m, at), :]
        n = n_ref[pl.ds(pl.multiple_of(at + m * ROWS, CH), CH), :]
        if active:
            u = n * gain + shift
            s = sigmoid(u)
            d = d * (s * (1.0 + u * (1.0 - s)))
            d_ref[rows(m, at), :] = d
        return (held[0] + fold(d), held[1] + fold(d * n))

    total = passes(first, (zero_pair(), zero_pair()))
    ones = [col(t[0]) for t in total]
    twos = [col(t[1]) for t in total]
    e_ref[e_at : e_at + 1, :] = twos[0] + twos[1]
    e_ref[e_at + 1 : e_at + 2, :] = ones[0] + ones[1]
    means = group_total([gain * v for v in ones + twos], bd)
    means = [v * (1.0 / COUNT) for v in means]

    def second(m, at, held):
        d = d_ref[rows(m, at), :]
        n = n_ref[pl.ds(pl.multiple_of(at + m * ROWS, CH), CH), :]
        return emit(m, at, rstd[m] * (d * gain - means[m] - n * means[2 + m]), held)

    return second


def unpack(low, high):
    lane = lax.broadcasted_iota(jnp.int32, low.shape, 1)
    first = jnp.where(lane < SL, low, pltpu.roll(high, SL, 1))
    second = jnp.where(lane < SL, pltpu.roll(low, SL, 1), high)
    return first, second


def conv_forward(a_ref, w_ref, h_ref, ready):
    for row in range(3):
        ready(row)
        total = None
        for c in range(3):
            part = dot_nt(a_ref[16 * row : 16 * row + TALL, C * c : C * c + C], w_ref[3 * row + c])
            total = part if total is None else total + part
        h_ref[...] = total if row == 0 else h_ref[...] + total


def conv_back(d_ref, w_ref, h_ref):
    for row in range(3):
        at = 16 * (2 - row)
        w = w_ref[3 * row : 3 * row + 3].reshape(3 * C, C)
        part = dot(d_ref[at : at + TALL, :], w)
        h_ref[...] = part if row == 0 else h_ref[...] + part


def conv_weight(a_ref, turned, dw_ref, row):
    for c in range(3):
        total = None
        for m in range(2):
            at = 16 * row + STEP * m
            part = dot(turned[m], a_ref[at : at + ROWS, C * c : C * c + C])
            total = part if total is None else total + part
        dw_ref[3 * row + c] = total.astype(BF)


class Links:
    def __init__(self, send, recv, own):
        self.send, self.recv, self.own = send, recv, own
        self.used, self.local = 0, 0
        self.sent = []

    def remote(self, src, dst, device):
        at = self.used
        self.used += 1
        copy = pltpu.make_async_remote_copy(
            src_ref=src, dst_ref=dst, send_sem=self.send.at[at], recv_sem=self.recv.at[at],
            device_id=device, device_id_type=MESH)
        copy.start()
        self.sent.append(copy)
        return copy

    def here(self, src, dst):
        copy = pltpu.make_async_copy(src, dst, self.own.at[self.local])
        self.local += 1
        copy.start()
        return copy

    def close(self):
        for copy in self.sent:
            copy.wait_send()


def block_sizes(n_dp):
    team = min(8, n_dp)
    return team, n_dp // team


class Reduction:
    def __init__(self, at, links, grad, out, work):
        self.at, self.links, self.grad, self.out, self.work = at, links, grad, out, work
        self.taps = grad.shape[0]

    def rows_of(self, y, core):
        return pl.ds(pl.multiple_of(SL * (2 * y + core), SL), SL)

    def core(self):
        at, w = self.at, self.work
        self.waits = [
            self.links.remote(self.grad.at[:, self.rows_of(y, 1 - at.core), :], w.rc.at[y], at.sibling)
            for y in range(2)]

    def cross(self):
        at, w = self.at, self.work
        for copy in self.waits:
            copy.wait_recv()
        far = 1 - at.y
        for t in range(self.taps):
            w.sy[t] = (self.grad[t, self.rows_of(far, at.core), :].astype(F32) + w.rc[far, t].astype(F32)).astype(BF)
        self.waits = [self.links.remote(w.sy, w.ry, at.across)]

    def piece(self, ref, p):
        at = self.at
        span = ref.shape[1] // (at.team // 2)
        half, quarter = p // (at.team // 2), p % (at.team // 2)
        return ref.at[half, pl.ds(pl.multiple_of(span * quarter, span), span), :]

    def scatter(self):
        at, w = self.at, self.work
        for copy in self.waits:
            copy.wait_recv()
        for t in range(self.taps):
            whole = (self.grad[t, self.rows_of(at.y, at.core), :].astype(F32) + w.rc[at.y, t].astype(F32)
                     + w.ry[t].astype(F32)).astype(BF)
            for half in range(2):
                w.sl[half, SL * t : SL * t + SL, :] = whole[:, 128 * half : 128 * half + 128]
        self.waits = []
        for s in range(1, at.team):
            p = (at.rank + s) % at.team
            self.waits.append(self.links.remote(self.piece(w.sl, p), w.rr.at[s], at.mate(p)))

    def spread(self):
        at, w = self.at, self.work
        for copy in self.waits:
            copy.wait_recv()
        total = self.piece(w.sl, at.rank)[...].astype(F32)
        for s in range(1, at.team):
            total = total + w.rr[s].astype(F32)
        w.pc[...] = total.astype(BF)
        if at.teams > 1:
            copies = [self.links.here(w.pc, w.rt.at[at.lead])]
            for s in range(1, at.teams):
                other = (at.lead + s) % at.teams
                copies.append(self.links.remote(w.pc, w.rt.at[at.lead], at.device(other * at.team + at.rank)))
            copies[0].wait()
            for copy in copies[1:]:
                copy.wait_recv()
                copy.wait_send()
                self.links.sent = [c for c in self.links.sent if c is not copy]
            total = w.rt[0].astype(F32)
            for s in range(1, at.teams):
                total = total + w.rt[s].astype(F32)
            w.pc[...] = total.astype(BF)
        target = self.piece(self.out, at.rank)
        self.own = self.links.here(w.pc, target)
        self.waits = []
        for s in range(1, at.team):
            self.waits.append(self.links.remote(w.pc, target, at.mate((at.rank + s) % at.team)))

    def finish(self):
        self.own.wait()
        for copy in self.waits:
            copy.wait_recv()


ITEMS = (("ga", 4), ("gb", 9), ("gc", 3), ("gd", 3), ("ge", 3))


def mega(n_dp, names, *refs):
    r = SimpleNamespace(**dict(zip(names, refs)))
    team, teams = block_sizes(n_dp)
    dp, chan = lax.axis_index("dp"), lax.axis_index("chan")
    core, y = chan % 2, chan // 2
    sibling, across, corner = (dp, 2 * y + 1 - core), (dp, 2 * (1 - y) + core), (dp, 2 * (1 - y) + 1 - core)
    quads = (sibling, across, corner)
    rank, lead = dp % team, dp // team
    at = SimpleNamespace(
        core=core, y=y, sibling=sibling, across=across, team=team, teams=teams, rank=rank, lead=lead,
        mate=lambda p: (lead * team + p, chan), device=lambda p: (p, chan))
    links = Links(r.send, r.recv, r.own)

    def others():
        return [(lax.rem(dp + s, n_dp), chan) for s in range(1, n_dp)]

    loads = SimpleNamespace(x=links.here(r.x, r.xl), dy=links.here(r.dy, r.dyl))
    barrier = pltpu.get_barrier_semaphore()
    for device in quads:
        pl.semaphore_signal(barrier, inc=1, device_id=device, device_id_type=MESH)
    for device in others():
        pl.semaphore_signal(barrier, inc=1, device_id=device, device_id_type=MESH)
    mine = pl.ds(pl.multiple_of(SL * chan, SL), SL)
    fill = [
        links.here(r.w1, r.w1g.at[:, mine, :]), links.here(r.we, r.weg.at[mine, :]),
        links.here(r.w2, r.w2g.at[:, mine, :]), links.here(r.wq, r.wqg.at[0:3, mine, :]),
        links.here(r.wo, r.wqg.at[3, mine, :])]

    at_row = lax.broadcasted_iota(jnp.int32, (C, C), 0) // (C // GROUPS)
    at_col = lax.broadcasted_iota(jnp.int32, (C, C), 1) // (C // GROUPS)
    r.bd[...] = jnp.where(at_row == at_col, 1.0, 0.0).astype(BF)
    for ref in (r.a1, r.a2, r.dd):
        for gap in range(3):
            ref[gap * STEP : gap * STEP + GAP, :] = jnp.zeros((GAP, 3 * C), BF)
    row8 = lax.broadcasted_iota(jnp.int32, (8, 128), 0)
    times = jnp.zeros((8, 128), F32)
    for i in range(8):
        times = jnp.where(row8 == i, r.ts[i].astype(F32), times)
    r.tl[...] = times
    r.pg[chan] = r.par[...]

    def pack(src, dst):
        for k in range(CHAN):
            for half in range(2):
                rows = slice(128 * half, 128 * half + 128)
                both = jnp.concatenate([src[2 * k, rows, :].astype(F32), src[2 * k + 1, rows, :].astype(F32)], axis=1)
                dst[k, rows, :] = both.astype(BF)

    loads.x.wait()
    pack(r.xl, r.xp)
    r.xg[chan] = r.xp[chan]
    pl.semaphore_wait(barrier, CHAN - 1 + n_dp - 1)

    moves_x = [links.remote(r.xp.at[d[1]], r.xg.at[chan], d) for d in quads]
    moves_par = [links.remote(r.par, r.pg.at[chan], d) for d in quads]

    def share(src, dst):
        return [links.remote(src, dst, d) for d in (sibling, across)]

    def relay(moves, piece):
        moves[1].wait_recv()
        moves.append(links.remote(piece, piece, sibling))

    def landed(moves):
        moves[0].wait_recv()
        moves[2].wait_recv()

    far = pl.ds(pl.multiple_of(SL * (2 * (1 - y) + core), SL), SL)

    def share_conv(w, g):
        return [share(w.at[3 * row : 3 * row + 3], g.at[3 * row : 3 * row + 3, mine, :]) for row in range(3)]

    moves_w1 = share_conv(r.w1, r.w1g)
    moves_we = share(r.we, r.weg.at[mine, :])
    moves_w2 = share_conv(r.w2, r.w2g)
    moves_wq = share(r.wq, r.wqg.at[0:3, mine, :])
    moves_wo = share(r.wo, r.wqg.at[3, mine, :])
    loads.dy.wait()
    pack(r.dyl, r.dyp)
    r.dyg[chan] = r.dyp[chan]
    moves_dy = [links.remote(r.dyp.at[d[1]], r.dyg.at[chan], d) for d in quads]
    tall_own = links.here(r.tl, r.tall.at[dp])
    moves_t = [links.remote(r.tl, r.tall.at[dp], d) for d in others()]

    steps = r.table.shape[0]
    own_t = jnp.broadcast_to(times[:, 0:1], (8, steps))
    hot = jnp.where(own_t == lax.broadcasted_iota(jnp.int32, (8, steps), 1).astype(F32), 1.0, 0.0)
    hot = jnp.concatenate([hot, jnp.zeros((8, steps), F32)], axis=0).astype(BF)
    temb = dot(hot, r.table[...])
    tsil = (temb * sigmoid(temb)).astype(BF)

    bd = r.bd[...]
    for copy in moves_x + moves_par:
        copy.wait_recv()
    for b in range(2):
        first, _ = unpack(r.pg[2 * b], r.pg[2 * b + 1])
        r.pa[:, 128 * b : 128 * b + 128] = first
    par = r.pa[...]
    gain1, shift1, gain2, shift2, gain3, shift3 = [par[i : i + 1] for i in range(6)]

    def spread_out(src, at, dst, scale=None):
        for b in range(2):
            pair = unpack(src[2 * b, pl.ds(at, CH), :].astype(F32), src[2 * b + 1, pl.ds(at, CH), :].astype(F32))
            for m in range(2):
                value = pair[m] if scale is None else pair[m] * scale[m]
                dst[pl.ds(pl.multiple_of(at + m * ROWS, CH), CH), 128 * b : 128 * b + 128] = value.astype(dst.dtype)

    def open_x(i, held):
        spread_out(r.xg, chunk_at(i), r.xf)
        return held

    lax.fori_loop(0, ROWS // CH, open_x, 0)

    def rows_of(m, at):
        return pl.ds(pl.multiple_of(at + m * ROWS, CH), CH)

    def rows_gap(m, at):
        return pl.ds(pl.multiple_of(at + m * STEP, 16), CH)

    def to_shift(dst):
        def emit(m, at, u):
            write_shift(dst, m, at, u * sigmoid(u), True)
        return emit

    rstd1 = norm_forward(lambda m, at: r.xf[rows_of(m, at), :], r.n1, gain1, shift1, bd, to_shift(r.a1))
    for copy in fill:
        copy.wait()
    for row in range(3):
        relay(moves_w1[row], r.w1g.at[3 * row : 3 * row + 3, far, :])
    relay(moves_we, r.weg.at[far, :])
    conv_forward(r.a1, r.w1g, r.h, lambda row: landed(moves_w1[row]))
    landed(moves_we)
    for row in range(3):
        relay(moves_w2[row], r.w2g.at[3 * row : 3 * row + 3, far, :])
    r.emb[0:16, :] = dot_nt(tsil, r.weg[...])
    emb = [r.emb[pl.ds(2 * chan + m, 1), :] for m in range(2)]
    we_out = links.here(r.weg, r.weo)

    rstd2 = norm_forward(lambda m, at: r.h[rows_gap(m, at), :] + emb[m], r.n2, gain2, shift2, bd, to_shift(r.a2))
    relay(moves_wq, r.wqg.at[0:3, far, :])
    relay(moves_wo, r.wqg.at[3, far, :])
    conv_forward(r.a2, r.w2g, r.h, lambda row: landed(moves_w2[row]))

    def load_resid(m, at):
        return r.xf[rows_of(m, at), :] + r.h[rows_gap(m, at), :]

    def to_a3(m, at, u):
        r.a3[rows_of(m, at), :] = u.astype(BF)

    rstd3 = norm_forward(load_resid, r.n3, gain3, shift3, bd, to_a3)
    landed(moves_wq)
    landed(moves_wo)
    for j, ref in enumerate((r.q, r.k, r.v)):
        ref[...] = dot_nt(r.a3[...], r.wqg[j]).astype(BF)
    for copy in moves_dy:
        copy.wait_recv()
    count = r.cnt[0]
    live = [jnp.where(2 * chan + m < count, 1.0, 0.0).astype(F32) for m in range(2)]

    def open_dy(i, held):
        spread_out(r.dyg, chunk_at(i), r.g, live)
        return held

    lax.fori_loop(0, ROWS // CH, open_dy, 0)
    scale = C ** (-0.5)
    half = [slice(0, ROWS), slice(ROWS, 2 * ROWS)]
    for m in range(2):
        s = dot_nt(r.q[half[m], :], r.k[half[m], :]) * scale
        p = jnp.exp(s - jnp.max(s, axis=1, keepdims=True))
        p = p * (1.0 / jnp.sum(p, axis=1, keepdims=True))
        r.p[half[m], :] = p
        r.pb[half[m], :] = p.astype(BF)
        r.o[half[m], :] = dot(p.astype(BF), r.v[half[m], :]).astype(BF)
    r.big[...] = dot_nt(r.o[...], r.wqg[3])

    def pack_out(at, pair, dst):
        for b in range(2):
            even, odd = unpack(*(v[:, 128 * b : 128 * b + 128] for v in pair))
            dst[2 * b, pl.ds(at, CH), :] = even.astype(BF)
            dst[2 * b + 1, pl.ds(at, CH), :] = odd.astype(BF)

    def to_y(i, held):
        at = chunk_at(i)
        pack_out(at, [(load_resid(m, at) + r.big[rows_of(m, at), :]) * live[m] for m in range(2)], r.yp)
        return held

    lax.fori_loop(0, ROWS // CH, to_y, 0)
    own_y = links.here(r.yp.at[chan], r.yo.at[chan])
    moves_y = [links.remote(r.yp.at[d[1]], r.yo.at[chan], d) for d in quads]

    for m in range(2):
        r.turn[m] = r.g[half[m], :].T
    r.dqo[3] = (dot(r.turn[0], r.o[half[0], :]) + dot(r.turn[1], r.o[half[1], :])).astype(BF)
    r.do[...] = dot(r.g[...], r.wqg[3]).astype(BF)
    for m in range(2):
        dp_m = dot_nt(r.do[half[m], :], r.v[half[m], :])
        p = r.p[half[m], :]
        ds = (p * (dp_m - jnp.sum(p * dp_m, axis=1, keepdims=True)) * scale).astype(BF)
        r.dv[half[m], :] = dot(r.pb[half[m], :].T, r.do[half[m], :]).astype(BF)
        r.dq[half[m], :] = dot(ds, r.k[half[m], :]).astype(BF)
        r.dk[half[m], :] = dot(ds.T, r.q[half[m], :]).astype(BF)
    for j, ref in enumerate((r.dq, r.dk, r.dv)):
        parts = [dot(ref[half[m], :].T, r.a3[half[m], :]) for m in range(2)]
        r.dqo[j] = (parts[0] + parts[1]).astype(BF)
    work = lambda name: SimpleNamespace(**{k: getattr(r, name + "_" + k) for k in ("rc", "sy", "ry", "sl", "rr", "pc", "rt")})
    red = SimpleNamespace()
    red.a = Reduction(at, links, r.dqo, r.ga, work("ga"))
    red.a.core()
    for m in range(2):
        total = None
        for j, ref in enumerate((r.dq, r.dk, r.dv)):
            part = dot(ref[half[m], :], r.wqg[j])
            total = part if total is None else total + part
        r.h[m * STEP : m * STEP + ROWS, :] = total
    red.a.cross()

    def to_dres(m, at, dv, held):
        value = r.g[rows_of(m, at), :].astype(F32) + dv
        r.dres[rows_of(m, at), :] = value
        write_shift(r.dd, m, at, value, False)
        return held

    passes(norm_back(r.h, r.n3, gain3, shift3, rstd3, bd, False, r.e, 4, to_dres))

    def turn():
        for m in range(2):
            r.turn[m] = r.dd[GAP + STEP * m : GAP + STEP * m + ROWS, C : 2 * C].T

    turn()
    for row in range(3):
        conv_weight(r.a2, r.turn, r.dw2, row)
    red.b = Reduction(at, links, r.dw2, r.gb, work("gb"))
    red.b.core()
    red.a.scatter()
    conv_back(r.dd, r.w2g, r.h)
    red.b.cross()

    def to_dh1(m, at, dv, held):
        write_shift(r.dd, m, at, dv, False)
        return held + fold(dv)

    demb = passes(norm_back(r.h, r.n2, gain2, shift2, rstd2, bd, True, r.e, 2, to_dh1), zero_pair())
    for m in range(2):
        r.dm[chan, m : m + 1, :] = col(demb[m]).astype(BF).astype(F32)
    moves_dm = [links.remote(r.dm.at[chan], r.dm.at[chan], d) for d in quads]
    turn()
    tail = []
    for row, name in enumerate(("gc", "gd", "ge")):
        conv_weight(r.a1, r.turn, r.dw1, row)
        item = Reduction(at, links, r.dw1.at[3 * row : 3 * row + 3], getattr(r, name), work(name))
        item.core()
        tail.append(item)
    red.a.spread()
    red.b.scatter()
    for item in tail:
        item.cross()
    for copy in moves_dm:
        copy.wait_recv()
    for j in range(CHAN):
        r.dl[2 * j : 2 * j + 2, :] = r.dm[j, 0:2, :]
    own_dm = links.here(r.dl, r.rows.at[dp])
    moves_rows = [links.remote(r.dl, r.rows.at[dp], d) for d in others()]
    conv_back(r.dd, r.w1g, r.h)

    def to_maps(i, held):
        at = chunk_at(i)
        pair = [back1(m, at, 0) for m in range(2)]
        pack_out(at, pair, r.mp)
        return held

    back1 = norm_back(r.h, r.n1, gain1, shift1, rstd1, bd, True, r.e, 0,
                      lambda m, at, dv, held: r.dres[rows_of(m, at), :] + dv)
    lax.fori_loop(0, ROWS // CH, to_maps, 0)
    own_mp = links.here(r.mp.at[chan], r.mo.at[chan])
    moves_mp = [links.remote(r.mp.at[d[1]], r.mo.at[chan], d) for d in quads]
    for b in range(2):
        block = r.e[:, 128 * b : 128 * b + 128]
        r.es[2 * b] = block
        r.es[2 * b + 1] = pltpu.roll(block, SL, 1)
    r.er[chan] = r.es[chan]
    moves_e = [links.remote(r.es.at[d[1]], r.er.at[chan], d) for d in quads]
    for item in tail:
        item.scatter()
    red.b.spread()
    for copy in moves_e:
        copy.wait_recv()
    r.et[...] = r.er[0] + r.er[1] + r.er[2] + r.er[3]
    own_e = links.here(r.et, r.ext.at[dp])
    moves_ext = [links.remote(r.et, r.ext.at[dp], d) for d in others()]
    for item in tail:
        item.spread()
    for item in [red.a, red.b] + tail:
        item.finish()
    for copy in (own_y, own_dm, own_mp, own_e, we_out, tall_own):
        copy.wait()
    for copy in moves_y + moves_mp + moves_rows + moves_ext + moves_t:
        copy.wait_recv()
    links.close()


def finish(n_dp, rows, tall, ext, ga, gb, gc, gd, ge, yo, mo, weg, table,
           y_out, dm_out, dt_out, d1_out, d2_out, de_out, dq_out, do_out, e0, e1, e2, e3, e4, e5, turned):
    maps = 8 * n_dp
    chan = lax.axis_index("chan")
    steps = table.shape[0]
    dem32 = rows[...].reshape(maps, C)
    dem = dem32.astype(BF)
    times = tall[...].reshape(maps, 128)
    wide = jnp.broadcast_to(times[:, 0:1], (maps, steps))
    hot = jnp.where(wide == lax.broadcasted_iota(jnp.int32, (maps, steps), 1).astype(F32), 1.0, 0.0)
    temb = dot(hot.astype(BF), table[...])
    s = sigmoid(temb)
    tsil = (temb * s).astype(BF)
    turned[...] = dem32.T
    own = turned[pl.ds(pl.multiple_of(SL * chan, SL), SL), :].astype(BF)
    de_out[...] = dot(own, tsil)
    dtemb = dot(dem, weg[...]) * (s * (1.0 + temb * (1.0 - s)))
    high = dtemb.astype(BF)
    low = (dtemb - high.astype(F32)).astype(BF)
    both = jnp.concatenate([high, low], axis=0)
    lanes = times.T[0:1, :]
    tall_hot = jnp.where(lax.broadcasted_iota(jnp.int32, (steps, maps), 0).astype(F32) == lanes, 1.0, 0.0)
    tall_hot = jnp.concatenate([tall_hot, tall_hot], axis=1).astype(BF)
    dt_out[...] = dot(tall_hot, both)

    def whole(src, dst, taps):
        for i, t in enumerate(taps):
            for half in range(2):
                dst[i, :, 128 * half : 128 * half + 128] = src[half, SL * t : SL * t + SL, :].astype(F32)

    whole(ga, dq_out, range(3))
    whole(ga, do_out, [3])
    whole(gb, d2_out, range(9))
    for row, src in enumerate((gc, gd, ge)):
        whole(src, d1_out.at[3 * row : 3 * row + 3], range(3))
    total = ext[0]
    for i in range(1, n_dp):
        total = total + ext[i]
    for i, out in enumerate((e0, e1, e2, e3, e4, e5)):
        out[...] = total[i : i + 1, 0:SL]
    for src, dst in ((yo, y_out), (mo, dm_out)):
        for j in range(CHAN):
            block = src[j].astype(F32)
            dst[2 * j] = block[:, 0:SL].astype(BF)
            dst[2 * j + 1] = pltpu.roll(block, SL, 1)[:, 0:SL].astype(BF)


def per_device(x_maps, timesteps, counts, emb_table, w_first, w_second, w_embed, w_qkv, w_out, gain_one, shift_one,
               gain_two, shift_two, gain_three, shift_three, cotangent, *, n_dp):
    team, teams = block_sizes(n_dp)
    slots, side, _, _ = x_maps.shape
    emb = w_embed.shape[0]
    steps = emb_table.shape[0]
    par = jnp.stack([gain_one, shift_one, gain_two, shift_two, gain_three, shift_three]).astype(F32)
    par = jnp.pad(par, ((0, 2), (0, 128 - SL)))
    inputs = dict(
        x=x_maps.reshape(slots, side * side, SL), dy=cotangent.reshape(slots, side * side, SL),
        ts=timesteps, cnt=counts, table=emb_table,
        w1=jnp.swapaxes(w_first, 2, 3).reshape(9, SL, C), w2=jnp.swapaxes(w_second, 2, 3).reshape(9, SL, C),
        we=w_embed.T, wq=jnp.transpose(w_qkv, (1, 2, 0)), wo=w_out.T, par=par)
    anywhere = pl.BlockSpec(memory_space=pl.ANY)
    vmem = pl.BlockSpec(memory_space=pltpu.VMEM)
    smem = pl.BlockSpec(memory_space=pltpu.SMEM)
    where = dict(ts=smem, cnt=smem, table=vmem, par=vmem)

    def of(shape, dtype):
        return jax.ShapeDtypeStruct(shape, dtype)

    outputs = dict(
        yo=of((CHAN, ROWS, 128), BF), mo=of((CHAN, ROWS, 128), BF),
        rows=of((n_dp, 8, C), F32), tall=of((n_dp, 8, 128), F32), ext=of((n_dp, 8, 128), F32), weo=of((C, emb), BF))
    outputs.update({name: of((2, SL * taps, 128), BF) for name, taps in ITEMS})
    v = pltpu.VMEM
    maps2 = 2 * ROWS
    scratch = dict(
        xl=v((slots, ROWS, SL), BF), dyl=v((slots, ROWS, SL), BF),
        xp=v((CHAN, ROWS, 128), BF), dyp=v((CHAN, ROWS, 128), BF),
        xg=v((CHAN, ROWS, 128), BF), dyg=v((CHAN, ROWS, 128), BF),
        yp=v((CHAN, ROWS, 128), BF), mp=v((CHAN, ROWS, 128), BF),
        w1g=v((9, C, C), BF), w2g=v((9, C, C), BF), weg=v((C, emb), BF), wqg=v((4, C, C), BF),
        bd=v((C, C), BF), tl=v((8, 128), F32), pg=v((CHAN, 8, 128), F32), pa=v((8, C), F32), emb=v((16, C), F32),
        a1=v((TALL + 2 * GAP, 3 * C), BF), a2=v((TALL + 2 * GAP, 3 * C), BF), dd=v((TALL + 2 * GAP, 3 * C), BF),
        h=v((TALL, C), F32), xf=v((maps2, C), F32), n1=v((maps2, C), F32), n2=v((maps2, C), F32),
        n3=v((maps2, C), F32), dres=v((maps2, C), F32), big=v((maps2, C), F32), p=v((maps2, C), F32),
        e=v((8, C), F32), es=v((CHAN, 8, 128), F32), er=v((CHAN, 8, 128), F32), et=v((8, 128), F32),
        dm=v((CHAN, 8, C), F32), dl=v((8, C), F32), turn=v((2, ROWS, C), BF),
        dw1=v((9, C, C), BF), dw2=v((9, C, C), BF), dqo=v((4, C, C), BF))
    for name in ("a3", "q", "k", "v", "pb", "o", "g", "do", "dq", "dk", "dv"):
        scratch[name] = v((maps2, C), BF)
    for name, taps in ITEMS:
        span = SL * taps // (team // 2)
        scratch.update({
            name + "_rc": v((2, taps, SL, C), BF), name + "_sy": v((taps, SL, C), BF), name + "_ry": v((taps, SL, C), BF),
            name + "_sl": v((2, SL * taps, 128), BF), name + "_rr": v((team, span, 128), BF),
            name + "_pc": v((span, 128), BF), name + "_rt": v((teams, span, 128), BF)})
    n_remote = 64 + 3 * (n_dp - 1) + len(ITEMS) * (3 + 2 * (team - 1) + teams - 1)
    scratch.update(
        send=pltpu.SemaphoreType.DMA((n_remote,)), recv=pltpu.SemaphoreType.DMA((n_remote,)),
        own=pltpu.SemaphoreType.DMA((32,)))
    names = list(inputs) + list(outputs) + list(scratch)
    got = pl.pallas_call(
        functools.partial(mega, n_dp, names),
        out_shape=tuple(outputs.values()),
        in_specs=[where.get(name, anywhere) for name in inputs],
        out_specs=tuple(anywhere for _ in outputs),
        scratch_shapes=list(scratch.values()),
        compiler_params=pltpu.CompilerParams(collective_id=0, has_side_effects=True, vmem_limit_bytes=56 << 20),
        name="blocks",
    )(*inputs.values())
    got = dict(zip(outputs, got))
    ends = [got[name] for name in ("rows", "tall", "ext", "ga", "gb", "gc", "gd", "ge", "yo", "mo", "weo")] + [emb_table]
    flat = of((1, SL), F32)
    out = pl.pallas_call(
        functools.partial(finish, n_dp),
        out_shape=(of((slots, ROWS, SL), BF), of((slots, ROWS, SL), BF), of((steps, emb), F32), of((9, SL, C), F32),
                   of((9, SL, C), F32), of((SL, emb), F32), of((3, SL, C), F32), of((1, SL, C), F32)) + (flat,) * 6,
        in_specs=[vmem] * len(ends),
        out_specs=(vmem,) * 14,
        scratch_shapes=[v((C, 8 * n_dp), F32)],
        compiler_params=pltpu.CompilerParams(vmem_limit_bytes=48 << 20),
        name="finish",
    )(*ends)
    y, dm, dt, d1, d2, de, dq, do = out[:8]
    return (
        y.reshape(x_maps.shape), dm.reshape(x_maps.shape), dt,
        jnp.swapaxes(d1.reshape(3, 3, SL, C), 2, 3), jnp.swapaxes(d2.reshape(3, 3, SL, C), 2, 3),
        de.T, jnp.transpose(dq, (2, 0, 1)), do.reshape(SL, C).T) + tuple(e.reshape(SL) for e in out[8:])


def solution(mesh):
    weights = (P(None, None, None, "chan"), P(None, None, None, "chan"), P(None, "chan"), P(None, None, "chan"),
               P(None, "chan")) + (P("chan"),) * 6
    maps = P("dp", None, None, "chan")
    return jax.shard_map(
        functools.partial(per_device, n_dp=mesh.shape["dp"]), mesh=mesh,
        in_specs=(maps, P("dp"), P("dp"), P()) + weights + (maps,),
        out_specs=(maps, maps, P()) + weights, check_vma=False)
```

```python
import functools
from types import SimpleNamespace

import jax
import jax.numpy as jnp
from jax import lax
from jax.experimental import pallas as pl
from jax.experimental.pallas import tpu as pltpu
from jax.sharding import PartitionSpec as P

F32 = jnp.float32
BF = jnp.bfloat16
MESH = pl.DeviceIdType.MESH
EPS = 1e-06
GROUPS = 32
CHAN = 4
ROWS = 256
C = 256
SL = C // CHAN
GAP = 16
STEP = ROWS + GAP
TALL = 2 * ROWS + GAP
CH = 32
COUNT = ROWS * (C // GROUPS)


def dot(a, b):
    return jnp.dot(a, b, preferred_element_type=F32)


def dot_nt(a, b):
    return lax.dot_general(a, b, (((1,), (1,)), ((), ())), preferred_element_type=F32)


def sigmoid(u):
    return 0.5 * jnp.tanh(0.5 * u) + 0.5


def fold(v):
    return v.reshape(v.shape[0] // 8, 8, v.shape[1]).sum(axis=0)


def group_total(rows, bd):
    at = lax.broadcasted_iota(jnp.int32, (8, C), 0)
    stack = jnp.zeros((8, C), F32)
    for i, row in enumerate(rows):
        stack = jnp.where(at == i, row, stack)
    high = stack.astype(BF).astype(F32)
    rest = stack - high
    mid = rest.astype(BF).astype(F32)
    parts = jnp.concatenate([high, mid, rest - mid, jnp.zeros((8, C), F32)], axis=0)
    total = dot(parts.astype(BF), bd)
    total = total[0:8] + total[8:16] + total[16:24]
    return [total[i : i + 1] for i in range(len(rows))]


def chunk_at(i):
    return pl.multiple_of(i * CH, CH)


def passes(body, carry=None):
    carry = (0, 0) if carry is None else carry

    def step(i, held):
        return tuple(body(m, chunk_at(i), held[m]) for m in range(2))

    return lax.fori_loop(0, ROWS // CH, step, carry)


def zero_pair():
    return (jnp.zeros((8, C), F32), jnp.zeros((8, C), F32))


def col(v):
    return jnp.sum(v, axis=0, keepdims=True)


def write_shift(dst, m, at, value, forward):
    place = lax.broadcasted_iota(jnp.int32, (CH, C), 0) % 16
    before = jnp.where(place == 0, 0.0, pltpu.roll(value, 1, 0))
    after = jnp.where(place == 15, 0.0, pltpu.roll(value, CH - 1, 0))
    first, last = (before, after) if forward else (after, before)
    rows = pl.ds(pl.multiple_of(at + (GAP + m * STEP), 16), CH)
    dst[rows, 0:C] = first.astype(BF)
    dst[rows, C : 2 * C] = value.astype(BF)
    dst[rows, 2 * C : 3 * C] = last.astype(BF)


def norm_forward(load, n_ref, gain, shift, bd, emit):
    def sums(m, at, held):
        return held + fold(load(m, at))

    total = passes(sums, zero_pair())
    mean = group_total([col(t) for t in total], bd)
    mean = [v * (1.0 / COUNT) for v in mean]

    def squares(m, at, held):
        d = load(m, at) - mean[m]
        return held + fold(d * d)

    total = passes(squares, zero_pair())
    var = group_total([col(t) for t in total], bd)
    rstd = [lax.rsqrt(v * (1.0 / COUNT) + EPS) for v in var]

    def last(m, at, held):
        n = (load(m, at) - mean[m]) * rstd[m]
        n_ref[pl.ds(pl.multiple_of(at + m * ROWS, CH), CH), :] = n
        emit(m, at, n * gain + shift)
        return held

    passes(last)
    return rstd


def norm_back(d_ref, n_ref, gain, shift, rstd, bd, active, e_ref, e_at, emit):
    def rows(m, at):
        return pl.ds(pl.multiple_of(at + m * STEP, 16), CH)

    def first(m, at, held):
        d = d_ref[rows(m, at), :]
        n = n_ref[pl.ds(pl.multiple_of(at + m * ROWS, CH), CH), :]
        if active:
            u = n * gain + shift
            s = sigmoid(u)
            d = d * (s * (1.0 + u * (1.0 - s)))
            d_ref[rows(m, at), :] = d
        return (held[0] + fold(d), held[1] + fold(d * n))

    total = passes(first, (zero_pair(), zero_pair()))
    ones = [col(t[0]) for t in total]
    twos = [col(t[1]) for t in total]
    e_ref[e_at : e_at + 1, :] = twos[0] + twos[1]
    e_ref[e_at + 1 : e_at + 2, :] = ones[0] + ones[1]
    means = group_total([gain * v for v in ones + twos], bd)
    means = [v * (1.0 / COUNT) for v in means]

    def second(m, at, held):
        d = d_ref[rows(m, at), :]
        n = n_ref[pl.ds(pl.multiple_of(at + m * ROWS, CH), CH), :]
        return emit(m, at, rstd[m] * (d * gain - means[m] - n * means[2 + m]), held)

    return second


def unpack(low, high):
    lane = lax.broadcasted_iota(jnp.int32, low.shape, 1)
    first = jnp.where(lane < SL, low, pltpu.roll(high, SL, 1))
    second = jnp.where(lane < SL, pltpu.roll(low, SL, 1), high)
    return first, second


def conv_forward(a_ref, w_ref, h_ref, ready):
    for row in range(3):
        ready(row)
        total = None
        for c in range(3):
            part = dot_nt(a_ref[16 * row : 16 * row + TALL, C * c : C * c + C], w_ref[3 * row + c])
            total = part if total is None else total + part
        h_ref[...] = total if row == 0 else h_ref[...] + total


def conv_back(d_ref, w_ref, h_ref):
    for row in range(3):
        at = 16 * (2 - row)
        w = w_ref[3 * row : 3 * row + 3].reshape(3 * C, C)
        part = dot(d_ref[at : at + TALL, :], w)
        h_ref[...] = part if row == 0 else h_ref[...] + part


def conv_weight(a_ref, turned, dw_ref, row):
    for c in range(3):
        total = None
        for m in range(2):
            at = 16 * row + STEP * m
            part = dot(turned[m], a_ref[at : at + ROWS, C * c : C * c + C])
            total = part if total is None else total + part
        dw_ref[3 * row + c] = total.astype(BF)


class Links:
    def __init__(self, send, recv, own):
        self.send, self.recv, self.own = send, recv, own
        self.used, self.local = 0, 0
        self.sent = []

    def remote(self, src, dst, device):
        at = self.used
        self.used += 1
        copy = pltpu.make_async_remote_copy(
            src_ref=src, dst_ref=dst, send_sem=self.send.at[at], recv_sem=self.recv.at[at],
            device_id=device, device_id_type=MESH)
        copy.start()
        self.sent.append(copy)
        return copy

    def here(self, src, dst):
        copy = pltpu.make_async_copy(src, dst, self.own.at[self.local])
        self.local += 1
        copy.start()
        return copy

    def close(self):
        for copy in self.sent:
            copy.wait_send()


def block_sizes(n_dp):
    team = min(8, n_dp)
    return team, n_dp // team


def aligned(start, size):
    return pl.ds(pl.multiple_of(start, size), size)


class Reduction:
    def __init__(self, at, links, grad, out, work):
        self.at, self.links, self.grad, self.out, self.w = at, links, grad, out, work
        self.taps = grad.shape[0]
        self.span = SL * self.taps // (at.team // 2)

    def core(self):
        at = self.at
        self.waits = [
            self.links.remote(self.grad.at[:, aligned(SL * (2 * y + 1 - at.core), SL), :], self.w.rc.at[y], at.sibling)
            for y in range(2)]

    def cross(self):
        at, w = self.at, self.w
        for copy in self.waits:
            copy.wait_recv()
        for y in range(2):
            for t in range(self.taps):
                mine = self.grad[t, aligned(SL * (2 * y + at.core), SL), :].astype(F32)
                total = (mine + w.rc[y, t].astype(F32)).astype(BF)
                for half in range(2):
                    w.sx[y, half, SL * t : SL * t + SL, :] = total[:, 128 * half : 128 * half + 128]
        y, b = at.y, at.bit
        self.waits = [
            self.links.remote(w.sx.at[1 - y, b], w.ry.at[0], at.across),
            self.links.remote(w.sx.at[1 - y, 1 - b], w.ry.at[2], at.oblique),
            self.links.remote(w.sx.at[y, 1 - b], w.ry.at[1], at.beside)]

    def piece(self, ref, p):
        return ref.at[aligned(self.span * p, self.span), :]

    def scatter(self):
        at, w = self.at, self.w
        for copy in self.waits:
            copy.wait_recv()
        total = w.sx[at.y, at.bit].astype(F32)
        for i in range(3):
            total = total + w.ry[i].astype(F32)
        w.hs[...] = total.astype(BF)
        self.waits = []
        for s in range(1, at.team // 2):
            p = (at.rank // 2 + s) % (at.team // 2)
            self.waits.append(self.links.remote(self.piece(w.hs, p), w.rz.at[s], at.mate(2 * p + at.bit)))

    def spread(self):
        at, w = self.at, self.w
        for copy in self.waits:
            copy.wait_recv()
        place = at.rank // 2
        total = self.piece(w.hs, place)[...].astype(F32)
        for s in range(1, at.team // 2):
            total = total + w.rz[s].astype(F32)
        w.pc[...] = total.astype(BF)
        if at.teams > 1:
            copies = [self.links.here(w.pc, w.rt.at[at.lead])]
            for s in range(1, at.teams):
                other = (at.lead + s) % at.teams
                copies.append(self.links.remote(w.pc, w.rt.at[at.lead], at.device(other * at.team + at.rank)))
            copies[0].wait()
            for copy in copies[1:]:
                copy.wait_recv()
                copy.wait_send()
                self.links.sent = [c for c in self.links.sent if c is not copy]
            total = w.rt[0].astype(F32)
            for s in range(1, at.teams):
                total = total + w.rt[s].astype(F32)
            w.pc[...] = total.astype(BF)
        target = self.piece(self.out.at[at.bit], place)
        self.own = self.links.here(w.pc, target)
        self.waits = []
        for s in range(1, at.team):
            self.waits.append(self.links.remote(w.pc, target, at.mate((at.rank + s) % at.team)))

    def finish(self):
        self.own.wait()
        for copy in self.waits:
            copy.wait_recv()


ITEMS = (("ga", 4), ("gb0", 3), ("gb1", 3), ("gb2", 3), ("gc0", 3), ("gc1", 3), ("gc2", 3))
GAINS = ("gain1", "shift1", "gain2", "shift2", "gain3", "shift3")


def mega(n_dp, names, *refs):
    r = SimpleNamespace(**dict(zip(names, refs)))
    team, teams = block_sizes(n_dp)
    dp, chan = lax.axis_index("dp"), lax.axis_index("chan")
    core, y, bit = chan % 2, chan // 2, dp % 2
    sibling, across, corner = (dp, 2 * y + 1 - core), (dp, 2 * (1 - y) + core), (dp, 2 * (1 - y) + 1 - core)
    beside, oblique = (dp + 1 - 2 * bit, chan), (dp + 1 - 2 * bit, 2 * (1 - y) + core)
    quads = (sibling, across, corner)
    rank, lead = dp % team, dp // team
    at = SimpleNamespace(
        core=core, y=y, bit=bit, sibling=sibling, across=across, beside=beside, oblique=oblique,
        team=team, teams=teams, rank=rank, lead=lead,
        mate=lambda p: (lead * team + p, chan), device=lambda p: (p, chan))
    links = Links(r.send, r.recv, r.own)

    def others():
        return [(lax.rem(dp + s, n_dp), chan) for s in range(1, n_dp)]

    barrier = pltpu.get_barrier_semaphore()
    for device in quads + (oblique,) + tuple(others()):
        pl.semaphore_signal(barrier, inc=1, device_id=device, device_id_type=MESH)
    load_x, load_dy = links.here(r.x, r.xl), links.here(r.dy, r.dyl)
    load_par = [links.here(getattr(r, name), r.pin.at[i]) for i, name in enumerate(GAINS)]
    load_ts, load_cnt, load_table = links.here(r.ts, r.tss), links.here(r.cnt, r.cns), links.here(r.table, r.tab)
    mine = aligned(SL * chan, SL)
    fill = [
        links.here(r.w1, r.w1g.at[:, mine, :]), links.here(r.w2, r.w2g.at[:, mine, :]),
        links.here(r.we, r.weg.at[:, mine, :]),
        links.here(r.wq, r.wqg.at[0:3, mine, :]), links.here(r.wo, r.wqg.at[3:4, mine, :])]

    def pack(src, dst):
        for k in range(CHAN):
            for half in range(2):
                rows = slice(128 * half, 128 * half + 128)
                both = jnp.concatenate([src[2 * k, rows, :].astype(F32), src[2 * k + 1, rows, :].astype(F32)], axis=1)
                dst[k, rows, :] = both.astype(BF)

    load_x.wait()
    pack(r.xl, r.xp)
    for copy in load_par:
        copy.wait()
    r.par[...] = jnp.zeros((8, 128), F32)
    for i in range(len(GAINS)):
        r.par[i : i + 1, 0:SL] = r.pin[i].astype(F32)
    pl.semaphore_wait(barrier, CHAN + n_dp - 1)

    part = 32 * bit
    far = SL * (2 * (1 - y) + core)

    class Share:
        def __init__(self, w, g):
            self.w, self.g, self.moves = w, g, {}
            self.moves["across"] = links.remote(
                w.at[:, aligned(part, 32), :], g.at[:, aligned(SL * chan + part, 32), :], across)

        def own(self):
            self.moves["own"] = links.remote(self.w, self.g.at[:, mine, :], sibling)

        def hand(self, name, rows, device):
            piece = self.g.at[:, aligned(rows, 32), :]
            self.moves[name] = links.remote(piece, piece, device)

        def relay(self):
            self.moves["across"].wait_recv()
            self.hand("beside", far + part, beside)
            self.hand("first", far + part, sibling)

        def relay_again(self):
            self.moves["beside"].wait_recv()
            self.hand("second", far + 32 - part, sibling)

        def landed(self):
            for name in ("own", "first", "second"):
                self.moves[name].wait_recv()

    def rows3(ref, row):
        return ref.at[3 * row : 3 * row + 3]

    one = [Share(rows3(r.w1, row), rows3(r.w1g, row)) for row in range(3)]
    moves_x = [links.remote(r.xp.at[d[1]], r.xg.at[chan], d) for d in quads]
    moves_par = [links.remote(r.par, r.pg.at[chan], d) for d in quads]
    mix = Share(r.we, r.weg)
    two = [Share(rows3(r.w2, row), rows3(r.w2g, row)) for row in range(3)]
    out = [Share(r.wq, r.wqg.at[0:3]), Share(r.wo, r.wqg.at[3:4])]
    for share in one + [mix] + two + out:
        share.own()

    at_row = lax.broadcasted_iota(jnp.int32, (C, C), 0) // (C // GROUPS)
    at_col = lax.broadcasted_iota(jnp.int32, (C, C), 1) // (C // GROUPS)
    r.bd[...] = jnp.where(at_row == at_col, 1.0, 0.0).astype(BF)
    for ref in (r.a1, r.a2, r.dd):
        for gap in range(3):
            ref[gap * STEP : gap * STEP + GAP, :] = jnp.zeros((GAP, 3 * C), BF)
    r.xg[chan] = r.xp[chan]
    r.pg[chan] = r.par[...]
    load_ts.wait()
    row8 = lax.broadcasted_iota(jnp.int32, (8, 128), 0)
    times = jnp.zeros((8, 128), F32)
    for i in range(8):
        times = jnp.where(row8 == i, r.tss[i].astype(F32), times)
    r.tl[...] = times
    r.ta[dp] = times
    moves_t = [links.remote(r.tl, r.ta.at[dp], d) for d in others()]
    load_dy.wait()
    pack(r.dyl, r.dyp)
    r.dyg[chan] = r.dyp[chan]
    steps = r.table.shape[0]
    load_table.wait()

    def embeddings(times):
        count = times.shape[0]
        wide = jnp.broadcast_to(times[:, 0:1], (count, steps))
        hot = jnp.where(wide == lax.broadcasted_iota(jnp.int32, (count, steps), 1).astype(F32), 1.0, 0.0)
        temb = dot(hot.astype(BF), r.tab[...])
        s = sigmoid(temb)
        return temb, s, (temb * s).astype(BF)

    _, _, tsil = embeddings(jnp.concatenate([times, times], axis=0))
    for share in one:
        share.relay()

    bd = r.bd[...]
    for copy in moves_x + moves_par:
        copy.wait_recv()
    for b in range(2):
        first, _ = unpack(r.pg[2 * b], r.pg[2 * b + 1])
        r.pa[:, 128 * b : 128 * b + 128] = first
    par = r.pa[...]
    gain1, shift1, gain2, shift2, gain3, shift3 = [par[i : i + 1] for i in range(6)]

    def spread_out(src, at, dst, scale=None):
        for b in range(2):
            pair = unpack(src[2 * b, pl.ds(at, CH), :].astype(F32), src[2 * b + 1, pl.ds(at, CH), :].astype(F32))
            for m in range(2):
                value = pair[m] if scale is None else pair[m] * scale[m]
                dst[pl.ds(pl.multiple_of(at + m * ROWS, CH), CH), 128 * b : 128 * b + 128] = value.astype(dst.dtype)

    def open_x(i, held):
        spread_out(r.xg, chunk_at(i), r.xf)
        return held

    lax.fori_loop(0, ROWS // CH, open_x, 0)

    def rows_of(m, at):
        return pl.ds(pl.multiple_of(at + m * ROWS, CH), CH)

    def rows_gap(m, at):
        return pl.ds(pl.multiple_of(at + m * STEP, 16), CH)

    def to_shift(dst):
        def emit(m, at, u):
            write_shift(dst, m, at, u * sigmoid(u), True)
        return emit

    rstd1 = norm_forward(lambda m, at: r.xf[rows_of(m, at), :], r.n1, gain1, shift1, bd, to_shift(r.a1))
    for share in one:
        share.relay_again()
    moves_dy = [links.remote(r.dyp.at[d[1]], r.dyg.at[chan], d) for d in quads]
    mix.relay()
    two[0].relay()
    for copy in fill:
        copy.wait()
    conv_forward(r.a1, r.w1g, r.h, lambda row: one[row].landed())
    mix.relay_again()
    two[0].relay_again()
    for share in two[1:] + out:
        share.relay()
    mix.landed()
    r.emb[0:16, :] = dot_nt(tsil, r.weg[0])
    emb = [r.emb[pl.ds(2 * chan + m, 1), :] for m in range(2)]

    rstd2 = norm_forward(lambda m, at: r.h[rows_gap(m, at), :] + emb[m], r.n2, gain2, shift2, bd, to_shift(r.a2))
    for share in two[1:] + out:
        share.relay_again()
    conv_forward(r.a2, r.w2g, r.h, lambda row: two[row].landed())

    def load_resid(m, at):
        return r.xf[rows_of(m, at), :] + r.h[rows_gap(m, at), :]

    def to_a3(m, at, u):
        r.a3[rows_of(m, at), :] = u.astype(BF)

    rstd3 = norm_forward(load_resid, r.n3, gain3, shift3, bd, to_a3)
    for share in out:
        share.landed()
    for j, ref in enumerate((r.q, r.k, r.v)):
        ref[...] = dot_nt(r.a3[...], r.wqg[j]).astype(BF)
    load_cnt.wait()
    count = r.cns[0]
    live = [jnp.where(2 * chan + m < count, 1.0, 0.0).astype(F32) for m in range(2)]
    scale = C ** (-0.5)
    half = [slice(0, ROWS), slice(ROWS, 2 * ROWS)]
    for m in range(2):
        s = dot_nt(r.q[half[m], :], r.k[half[m], :]) * scale
        p = jnp.exp(s - jnp.max(s, axis=1, keepdims=True))
        p = p * (1.0 / jnp.sum(p, axis=1, keepdims=True))
        r.p[half[m], :] = p
        r.pb[half[m], :] = p.astype(BF)
        r.o[half[m], :] = dot(p.astype(BF), r.v[half[m], :]).astype(BF)
    r.big[...] = dot_nt(r.o[...], r.wqg[3])

    def pack_out(at, pair, dst):
        for b in range(2):
            even, odd = unpack(*(v[:, 128 * b : 128 * b + 128] for v in pair))
            dst[2 * b, pl.ds(at, CH), :] = even.astype(BF)
            dst[2 * b + 1, pl.ds(at, CH), :] = odd.astype(BF)

    def to_y(i, held):
        at = chunk_at(i)
        pack_out(at, [(load_resid(m, at) + r.big[rows_of(m, at), :]) * live[m] for m in range(2)], r.yp)
        return held

    lax.fori_loop(0, ROWS // CH, to_y, 0)
    own_y = links.here(r.yp.at[chan], r.yo.at[chan])
    moves_y = [links.remote(r.yp.at[d[1]], r.yo.at[chan], d) for d in quads]

    for copy in moves_dy:
        copy.wait_recv()

    def open_dy(i, held):
        spread_out(r.dyg, chunk_at(i), r.g, live)
        return held

    lax.fori_loop(0, ROWS // CH, open_dy, 0)
    for m in range(2):
        r.turn[m] = r.g[half[m], :].T
    r.dqo[3] = (dot(r.turn[0], r.o[half[0], :]) + dot(r.turn[1], r.o[half[1], :])).astype(BF)
    r.do[...] = dot(r.g[...], r.wqg[3]).astype(BF)
    for m in range(2):
        dp_m = dot_nt(r.do[half[m], :], r.v[half[m], :])
        p = r.p[half[m], :]
        ds = (p * (dp_m - jnp.sum(p * dp_m, axis=1, keepdims=True)) * scale).astype(BF)
        r.dv[half[m], :] = dot(r.pb[half[m], :].T, r.do[half[m], :]).astype(BF)
        r.dq[half[m], :] = dot(ds, r.k[half[m], :]).astype(BF)
        r.dk[half[m], :] = dot(ds.T, r.q[half[m], :]).astype(BF)
    for j, ref in enumerate((r.dq, r.dk, r.dv)):
        parts = [dot(ref[half[m], :].T, r.a3[half[m], :]) for m in range(2)]
        r.dqo[j] = (parts[0] + parts[1]).astype(BF)

    def reduction(name, grad):
        work = SimpleNamespace(**{k: getattr(r, name + "_" + k) for k in ("rc", "sx", "ry", "hs", "rz", "pc", "rt")})
        item = Reduction(at, links, grad, getattr(r, name), work)
        item.core()
        return item

    attn = reduction("ga", r.dqo)
    for m in range(2):
        total = None
        for j, ref in enumerate((r.dq, r.dk, r.dv)):
            part_j = dot(ref[half[m], :], r.wqg[j])
            total = part_j if total is None else total + part_j
        r.h[m * STEP : m * STEP + ROWS, :] = total
    attn.cross()

    def to_dres(m, at, dv, held):
        value = r.g[rows_of(m, at), :].astype(F32) + dv
        r.dres[rows_of(m, at), :] = value
        write_shift(r.dd, m, at, value, False)
        return held

    passes(norm_back(r.h, r.n3, gain3, shift3, rstd3, bd, False, r.e, 4, to_dres))

    def turn():
        for m in range(2):
            r.turn[m] = r.dd[GAP + STEP * m : GAP + STEP * m + ROWS, C : 2 * C].T

    turn()
    second = []
    for row in range(3):
        conv_weight(r.a2, r.turn, r.dw2, row)
        second.append(reduction(f"gb{row}", rows3(r.dw2, row)))
    second[0].cross()
    conv_back(r.dd, r.w2g, r.h)
    second[1].cross()
    second[2].cross()
    attn.scatter()

    def to_dh1(m, at, dv, held):
        write_shift(r.dd, m, at, dv, False)
        return held + fold(dv)

    demb = passes(norm_back(r.h, r.n2, gain2, shift2, rstd2, bd, True, r.e, 2, to_dh1), zero_pair())
    for m in range(2):
        r.dm[chan, m : m + 1, :] = col(demb[m]).astype(BF).astype(F32)
    moves_dm = [links.remote(r.dm.at[chan], r.dm.at[chan], d) for d in quads]
    turn()
    first = []
    for row in range(3):
        conv_weight(r.a1, r.turn, r.dw1, row)
        first.append(reduction(f"gc{row}", rows3(r.dw1, row)))
        if row > 0:
            first[row - 1].cross()
    second[0].scatter()
    conv_back(r.dd, r.w1g, r.h)
    first[2].cross()
    attn.spread()
    second[1].scatter()
    second[2].scatter()
    for copy in moves_dm:
        copy.wait_recv()
    for j in range(CHAN):
        r.dl[2 * j : 2 * j + 2, :] = r.dm[j, 0:2, :]
    r.ra[dp] = r.dl[...]
    moves_rows = [links.remote(r.dl, r.ra.at[dp], d) for d in others()]
    back1 = norm_back(r.h, r.n1, gain1, shift1, rstd1, bd, True, r.e, 0,
                      lambda m, at, dv, held: r.dres[rows_of(m, at), :] + dv)

    def to_maps(i, held):
        at = chunk_at(i)
        pack_out(at, [back1(m, at, 0) for m in range(2)], r.mp)
        return held

    lax.fori_loop(0, ROWS // CH, to_maps, 0)
    own_mp = links.here(r.mp.at[chan], r.mo.at[chan])
    moves_mp = [links.remote(r.mp.at[d[1]], r.mo.at[chan], d) for d in quads]
    for b in range(2):
        block = r.e[:, 128 * b : 128 * b + 128]
        r.es[2 * b] = block
        r.es[2 * b + 1] = pltpu.roll(block, SL, 1)
    r.er[chan] = r.es[chan]
    moves_e = [links.remote(r.es.at[d[1]], r.er.at[chan], d) for d in quads]
    second[0].spread()
    first[0].scatter()
    second[1].spread()
    second[2].spread()
    first[1].scatter()
    first[2].scatter()
    for copy in moves_e:
        copy.wait_recv()
    r.et[...] = r.er[0] + r.er[1] + r.er[2] + r.er[3]
    own_e = links.here(r.et, r.ext.at[dp])
    moves_ext = [links.remote(r.et, r.ext.at[dp], d) for d in others()]
    first[0].spread()
    for copy in moves_t + moves_rows:
        copy.wait_recv()
    maps = 8 * n_dp
    temb, s, tsil = embeddings(r.ta[...].reshape(maps, 128))
    rows = r.ra[...].reshape(maps, C)
    r.rt[...] = rows.T
    r.dew[...] = dot(r.rt[mine, :].astype(BF), tsil)
    dtemb = dot(rows.astype(BF), r.weg[0]) * (s * (1.0 + temb * (1.0 - s)))
    high = dtemb.astype(BF)
    r.bw[0:maps, :] = high
    r.bw[maps:, :] = (dtemb - high.astype(F32)).astype(BF)
    ends = [links.here(r.dew, r.de), links.here(r.bw, r.both), links.here(r.ta, r.tall)]
    first[1].spread()
    first[2].spread()
    for item in [attn] + second + first:
        item.finish()
    for copy in [own_y, own_mp, own_e] + ends:
        copy.wait()
    for copy in moves_y + moves_mp + moves_ext:
        copy.wait_recv()
    links.close()


def finish(n_dp, names, *refs):
    r = SimpleNamespace(**dict(zip(names, refs)))
    maps = 8 * n_dp
    steps = r.dt.shape[0]
    links = Links(None, None, r.own)
    items = [name for name, _ in ITEMS]
    load = {name: links.here(getattr(r, name), getattr(r, name + "_v"))
            for name in ["tall", "both", "yo", "mo"] + items + ["ext"]}
    stores = [links.here(r.de, r.de_out)]

    def out(src, dst):
        stores.append(links.here(src, dst))

    load["tall"].wait()
    load["both"].wait()
    lanes = r.tall_v[...].reshape(maps, 128).T[0:1, :]
    lanes = jnp.concatenate([lanes, lanes], axis=1)
    for start in range(0, steps, 256):
        size = min(256, steps - start)
        ids = lax.broadcasted_iota(jnp.int32, (size, 2 * maps), 0).astype(F32) + float(start)
        hot = jnp.where(ids == lanes, 1.0, 0.0).astype(BF)
        r.dt_v[start : start + size, :] = dot(hot, r.both_v[...])
        out(r.dt_v.at[start : start + size], r.dt.at[start : start + size])

    def unpack_maps(name, dst, dst_v):
        load[name].wait()
        src = getattr(r, name + "_v")
        for j in range(CHAN):
            block = src[j].astype(F32)
            dst_v[2 * j] = block[:, 0:SL].astype(BF)
            dst_v[2 * j + 1] = pltpu.roll(block, SL, 1)[:, 0:SL].astype(BF)
        out(dst_v, dst)

    def whole(name, dst_v, base, taps):
        src = getattr(r, name + "_v")
        for i, t in enumerate(taps):
            for half in range(2):
                dst_v[base + i, :, 128 * half : 128 * half + 128] = src[half, SL * t : SL * t + SL, :].astype(F32)

    unpack_maps("yo", r.y, r.y_v)
    unpack_maps("mo", r.dm, r.dm_v)
    load["ga"].wait()
    whole("ga", r.dq_v, 0, range(3))
    out(r.dq_v, r.dq)
    whole("ga", r.do_v, 0, [3])
    out(r.do_v, r.do)
    for kind, dst_v, dst in (("gb", r.d2_v, r.d2), ("gc", r.d1_v, r.d1)):
        for row in range(3):
            load[f"{kind}{row}"].wait()
            whole(f"{kind}{row}", dst_v, 3 * row, range(3))
            out(dst_v.at[3 * row : 3 * row + 3], dst.at[3 * row : 3 * row + 3])
    load["ext"].wait()
    total = r.ext_v[0]
    for i in range(1, n_dp):
        total = total + r.ext_v[i]
    for i in range(6):
        r.gains_v[i] = total[i : i + 1, 0:SL]
        out(r.gains_v.at[i], getattr(r, f"e{i}"))
    for copy in stores:
        copy.wait()


def per_device(x_maps, timesteps, counts, emb_table, w_first, w_second, w_embed, w_qkv, w_out, gain_one, shift_one,
               gain_two, shift_two, gain_three, shift_three, cotangent, *, n_dp):
    team, teams = block_sizes(n_dp)
    slots, side, _, _ = x_maps.shape
    emb = w_embed.shape[0]
    steps = emb_table.shape[0]
    inputs = dict(
        x=x_maps.reshape(slots, side * side, SL), dy=cotangent.reshape(slots, side * side, SL),
        ts=timesteps, cnt=counts, table=emb_table,
        w1=jnp.swapaxes(w_first, 2, 3).reshape(9, SL, C), w2=jnp.swapaxes(w_second, 2, 3).reshape(9, SL, C),
        we=w_embed.T[None], wq=jnp.transpose(w_qkv, (1, 2, 0)), wo=w_out.T[None])
    gains = (gain_one, shift_one, gain_two, shift_two, gain_three, shift_three)
    inputs.update({name: v.reshape(1, SL) for name, v in zip(GAINS, gains)})
    anywhere = pl.BlockSpec(memory_space=pl.ANY)

    def of(shape, dtype):
        return jax.ShapeDtypeStruct(shape, dtype)

    maps = 8 * n_dp
    middle = dict(
        yo=of((CHAN, ROWS, 128), BF), mo=of((CHAN, ROWS, 128), BF), tall=of((n_dp, 8, 128), F32),
        ext=of((n_dp, 8, 128), F32), both=of((2 * maps, emb), BF), de=of((SL, emb), F32))
    middle.update({name: of((2, SL * taps, 128), BF) for name, taps in ITEMS})
    v = pltpu.VMEM
    maps2 = 2 * ROWS
    scratch = dict(
        xl=v((slots, ROWS, SL), BF), dyl=v((slots, ROWS, SL), BF), pin=v((len(GAINS), 1, SL), BF),
        tss=pltpu.SMEM((slots,), jnp.int32), cns=pltpu.SMEM((1,), jnp.int32), tab=v((steps, emb), BF),
        xp=v((CHAN, ROWS, 128), BF), dyp=v((CHAN, ROWS, 128), BF),
        xg=v((CHAN, ROWS, 128), BF), dyg=v((CHAN, ROWS, 128), BF),
        yp=v((CHAN, ROWS, 128), BF), mp=v((CHAN, ROWS, 128), BF),
        w1g=v((9, C, C), BF), w2g=v((9, C, C), BF), weg=v((1, C, emb), BF), wqg=v((4, C, C), BF),
        bd=v((C, C), BF), tl=v((8, 128), F32), ta=v((n_dp, 8, 128), F32), par=v((8, 128), F32),
        pg=v((CHAN, 8, 128), F32), pa=v((8, C), F32), emb=v((16, C), F32),
        a1=v((TALL + 2 * GAP, 3 * C), BF), a2=v((TALL + 2 * GAP, 3 * C), BF), dd=v((TALL + 2 * GAP, 3 * C), BF),
        h=v((TALL, C), F32), xf=v((maps2, C), F32), n1=v((maps2, C), F32), n2=v((maps2, C), F32),
        n3=v((maps2, C), F32), dres=v((maps2, C), F32), big=v((maps2, C), F32), p=v((maps2, C), F32),
        e=v((8, C), F32), es=v((CHAN, 8, 128), F32), er=v((CHAN, 8, 128), F32), et=v((8, 128), F32),
        dm=v((CHAN, 8, C), F32), dl=v((8, C), F32), ra=v((n_dp, 8, C), F32), rt=v((C, maps), F32),
        dew=v((SL, emb), F32), bw=v((2 * maps, emb), BF), turn=v((2, ROWS, C), BF),
        dw1=v((9, C, C), BF), dw2=v((9, C, C), BF), dqo=v((4, C, C), BF))
    for name in ("a3", "q", "k", "v", "pb", "o", "g", "do", "dq", "dk", "dv"):
        scratch[name] = v((maps2, C), BF)
    for name, taps in ITEMS:
        rows, span = SL * taps, SL * taps // (team // 2)
        scratch.update({
            name + "_rc": v((2, taps, SL, C), BF), name + "_sx": v((2, 2, rows, 128), BF),
            name + "_ry": v((3, rows, 128), BF), name + "_hs": v((rows, 128), BF),
            name + "_rz": v((team // 2, span, 128), BF), name + "_pc": v((span, 128), BF),
            name + "_rt": v((teams, span, 128), BF)})
    n_remote = 72 + 3 * (n_dp - 1) + len(ITEMS) * (5 + team // 2 + team + teams)
    scratch.update(
        send=pltpu.SemaphoreType.DMA((n_remote,)), recv=pltpu.SemaphoreType.DMA((n_remote,)),
        own=pltpu.SemaphoreType.DMA((48,)))
    got = pl.pallas_call(
        functools.partial(mega, n_dp, list(inputs) + list(middle) + list(scratch)),
        out_shape=tuple(middle.values()),
        in_specs=[anywhere] * len(inputs),
        out_specs=(anywhere,) * len(middle),
        scratch_shapes=list(scratch.values()),
        compiler_params=pltpu.CompilerParams(collective_id=0, has_side_effects=True, vmem_limit_bytes=60 << 20),
        name="blocks",
    )(*inputs.values())
    results = dict(
        y=of((slots, ROWS, SL), BF), dm=of((slots, ROWS, SL), BF), dt=of((steps, emb), F32), d1=of((9, SL, C), F32),
        d2=of((9, SL, C), F32), de_out=of((SL, emb), F32), dq=of((3, SL, C), F32), do=of((1, SL, C), F32))
    results.update({f"e{i}": of((1, SL), F32) for i in range(6)})
    scratch = {name + "_v": v(o.shape, o.dtype) for name, o in middle.items() if name != "de"}
    scratch.update({name + "_v": v(o.shape, o.dtype) for name, o in results.items() if name[0] != "e"})
    scratch.update(gains_v=v((6, 1, SL), F32), own=pltpu.SemaphoreType.DMA((48,)))
    got = pl.pallas_call(
        functools.partial(finish, n_dp, list(middle) + list(results) + list(scratch)),
        out_shape=tuple(results.values()),
        in_specs=[anywhere] * len(middle),
        out_specs=(anywhere,) * len(results),
        scratch_shapes=list(scratch.values()),
        compiler_params=pltpu.CompilerParams(vmem_limit_bytes=60 << 20),
        name="finish",
    )(*got)
    got = dict(zip(results, got))
    return (
        got["y"].reshape(x_maps.shape), got["dm"].reshape(x_maps.shape), got["dt"],
        jnp.swapaxes(got["d1"].reshape(3, 3, SL, C), 2, 3), jnp.swapaxes(got["d2"].reshape(3, 3, SL, C), 2, 3),
        got["de_out"].T, jnp.transpose(got["dq"], (2, 0, 1)), got["do"].reshape(SL, C).T,
    ) + tuple(got[f"e{i}"].reshape(SL) for i in range(6))


def solution(mesh):
    weights = (P(None, None, None, "chan"), P(None, None, None, "chan"), P(None, "chan"), P(None, None, "chan"),
               P(None, "chan")) + (P("chan"),) * 6
    maps = P("dp", None, None, "chan")
    return jax.shard_map(
        functools.partial(per_device, n_dp=mesh.shape["dp"]), mesh=mesh,
        in_specs=(maps, P("dp"), P("dp"), P()) + weights + (maps,),
        out_specs=(maps, maps, P()) + weights, check_vma=False)
```

```python
import functools
from types import SimpleNamespace

import jax
import jax.numpy as jnp
from jax import lax
from jax.experimental import pallas as pl
from jax.experimental.pallas import tpu as pltpu
from jax.sharding import PartitionSpec as P

F32 = jnp.float32
BF = jnp.bfloat16
MESH = pl.DeviceIdType.MESH
EPS = 1e-06
GROUPS = 32
CHAN = 4
ROWS = 256
C = 256
SL = C // CHAN
GAP = 16
STEP = ROWS + GAP
TALL = 2 * ROWS + GAP
CH = 32
COUNT = ROWS * (C // GROUPS)


def dot(a, b):
    return jnp.dot(a, b, preferred_element_type=F32)


def dot_nt(a, b):
    return lax.dot_general(a, b, (((1,), (1,)), ((), ())), preferred_element_type=F32)


def sigmoid(u):
    return 0.5 * jnp.tanh(0.5 * u) + 0.5


def fold(v):
    return v.reshape(v.shape[0] // 8, 8, v.shape[1]).sum(axis=0)


def group_total(rows, bd):
    at = lax.broadcasted_iota(jnp.int32, (8, C), 0)
    stack = jnp.zeros((8, C), F32)
    for i, row in enumerate(rows):
        stack = jnp.where(at == i, row, stack)
    high = stack.astype(BF).astype(F32)
    rest = stack - high
    mid = rest.astype(BF).astype(F32)
    parts = jnp.concatenate([high, mid, rest - mid, jnp.zeros((8, C), F32)], axis=0)
    total = dot(parts.astype(BF), bd)
    total = total[0:8] + total[8:16] + total[16:24]
    return [total[i : i + 1] for i in range(len(rows))]


def chunk_at(i):
    return pl.multiple_of(i * CH, CH)


def passes(body, carry=None):
    carry = (0, 0) if carry is None else carry

    def step(i, held):
        return tuple(body(m, chunk_at(i), held[m]) for m in range(2))

    return lax.fori_loop(0, ROWS // CH, step, carry)


def zero_pair():
    return (jnp.zeros((8, C), F32), jnp.zeros((8, C), F32))


def col(v):
    return jnp.sum(v, axis=0, keepdims=True)


def write_shift(dst, m, at, value, forward):
    place = lax.broadcasted_iota(jnp.int32, (CH, C), 0) % 16
    before = jnp.where(place == 0, 0.0, pltpu.roll(value, 1, 0))
    after = jnp.where(place == 15, 0.0, pltpu.roll(value, CH - 1, 0))
    first, last = (before, after) if forward else (after, before)
    rows = pl.ds(pl.multiple_of(at + (GAP + m * STEP), 16), CH)
    dst[rows, 0:C] = first.astype(BF)
    dst[rows, C : 2 * C] = value.astype(BF)
    dst[rows, 2 * C : 3 * C] = last.astype(BF)


def norm_forward(load, n_ref, gain, shift, bd, emit, midway=None):
    def sums(m, at, held):
        return held + fold(load(m, at))

    total = passes(sums, zero_pair())
    mean = group_total([col(t) for t in total], bd)
    mean = [v * (1.0 / COUNT) for v in mean]

    def squares(m, at, held):
        d = load(m, at) - mean[m]
        return held + fold(d * d)

    total = passes(squares, zero_pair())
    var = group_total([col(t) for t in total], bd)
    rstd = [lax.rsqrt(v * (1.0 / COUNT) + EPS) for v in var]
    if midway is not None:
        midway()

    def last(m, at, held):
        n = (load(m, at) - mean[m]) * rstd[m]
        n_ref[pl.ds(pl.multiple_of(at + m * ROWS, CH), CH), :] = n
        emit(m, at, n * gain + shift)
        return held

    passes(last)
    return rstd


def norm_back(d_ref, n_ref, gain, shift, rstd, bd, active, e_ref, e_at, emit):
    def rows(m, at):
        return pl.ds(pl.multiple_of(at + m * STEP, 16), CH)

    def first(m, at, held):
        d = d_ref[rows(m, at), :]
        n = n_ref[pl.ds(pl.multiple_of(at + m * ROWS, CH), CH), :]
        if active:
            u = n * gain + shift
            s = sigmoid(u)
            d = d * (s * (1.0 + u * (1.0 - s)))
            d_ref[rows(m, at), :] = d
        return (held[0] + fold(d), held[1] + fold(d * n))

    total = passes(first, (zero_pair(), zero_pair()))
    ones = [col(t[0]) for t in total]
    twos = [col(t[1]) for t in total]
    e_ref[e_at : e_at + 1, :] = twos[0] + twos[1]
    e_ref[e_at + 1 : e_at + 2, :] = ones[0] + ones[1]
    means = group_total([gain * v for v in ones + twos], bd)
    means = [v * (1.0 / COUNT) for v in means]

    def second(m, at, held):
        d = d_ref[rows(m, at), :]
        n = n_ref[pl.ds(pl.multiple_of(at + m * ROWS, CH), CH), :]
        return emit(m, at, rstd[m] * (d * gain - means[m] - n * means[2 + m]), held)

    return second


def unpack(low, high):
    lane = lax.broadcasted_iota(jnp.int32, low.shape, 1)
    first = jnp.where(lane < SL, low, pltpu.roll(high, SL, 1))
    second = jnp.where(lane < SL, pltpu.roll(low, SL, 1), high)
    return first, second


def conv_forward(a_ref, w_ref, h_ref, ready, order):
    for row in order:
        ready(row)
        total = None
        for c in range(3):
            part = dot_nt(a_ref[16 * row : 16 * row + TALL, C * c : C * c + C], w_ref[3 * row + c])
            total = part if total is None else total + part
        h_ref[...] = total if row == order[0] else h_ref[...] + total


def conv_back(d_ref, w_ref, h_ref, between=None):
    for row in range(3):
        at = 16 * (2 - row)
        w = w_ref[3 * row : 3 * row + 3].reshape(3 * C, C)
        part = dot(d_ref[at : at + TALL, :], w)
        h_ref[...] = part if row == 0 else h_ref[...] + part
        if between is not None:
            between(row)


def conv_weight(a_ref, turned, dw_ref, row):
    for c in range(3):
        total = None
        for m in range(2):
            at = 16 * row + STEP * m
            part = dot(turned[m], a_ref[at : at + ROWS, C * c : C * c + C])
            total = part if total is None else total + part
        dw_ref[3 * row + c] = total.astype(BF)


class Group:
    def __init__(self, links):
        self.links, self.at, self.rows = links, links.used, 0
        links.used += 1

    def remote(self, src, dst, device):
        links, rows = self.links, rows_in(src)
        if links.sending + rows > links.idle.shape[0]:
            links.ended.append((links.senders, links.sending))
            links.senders, links.sending = links.senders + 1, 0
        links.sending += rows
        self.rows += rows
        pltpu.make_async_remote_copy(
            src_ref=src, dst_ref=dst, send_sem=links.send.at[links.senders], recv_sem=links.recv.at[self.at],
            device_id=device, device_id_type=MESH).start()

    def wait(self):
        self.links.wait_rows(self.links.recv.at[self.at], self.rows)


def rows_in(ref):
    size = ref.dtype.itemsize
    for n in ref.shape:
        size *= n
    return size // 256


class Links:
    def __init__(self, send, recv, own, idle):
        self.send, self.recv, self.own, self.idle = send, recv, own, idle
        self.used, self.local, self.senders, self.sending = 0, 0, 0, 0
        self.ended = []

    def wait_rows(self, semaphore, rows):
        view = self.idle.at[0:rows]
        pltpu.make_async_copy(view, view, semaphore).wait()

    def group(self, copies=()):
        group = Group(self)
        for src, dst, device in copies:
            group.remote(src, dst, device)
        return group

    def here(self, src, dst):
        copy = pltpu.make_async_copy(src, dst, self.own.at[self.local])
        self.local += 1
        copy.start()
        return copy

    def close(self):
        for at, rows in self.ended + [(self.senders, self.sending)]:
            self.wait_rows(self.send.at[at], rows)


def block_sizes(n_dp):
    team = min(8, n_dp)
    return team, n_dp // team


def aligned(start, size):
    return pl.ds(pl.multiple_of(start, size), size)


def reduction_scratch(taps, order, spread, team, teams):
    rows, span = SL * taps, SL * taps // (team // 2)
    left = rows if spread is None else span
    shapes = dict(rc=(2, taps, SL, C), s0=(2, 2, rows, 128), pc=(1, 1, left, 128), rt=(teams, 1, 1, left, 128))
    if spread is None:
        shapes.update({f"c{i}": (1, 1, rows, 128) for i in range(3)})
    size = dict(y=2, x=2, z=team // 2)
    for k, axes in enumerate(order):
        peers = 1
        for axis in axes:
            peers *= size[axis]
            size[axis] = 1
        shape = (size["y"], size["x"], size["z"] * span, 128)
        shapes[f"r{k}"] = (max(peers - 1, 1),) + shape
        shapes[f"s{k + 1}"] = shape
    buffers = {name: pltpu.VMEM(shape, BF) for name, shape in shapes.items()}
    if spread is None:
        buffers.update(cs=pltpu.SemaphoreType.DMA((3,)), cr=pltpu.SemaphoreType.DMA((3,)))
    return buffers


class Reduction:
    def __init__(self, at, links, grad, out, work, order, spread):
        self.at, self.links, self.grad, self.out, self.w = at, links, grad, out, work
        self.order, self.spread = order, spread
        self.taps = grad.shape[0]
        self.span = SL * self.taps // (at.team // 2)
        self.size = dict(y=2, x=2, z=at.team // 2)
        self.stage = -1
        self.whole = dict(y=True, x=True, z=True)
        w = self.w
        self.group = links.group([
            (grad.at[:, aligned(SL * (2 * y + 1 - at.core), SL), :], w.rc.at[y], at.sibling) for y in range(2)])

    def view(self, ref, place):
        parts = []
        for axis in "yx":
            parts.append(pl.ds(place[axis], 1) if axis in place and self.whole[axis] else slice(None))
        if "z" in place and self.whole["z"]:
            parts.append(aligned(self.span * place["z"], self.span))
        else:
            parts.append(slice(None))
        return ref.at[tuple(parts)]

    def peers(self, axes):
        steps = [{}]
        for axis in axes:
            steps = [{**step, axis: s} for step in steps for s in range(self.size[axis])]
        for step in steps[1:]:
            yield {axis: (self.at.place[axis] + s) % self.size[axis] for axis, s in step.items()}

    def send(self):
        axes = self.order[self.stage]
        current, arriving = getattr(self.w, f"s{self.stage}"), getattr(self.w, f"r{self.stage}")
        self.group = self.links.group([
            (self.view(current, place), arriving.at[slot], self.at.peer(place))
            for slot, place in enumerate(self.peers(axes))])

    def collect(self):
        at, w = self.at, self.w
        if self.group.rows:
            self.group.wait()
        if self.stage < 0:
            for y in range(2):
                for t in range(self.taps):
                    mine = self.grad[t, aligned(SL * (2 * y + at.core), SL), :].astype(F32)
                    total = (mine + w.rc[y, t].astype(F32)).astype(BF)
                    for half in range(2):
                        w.s0[y, half, SL * t : SL * t + SL, :] = total[:, 128 * half : 128 * half + 128]
            return
        axes = self.order[self.stage]
        current, arriving = getattr(w, f"s{self.stage}"), getattr(w, f"r{self.stage}")
        total = self.view(current, {axis: at.place[axis] for axis in axes})[...].astype(F32)
        for slot in range(len(list(self.peers(axes)))):
            total = total + arriving[slot].astype(F32)
        getattr(w, f"s{self.stage + 1}")[...] = total.astype(BF)
        for axis in axes:
            self.whole[axis] = False

    def across_teams(self, piece):
        at, w = self.at, self.w
        own = self.links.here(piece, w.rt.at[at.lead])
        group = self.links.group([
            (piece, w.rt.at[at.lead], at.device((at.lead + s) % at.teams * at.team + at.rank))
            for s in range(1, at.teams)])
        own.wait()
        group.wait()
        total = w.rt[0].astype(F32)
        for s in range(1, at.teams):
            total = total + w.rt[s].astype(F32)
        w.pc[...] = total.astype(BF)
        return w.pc

    def region(self, axes):
        place = self.at.place
        rows = slice(None) if "z" in axes else aligned(self.span * place["z"], self.span)
        return self.out.at[:, pl.ds(place["x"], 1), rows]

    def advance(self):
        last = len(self.order)
        if self.stage < last:
            self.collect()
        self.stage += 1
        if self.stage < last:
            self.send()
            return
        axes = self.spread[self.stage - last]
        if self.stage == last:
            source = getattr(self.w, f"s{last}")
            if self.at.teams > 1:
                source = self.across_teams(source)
            target = self.region("")
            self.own = self.links.here(source, target)
        else:
            if self.stage == last + 1:
                self.own.wait()
            if self.group.rows:
                self.group.wait()
            source = target = self.region("".join(self.spread[: self.stage - last]))
        self.group = self.links.group([(source, target, self.at.peer(place)) for place in self.peers(axes)])

    def finish(self):
        if self.spread is None or len(self.spread) == 1:
            self.own.wait()
        if self.group.rows:
            self.group.wait()


class Chain(Reduction):
    def copy(self, step, src, dst, z):
        w = self.w
        return pltpu.make_async_remote_copy(
            src_ref=src, dst_ref=dst, send_sem=w.cs.at[step], recv_sem=w.cr.at[step],
            device_id=self.at.peer(dict(z=z)), device_id_type=MESH)

    def prepare(self):
        z, w = self.at.place["z"], self.w
        total = getattr(w, f"s{len(self.order)}")
        count = self.size["z"]
        self.end = (z == 0) | (z == count - 1)
        self.inner = jnp.logical_not(self.end)
        middle = jnp.where(z < 2, 1, 2)
        self.inward = self.copy(0, total, w.c0, middle)
        self.swap = self.copy(1, w.c1, w.c2, count - 1 - z)
        self.outward = self.copy(2, w.pc, w.pc, jnp.where(z < 2, 0, 3))
        return total

    def advance(self):
        w, last = self.w, len(self.order)
        if self.stage < last - 1:
            self.collect()
            self.stage += 1
            self.send()
            return
        long, alone = self.size["z"] == 4, self.size["z"] == 1
        if self.stage == last - 1:
            self.collect()
            total = self.prepare()
            if long:
                pl.when(self.end)(self.inward.start)
            else:
                w.c1[...] = total[...]
        elif self.stage == last:
            if long:
                @pl.when(self.inner)
                def _():
                    self.inward.wait_recv()
                    total = getattr(w, f"s{last}")[...].astype(F32) + w.c0[...].astype(F32)
                    w.c1[...] = total.astype(BF)
                    self.swap.start()
            elif not alone:
                self.swap.start()
        elif self.stage == last + 1:
            def join():
                self.swap.wait_recv()
                w.pc[...] = (w.c1[...].astype(F32) + w.c2[...].astype(F32)).astype(BF)

            if long:
                @pl.when(self.inner)
                def _():
                    join()
                    self.outward.start()
            elif alone:
                w.pc[...] = w.c1[...]
            else:
                join()
        else:
            if long:
                pl.when(self.end)(self.outward.wait_recv)
                pl.when(self.end)(self.inward.wait_send)

                @pl.when(self.inner)
                def _():
                    self.swap.wait_send()
                    self.outward.wait_send()
            elif not alone:
                self.swap.wait_send()
            source = self.across_teams(w.pc) if self.at.teams > 1 else w.pc
            target = self.region("z")
            self.own = self.links.here(source, target)
            self.group = self.links.group([(source, target, self.at.peer(place)) for place in self.peers("x")])
        self.stage += 1


YX, XY, YXZ, XYZ = ("y", "x"), ("x", "y"), ("y", "x", "z"), ("x", "y", "z")
STEPS, ONCE = ("z", "x"), ("zx",)
ITEMS = {
    "ga": (4, YX, None), "gb0": (3, XY, None), "gb1": (3, YX, None), "gb2": (3, YX, None),
    "gc0": (3, YXZ, STEPS), "gc1": (3, XYZ, STEPS), "gc2": (3, YXZ, ONCE)}
GAINS = ("gain1", "shift1", "gain2", "shift2", "gain3", "shift3")


def mega(n_dp, names, *refs):
    r = SimpleNamespace(**dict(zip(names, refs)))
    team, teams = block_sizes(n_dp)
    dp, chan = lax.axis_index("dp"), lax.axis_index("chan")
    core, y, bit = chan % 2, chan // 2, dp % 2
    sibling, across, corner = (dp, 2 * y + 1 - core), (dp, 2 * (1 - y) + core), (dp, 2 * (1 - y) + 1 - core)
    beside, oblique = (dp + 1 - 2 * bit, chan), (dp + 1 - 2 * bit, 2 * (1 - y) + core)
    quads = (sibling, across, corner)
    rank, lead = dp % team, dp // team
    own_place = dict(y=y, x=bit, z=rank // 2)

    def peer(place):
        place = {**own_place, **place}
        return (lead * team + 2 * place["z"] + place["x"], 2 * place["y"] + core)

    at = SimpleNamespace(core=core, sibling=sibling, team=team, teams=teams, rank=rank, lead=lead, place=own_place,
                         peer=peer, device=lambda p: (p, chan))
    links = Links(r.send, r.recv, r.own, r.idle)

    def others():
        return [(lax.rem(dp + s, n_dp), chan) for s in range(1, n_dp)]

    barrier = pltpu.get_barrier_semaphore()
    for device in quads + (oblique,) + tuple(others()):
        pl.semaphore_signal(barrier, inc=1, device_id=device, device_id_type=MESH)
    load_x, load_ts, load_table = links.here(r.x, r.xl), links.here(r.ts, r.tss), links.here(r.table, r.tab)
    load_par = [links.here(getattr(r, name), r.pin.at[i]) for i, name in enumerate(GAINS)]
    load_we, load_dy, load_cnt = links.here(r.we, r.wel), links.here(r.dy, r.dyl), links.here(r.cnt, r.cns)
    mine = aligned(SL * chan, SL)
    fill = [
        links.here(r.w1, r.w1g.at[:, mine, :]), links.here(r.w2, r.w2g.at[:, mine, :]),
        links.here(r.we, r.weg.at[:, mine, :]),
        links.here(r.wq, r.wqg.at[0:3, mine, :]), links.here(r.wo, r.wqg.at[3:4, mine, :])]

    def pack(src, dst):
        for k in range(CHAN):
            for half in range(2):
                rows = slice(128 * half, 128 * half + 128)
                both = jnp.concatenate([src[2 * k, rows, :].astype(F32), src[2 * k + 1, rows, :].astype(F32)], axis=1)
                dst[k, rows, :] = both.astype(BF)

    load_x.wait()
    pack(r.xl, r.xp)
    for copy in load_par:
        copy.wait()
    r.par[...] = jnp.zeros((8, 128), F32)
    for i in range(len(GAINS)):
        r.par[i : i + 1, 0:SL] = r.pin[i].astype(F32)
    pl.semaphore_wait(barrier, CHAN + n_dp - 1)

    part = 32 * bit
    far = SL * (2 * (1 - y) + core)

    class Share:
        def __init__(self, w, g, half):
            self.w, self.g, self.half = w, g, half
            self.from_sibling = links.group()
            rows = (part, 32) if half else (0, SL)
            self.over = links.group([
                (w.at[:, aligned(*rows), :], g.at[:, aligned(SL * chan + rows[0], rows[1]), :], across)])

        def own(self):
            self.from_sibling.remote(self.w, self.g.at[:, mine, :], sibling)

        def relay(self):
            self.over.wait()
            if self.half:
                piece = self.g.at[:, aligned(far + part, 32), :]
                self.around = links.group([(piece, piece, beside)])
            else:
                piece = self.g.at[:, aligned(far, SL), :]
            self.from_sibling.remote(piece, piece, sibling)

        def relay_again(self):
            self.around.wait()
            piece = self.g.at[:, aligned(far + 32 - part, 32), :]
            self.from_sibling.remote(piece, piece, sibling)

        def landed(self):
            self.from_sibling.wait()

    def rows3(ref, row):
        return ref.at[3 * row : 3 * row + 3]

    one = [Share(rows3(r.w1, row), rows3(r.w1g, row), True) for row in range(3)]
    for share in one:
        share.own()
    moves_x = links.group(
        [(r.xp.at[d[1]], r.xg.at[chan], d) for d in quads] + [(r.par, r.pg.at[chan], d) for d in quads])

    load_ts.wait()
    row8 = lax.broadcasted_iota(jnp.int32, (8, 128), 0)
    times = jnp.zeros((8, 128), F32)
    for i in range(8):
        times = jnp.where(row8 == i, r.tss[i].astype(F32), times)
    r.tl[...] = times
    r.ta[dp] = times
    steps = r.table.shape[0]
    load_table.wait()

    def embeddings(times):
        count = times.shape[0]
        wide = jnp.broadcast_to(times[:, 0:1], (count, steps))
        hot = jnp.where(wide == lax.broadcasted_iota(jnp.int32, (count, steps), 1).astype(F32), 1.0, 0.0)
        temb = dot(hot.astype(BF), r.tab[...])
        s = sigmoid(temb)
        return temb, s, (temb * s).astype(BF)

    _, _, tsil = embeddings(jnp.concatenate([times, times], axis=0))
    load_we.wait()
    r.el[...] = jnp.zeros((8, 128), F32)
    r.el[:, 0:SL] = dot_nt(tsil, r.wel[0])[0:8]
    r.eg[chan] = r.el[...]
    moves_emb = links.group([(r.el, r.eg.at[chan], d) for d in quads])
    two = [Share(rows3(r.w2, row), rows3(r.w2g, row), row < 2) for row in range(3)]
    out = [Share(r.wq, r.wqg.at[0:3], False), Share(r.wo, r.wqg.at[3:4], False)]
    for share in two + out:
        share.own()
    load_dy.wait()
    pack(r.dyl, r.dyp)
    moves_late = links.group([(r.tl, r.ta.at[dp], d) for d in others()])
    r.dyg[chan] = r.dyp[chan]
    moves_dy = links.group([(r.dyp.at[d[1]], r.dyg.at[chan], d) for d in quads])
    mix = Share(r.we, r.weg, False)
    mix.own()
    at_row = lax.broadcasted_iota(jnp.int32, (C, C), 0) // (C // GROUPS)
    at_col = lax.broadcasted_iota(jnp.int32, (C, C), 1) // (C // GROUPS)
    r.bd[...] = jnp.where(at_row == at_col, 1.0, 0.0).astype(BF)
    for ref in (r.a1, r.a2, r.dd):
        for gap in range(3):
            ref[gap * STEP : gap * STEP + GAP, :] = jnp.zeros((GAP, 3 * C), BF)
    r.xg[chan] = r.xp[chan]
    r.pg[chan] = r.par[...]
    for share in one:
        share.relay()
    one[0].relay_again()
    one[1].relay_again()

    bd = r.bd[...]
    moves_x.wait()
    for b in range(2):
        first, _ = unpack(r.pg[2 * b], r.pg[2 * b + 1])
        r.pa[:, 128 * b : 128 * b + 128] = first
    par = r.pa[...]
    gain1, shift1, gain2, shift2, gain3, shift3 = [par[i : i + 1] for i in range(6)]

    def spread_out(src, at, dst, scale=None):
        for b in range(2):
            pair = unpack(src[2 * b, pl.ds(at, CH), :].astype(F32), src[2 * b + 1, pl.ds(at, CH), :].astype(F32))
            for m in range(2):
                value = pair[m] if scale is None else pair[m] * scale[m]
                dst[pl.ds(pl.multiple_of(at + m * ROWS, CH), CH), 128 * b : 128 * b + 128] = value.astype(dst.dtype)

    def open_x(i, held):
        spread_out(r.xg, chunk_at(i), r.xf)
        return held

    lax.fori_loop(0, ROWS // CH, open_x, 0)

    def rows_of(m, at):
        return pl.ds(pl.multiple_of(at + m * ROWS, CH), CH)

    def rows_gap(m, at):
        return pl.ds(pl.multiple_of(at + m * STEP, 16), CH)

    def to_shift(dst):
        def emit(m, at, u):
            write_shift(dst, m, at, u * sigmoid(u), True)
        return emit

    rstd1 = norm_forward(lambda m, at: r.xf[rows_of(m, at), :], r.n1, gain1, shift1, bd, to_shift(r.a1),
                         one[2].relay_again)
    for copy in fill:
        copy.wait()

    def ready_one(row):
        if row == 2:
            two[0].relay()
        one[row].landed()

    conv_forward(r.a1, r.w1g, r.h, ready_one, (0, 1, 2))
    two[1].relay()
    moves_emb.wait()
    for b in range(2):
        first, _ = unpack(r.eg[2 * b], r.eg[2 * b + 1])
        r.emb[:, 128 * b : 128 * b + 128] = first
    emb = [r.emb[pl.ds(2 * chan + m, 1), :] for m in range(2)]
    rstd2 = norm_forward(lambda m, at: r.h[rows_gap(m, at), :] + emb[m], r.n2, gain2, shift2, bd, to_shift(r.a2))
    two[2].relay()
    two[0].relay_again()

    def ready_two(row):
        if row == 0:
            two[1].relay_again()
        if row == 1:
            for share in out:
                share.relay()
        two[row].landed()

    conv_forward(r.a2, r.w2g, r.h, ready_two, (2, 0, 1))

    def load_resid(m, at):
        return r.xf[rows_of(m, at), :] + r.h[rows_gap(m, at), :]

    def to_a3(m, at, u):
        r.a3[rows_of(m, at), :] = u.astype(BF)

    rstd3 = norm_forward(load_resid, r.n3, gain3, shift3, bd, to_a3)
    out[0].landed()
    for j, ref in enumerate((r.q, r.k, r.v)):
        ref[...] = dot_nt(r.a3[...], r.wqg[j]).astype(BF)
    mix.relay()
    load_cnt.wait()
    count = r.cns[0]
    live = [jnp.where(2 * chan + m < count, 1.0, 0.0).astype(F32) for m in range(2)]
    scale = C ** (-0.5)
    half = [slice(0, ROWS), slice(ROWS, 2 * ROWS)]
    for m in range(2):
        s = dot_nt(r.q[half[m], :], r.k[half[m], :]) * scale
        p = jnp.exp(s - jnp.max(s, axis=1, keepdims=True))
        p = p * (1.0 / jnp.sum(p, axis=1, keepdims=True))
        r.p[half[m], :] = p
        r.pb[half[m], :] = p.astype(BF)
        r.o[half[m], :] = dot(p.astype(BF), r.v[half[m], :]).astype(BF)
    out[1].landed()
    r.big[...] = dot_nt(r.o[...], r.wqg[3])

    def pack_out(at, pair, dst):
        for b in range(2):
            even, odd = unpack(*(v[:, 128 * b : 128 * b + 128] for v in pair))
            dst[2 * b, pl.ds(at, CH), :] = even.astype(BF)
            dst[2 * b + 1, pl.ds(at, CH), :] = odd.astype(BF)

    def to_y(i, held):
        at = chunk_at(i)
        pack_out(at, [(load_resid(m, at) + r.big[rows_of(m, at), :]) * live[m] for m in range(2)], r.yp)
        return held

    lax.fori_loop(0, ROWS // CH, to_y, 0)
    own_y = links.here(r.yp.at[chan], r.yo.at[chan])
    moves_out = links.group([(r.yp.at[d[1]], r.yo.at[chan], d) for d in quads])

    moves_dy.wait()

    def open_dy(i, held):
        spread_out(r.dyg, chunk_at(i), r.g, live)
        return held

    lax.fori_loop(0, ROWS // CH, open_dy, 0)
    for m in range(2):
        r.turn[m] = r.g[half[m], :].T
    r.dqo[3] = (dot(r.turn[0], r.o[half[0], :]) + dot(r.turn[1], r.o[half[1], :])).astype(BF)
    r.do[...] = dot(r.g[...], r.wqg[3]).astype(BF)
    for m in range(2):
        dp_m = dot_nt(r.do[half[m], :], r.v[half[m], :])
        p = r.p[half[m], :]
        ds = (p * (dp_m - jnp.sum(p * dp_m, axis=1, keepdims=True)) * scale).astype(BF)
        r.dv[half[m], :] = dot(r.pb[half[m], :].T, r.do[half[m], :]).astype(BF)
        r.dq[half[m], :] = dot(ds, r.k[half[m], :]).astype(BF)
        r.dk[half[m], :] = dot(ds.T, r.q[half[m], :]).astype(BF)
    for j, ref in enumerate((r.dq, r.dk, r.dv)):
        parts = [dot(ref[half[m], :].T, r.a3[half[m], :]) for m in range(2)]
        r.dqo[j] = (parts[0] + parts[1]).astype(BF)

    def reduction(name, grad):
        _, order, spread = ITEMS[name]
        work = SimpleNamespace(**{k[len(name) + 1 :]: getattr(r, k) for k in names if k.startswith(name + "_")})
        kind = Chain if spread is None else Reduction
        return kind(at, links, grad, getattr(r, name), work, order, spread)

    ga = reduction("ga", r.dqo)
    for m in range(2):
        total = None
        for j, ref in enumerate((r.dq, r.dk, r.dv)):
            part_j = dot(ref[half[m], :], r.wqg[j])
            total = part_j if total is None else total + part_j
        r.h[m * STEP : m * STEP + ROWS, :] = total
    ga.advance()

    def to_dres(m, at, dv, held):
        value = r.g[rows_of(m, at), :].astype(F32) + dv
        r.dres[rows_of(m, at), :] = value
        write_shift(r.dd, m, at, value, False)
        return held

    passes(norm_back(r.h, r.n3, gain3, shift3, rstd3, bd, False, r.e, 4, to_dres))

    def turn():
        for m in range(2):
            r.turn[m] = r.dd[GAP + STEP * m : GAP + STEP * m + ROWS, C : 2 * C].T

    turn()
    gb = []
    for row in range(3):
        conv_weight(r.a2, r.turn, r.dw2, row)
        gb.append(reduction(f"gb{row}", rows3(r.dw2, row)))
    def between(row):
        if row == 0:
            gb[0].advance()
            gb[1].advance()
        if row == 1:
            gb[2].advance()

    conv_back(r.dd, r.w2g, r.h, between)

    def to_dh1(m, at, dv, held):
        write_shift(r.dd, m, at, dv, False)
        return held + fold(dv)

    demb = passes(norm_back(r.h, r.n2, gain2, shift2, rstd2, bd, True, r.e, 2, to_dh1), zero_pair())
    for m in range(2):
        r.dm[chan, m : m + 1, :] = col(demb[m]).astype(BF).astype(F32)
    moves_dm = links.group([(r.dm.at[chan], r.dm.at[chan], d) for d in quads])
    turn()
    gc = []
    for row in range(3):
        conv_weight(r.a1, r.turn, r.dw1, row)
        gc.append(reduction(f"gc{row}", rows3(r.dw1, row)))
        if row == 1:
            gc[0].advance()
            ga.advance()
    for item in (gb[0], gc[1], gb[1], gc[2]):
        item.advance()
    conv_back(r.dd, r.w1g, r.h)
    for item in (ga, gb[2]):
        item.advance()
    back1 = norm_back(r.h, r.n1, gain1, shift1, rstd1, bd, True, r.e, 0,
                      lambda m, at, dv, held: r.dres[rows_of(m, at), :] + dv)

    def to_maps(i, held):
        at = chunk_at(i)
        pack_out(at, [back1(m, at, 0) for m in range(2)], r.mp)
        return held

    lax.fori_loop(0, ROWS // CH, to_maps, 0)
    own_mp = links.here(r.mp.at[chan], r.mo.at[chan])
    for d in quads:
        moves_out.remote(r.mp.at[d[1]], r.mo.at[chan], d)
    moves_dm.wait()
    for j in range(CHAN):
        r.dl[2 * j : 2 * j + 2, :] = r.dm[j, 0:2, :]
    r.ra[dp] = r.dl[...]
    for d in others():
        moves_late.remote(r.dl, r.ra.at[dp], d)
    for b in range(2):
        block = r.e[:, 128 * b : 128 * b + 128]
        r.es[2 * b] = block
        r.es[2 * b + 1] = pltpu.roll(block, SL, 1)
    r.er[chan] = r.es[chan]
    moves_e = links.group([(r.es.at[d[1]], r.er.at[chan], d) for d in quads])
    for item in (gb[1], gc[0], gc[1], gb[0], gb[2], ga, gb[1], gc[2], gc[0], gc[1], gb[0], gb[2]):
        item.advance()
    moves_e.wait()
    r.et[...] = r.er[0] + r.er[1] + r.er[2] + r.er[3]
    own_e = links.here(r.et, r.ext.at[dp])
    for d in others():
        moves_out.remote(r.et, r.ext.at[dp], d)
    for item in (ga, gb[1], gc[2]):
        item.advance()
    mix.landed()
    moves_late.wait()
    maps = 8 * n_dp
    temb, s, tsil = embeddings(r.ta[...].reshape(maps, 128))
    rows = r.ra[...].reshape(maps, C)
    r.rt[...] = rows.T
    r.dew[...] = dot(r.rt[mine, :].astype(BF), tsil)
    dtemb = dot(rows.astype(BF), r.weg[0]) * (s * (1.0 + temb * (1.0 - s)))
    high = dtemb.astype(BF)
    r.bw[0:maps, :] = high
    r.bw[maps:, :] = (dtemb - high.astype(F32)).astype(BF)
    ends = [links.here(r.dew, r.de), links.here(r.bw, r.both), links.here(r.ta, r.tall)]
    for item in (gc[0], gb[0], gb[2], gc[1], gb[1], ga, gc[2], gb[0], gb[2], gc[0], gc[1]):
        item.advance()
    for item in [ga] + gb + gc:
        item.finish()
    for copy in [own_y, own_mp, own_e] + ends:
        copy.wait()
    moves_out.wait()
    links.close()


def finish(n_dp, names, *refs):
    r = SimpleNamespace(**dict(zip(names, refs)))
    maps = 8 * n_dp
    steps = r.dt.shape[0]
    links = Links(None, None, r.own, None)
    items = list(ITEMS)
    load = {name: links.here(getattr(r, name), getattr(r, name + "_v"))
            for name in ["tall", "both", "yo", "mo"] + items + ["ext"]}
    stores = [links.here(r.de, r.de_out)]

    def out(src, dst):
        stores.append(links.here(src, dst))

    load["tall"].wait()
    load["both"].wait()
    lanes = r.tall_v[...].reshape(maps, 128).T[0:1, :]
    lanes = jnp.concatenate([lanes, lanes], axis=1)
    for start in range(0, steps, 256):
        size = min(256, steps - start)
        ids = lax.broadcasted_iota(jnp.int32, (size, 2 * maps), 0).astype(F32) + float(start)
        hot = jnp.where(ids == lanes, 1.0, 0.0).astype(BF)
        r.dt_v[start : start + size, :] = dot(hot, r.both_v[...])
        out(r.dt_v.at[start : start + size], r.dt.at[start : start + size])

    def unpack_maps(name, dst, dst_v):
        load[name].wait()
        src = getattr(r, name + "_v")
        for j in range(CHAN):
            block = src[j].astype(F32)
            dst_v[2 * j] = block[:, 0:SL].astype(BF)
            dst_v[2 * j + 1] = pltpu.roll(block, SL, 1)[:, 0:SL].astype(BF)
        out(dst_v, dst)

    def whole(name, dst_v, base, taps):
        src = getattr(r, name + "_v")
        for i, t in enumerate(taps):
            for half in range(2):
                dst_v[base + i, :, 128 * half : 128 * half + 128] = src[0, half, SL * t : SL * t + SL, :].astype(F32)

    unpack_maps("yo", r.y, r.y_v)
    unpack_maps("mo", r.dm, r.dm_v)
    load["ga"].wait()
    whole("ga", r.dq_v, 0, range(3))
    out(r.dq_v, r.dq)
    whole("ga", r.do_v, 0, [3])
    out(r.do_v, r.do)
    for kind, dst_v, dst in (("gb", r.d2_v, r.d2), ("gc", r.d1_v, r.d1)):
        for row in range(3):
            load[f"{kind}{row}"].wait()
            whole(f"{kind}{row}", dst_v, 3 * row, range(3))
            out(dst_v.at[3 * row : 3 * row + 3], dst.at[3 * row : 3 * row + 3])
    load["ext"].wait()
    total = r.ext_v[0]
    for i in range(1, n_dp):
        total = total + r.ext_v[i]
    for i in range(6):
        r.gains_v[i] = total[i : i + 1, 0:SL]
        out(r.gains_v.at[i], getattr(r, f"e{i}"))
    for copy in stores:
        copy.wait()


def per_device(x_maps, timesteps, counts, emb_table, w_first, w_second, w_embed, w_qkv, w_out, gain_one, shift_one,
               gain_two, shift_two, gain_three, shift_three, cotangent, *, n_dp):
    team, teams = block_sizes(n_dp)
    slots, side, _, _ = x_maps.shape
    emb = w_embed.shape[0]
    steps = emb_table.shape[0]
    inputs = dict(
        x=x_maps.reshape(slots, side * side, SL), dy=cotangent.reshape(slots, side * side, SL),
        ts=timesteps, cnt=counts, table=emb_table,
        w1=jnp.swapaxes(w_first, 2, 3).reshape(9, SL, C), w2=jnp.swapaxes(w_second, 2, 3).reshape(9, SL, C),
        we=w_embed.T[None], wq=jnp.transpose(w_qkv, (1, 2, 0)), wo=w_out.T[None])
    gains = (gain_one, shift_one, gain_two, shift_two, gain_three, shift_three)
    inputs.update({name: v.reshape(1, SL) for name, v in zip(GAINS, gains)})
    anywhere = pl.BlockSpec(memory_space=pl.ANY)

    def of(shape, dtype):
        return jax.ShapeDtypeStruct(shape, dtype)

    maps = 8 * n_dp
    middle = dict(
        yo=of((CHAN, ROWS, 128), BF), mo=of((CHAN, ROWS, 128), BF), tall=of((n_dp, 8, 128), F32),
        ext=of((n_dp, 8, 128), F32), both=of((2 * maps, emb), BF), de=of((SL, emb), F32))
    middle.update({name: of((1, 2, SL * item[0], 128), BF) for name, item in ITEMS.items()})
    v = pltpu.VMEM
    maps2 = 2 * ROWS
    scratch = dict(
        xl=v((slots, ROWS, SL), BF), dyl=v((slots, ROWS, SL), BF), pin=v((len(GAINS), 1, SL), BF),
        tss=pltpu.SMEM((slots,), jnp.int32), cns=pltpu.SMEM((1,), jnp.int32), tab=v((steps, emb), BF),
        xp=v((CHAN, ROWS, 128), BF), dyp=v((CHAN, ROWS, 128), BF),
        xg=v((CHAN, ROWS, 128), BF), dyg=v((CHAN, ROWS, 128), BF),
        yp=v((CHAN, ROWS, 128), BF), mp=v((CHAN, ROWS, 128), BF),
        w1g=v((9, C, C), BF), w2g=v((9, C, C), BF), weg=v((1, C, emb), BF), wqg=v((4, C, C), BF),
        bd=v((C, C), BF), tl=v((8, 128), F32), ta=v((n_dp, 8, 128), F32), par=v((8, 128), F32),
        pg=v((CHAN, 8, 128), F32), pa=v((8, C), F32), emb=v((8, C), F32),
        wel=v((1, SL, emb), BF), el=v((8, 128), F32), eg=v((CHAN, 8, 128), F32),
        a1=v((TALL + 2 * GAP, 3 * C), BF), a2=v((TALL + 2 * GAP, 3 * C), BF), dd=v((TALL + 2 * GAP, 3 * C), BF),
        h=v((TALL, C), F32), xf=v((maps2, C), F32), n1=v((maps2, C), F32), n2=v((maps2, C), F32),
        n3=v((maps2, C), F32), dres=v((maps2, C), F32), big=v((maps2, C), F32), p=v((maps2, C), F32),
        e=v((8, C), F32), es=v((CHAN, 8, 128), F32), er=v((CHAN, 8, 128), F32), et=v((8, 128), F32),
        dm=v((CHAN, 8, C), F32), dl=v((8, C), F32), ra=v((n_dp, 8, C), F32), rt=v((C, maps), F32),
        dew=v((SL, emb), F32), bw=v((2 * maps, emb), BF), turn=v((2, ROWS, C), BF),
        dw1=v((9, C, C), BF), dw2=v((9, C, C), BF), dqo=v((4, C, C), BF))
    for name in ("a3", "q", "k", "v", "pb", "o", "g", "do", "dq", "dk", "dv"):
        scratch[name] = v((maps2, C), BF)
    for name, (taps, order, spread) in ITEMS.items():
        buffers = reduction_scratch(taps, order, spread, team, teams)
        scratch.update({name + "_" + k: b for k, b in buffers.items()})
    groups = 48 + len(ITEMS) * 7
    scratch.update(
        idle=v((4096, 128), BF), send=pltpu.SemaphoreType.DMA((24,)), recv=pltpu.SemaphoreType.DMA((groups,)),
        own=pltpu.SemaphoreType.DMA((40,)))
    got = pl.pallas_call(
        functools.partial(mega, n_dp, list(inputs) + list(middle) + list(scratch)),
        out_shape=tuple(middle.values()),
        in_specs=[anywhere] * len(inputs),
        out_specs=(anywhere,) * len(middle),
        scratch_shapes=list(scratch.values()),
        compiler_params=pltpu.CompilerParams(collective_id=0, has_side_effects=True, vmem_limit_bytes=60 << 20),
        name="blocks",
    )(*inputs.values())
    results = dict(
        y=of((slots, ROWS, SL), BF), dm=of((slots, ROWS, SL), BF), dt=of((steps, emb), F32), d1=of((9, SL, C), F32),
        d2=of((9, SL, C), F32), de_out=of((SL, emb), F32), dq=of((3, SL, C), F32), do=of((1, SL, C), F32))
    results.update({f"e{i}": of((1, SL), F32) for i in range(6)})
    scratch = {name + "_v": v(o.shape, o.dtype) for name, o in middle.items() if name != "de"}
    scratch.update({name + "_v": v(o.shape, o.dtype) for name, o in results.items() if name[0] != "e"})
    scratch.update(gains_v=v((6, 1, SL), F32), own=pltpu.SemaphoreType.DMA((48,)))
    got = pl.pallas_call(
        functools.partial(finish, n_dp, list(middle) + list(results) + list(scratch)),
        out_shape=tuple(results.values()),
        in_specs=[anywhere] * len(middle),
        out_specs=(anywhere,) * len(results),
        scratch_shapes=list(scratch.values()),
        compiler_params=pltpu.CompilerParams(vmem_limit_bytes=60 << 20),
        name="finish",
    )(*got)
    got = dict(zip(results, got))
    return (
        got["y"].reshape(x_maps.shape), got["dm"].reshape(x_maps.shape), got["dt"],
        jnp.swapaxes(got["d1"].reshape(3, 3, SL, C), 2, 3), jnp.swapaxes(got["d2"].reshape(3, 3, SL, C), 2, 3),
        got["de_out"].T, jnp.transpose(got["dq"], (2, 0, 1)), got["do"].reshape(SL, C).T,
    ) + tuple(got[f"e{i}"].reshape(SL) for i in range(6))


def solution(mesh):
    weights = (P(None, None, None, "chan"), P(None, None, None, "chan"), P(None, "chan"), P(None, None, "chan"),
               P(None, "chan")) + (P("chan"),) * 6
    maps = P("dp", None, None, "chan")
    return jax.shard_map(
        functools.partial(per_device, n_dp=mesh.shape["dp"]), mesh=mesh,
        in_specs=(maps, P("dp"), P("dp"), P()) + weights + (maps,),
        out_specs=(maps, maps, P()) + weights, check_vma=False)
```

```python
import functools
from types import SimpleNamespace

import jax
import jax.numpy as jnp
from jax import lax
from jax.experimental import pallas as pl
from jax.experimental.pallas import tpu as pltpu
from jax.sharding import PartitionSpec as P

F32 = jnp.float32
BF = jnp.bfloat16
MESH = pl.DeviceIdType.MESH
EPS = 1e-06
GROUPS = 32
CHAN = 4
ROWS = 256
C = 256
SL = C // CHAN
GAP = 16
STEP = ROWS + GAP
TALL = 2 * ROWS + GAP
CH = 32
COUNT = ROWS * (C // GROUPS)


def dot(a, b):
    return jnp.dot(a, b, preferred_element_type=F32)


def dot_nt(a, b):
    return lax.dot_general(a, b, (((1,), (1,)), ((), ())), preferred_element_type=F32)


def sigmoid(u):
    return 0.5 * jnp.tanh(0.5 * u) + 0.5


def fold(v):
    return v.reshape(v.shape[0] // 8, 8, v.shape[1]).sum(axis=0)


def group_total(rows, bd):
    at = lax.broadcasted_iota(jnp.int32, (8, C), 0)
    stack = jnp.zeros((8, C), F32)
    for i, row in enumerate(rows):
        stack = jnp.where(at == i, row, stack)
    high = stack.astype(BF).astype(F32)
    rest = stack - high
    mid = rest.astype(BF).astype(F32)
    parts = jnp.concatenate([high, mid, rest - mid, jnp.zeros((8, C), F32)], axis=0)
    total = dot(parts.astype(BF), bd)
    total = total[0:8] + total[8:16] + total[16:24]
    return [total[i : i + 1] for i in range(len(rows))]


def chunk_at(i):
    return pl.multiple_of(i * CH, CH)


def passes(body, carry=None):
    carry = (0, 0) if carry is None else carry

    def step(i, held):
        return tuple(body(m, chunk_at(i), held[m]) for m in range(2))

    return lax.fori_loop(0, ROWS // CH, step, carry)


def zero_pair():
    return (jnp.zeros((8, C), F32), jnp.zeros((8, C), F32))


def col(v):
    return jnp.sum(v, axis=0, keepdims=True)


def write_shift(dst, m, at, value, forward):
    place = lax.broadcasted_iota(jnp.int32, (CH, C), 0) % 16
    before = jnp.where(place == 0, 0.0, pltpu.roll(value, 1, 0))
    after = jnp.where(place == 15, 0.0, pltpu.roll(value, CH - 1, 0))
    first, last = (before, after) if forward else (after, before)
    rows = pl.ds(pl.multiple_of(at + (GAP + m * STEP), 16), CH)
    dst[rows, 0:C] = first.astype(BF)
    dst[rows, C : 2 * C] = value.astype(BF)
    dst[rows, 2 * C : 3 * C] = last.astype(BF)


def norm_forward(load, n_ref, gain, shift, bd, emit, first=None, early=None, midway=None):
    def sums(m, at, held):
        return held + fold((first or load)(m, at))

    total = passes(sums, zero_pair())
    if early is not None:
        early()
    mean = group_total([col(t) for t in total], bd)
    mean = [v * (1.0 / COUNT) for v in mean]

    def squares(m, at, held):
        d = load(m, at) - mean[m]
        return held + fold(d * d)

    total = passes(squares, zero_pair())
    var = group_total([col(t) for t in total], bd)
    rstd = [lax.rsqrt(v * (1.0 / COUNT) + EPS) for v in var]
    if midway is not None:
        midway()

    def last(m, at, held):
        n = (load(m, at) - mean[m]) * rstd[m]
        n_ref[pl.ds(pl.multiple_of(at + m * ROWS, CH), CH), :] = n
        emit(m, at, n * gain + shift)
        return held

    passes(last)
    return rstd


def norm_back(d_ref, n_ref, gain, shift, rstd, bd, active, e_ref, e_at, emit):
    def rows(m, at):
        return pl.ds(pl.multiple_of(at + m * STEP, 16), CH)

    def first(m, at, held):
        d = d_ref[rows(m, at), :]
        n = n_ref[pl.ds(pl.multiple_of(at + m * ROWS, CH), CH), :]
        if active:
            u = n * gain + shift
            s = sigmoid(u)
            d = d * (s * (1.0 + u * (1.0 - s)))
            d_ref[rows(m, at), :] = d
        return (held[0] + fold(d), held[1] + fold(d * n))

    total = passes(first, (zero_pair(), zero_pair()))
    ones = [col(t[0]) for t in total]
    twos = [col(t[1]) for t in total]
    e_ref[e_at : e_at + 1, :] = twos[0] + twos[1]
    e_ref[e_at + 1 : e_at + 2, :] = ones[0] + ones[1]
    means = group_total([gain * v for v in ones + twos], bd)
    means = [v * (1.0 / COUNT) for v in means]

    def second(m, at, held):
        d = d_ref[rows(m, at), :]
        n = n_ref[pl.ds(pl.multiple_of(at + m * ROWS, CH), CH), :]
        return emit(m, at, rstd[m] * (d * gain - means[m] - n * means[2 + m]), held)

    return second


def unpack(low, high):
    lane = lax.broadcasted_iota(jnp.int32, low.shape, 1)
    first = jnp.where(lane < SL, low, pltpu.roll(high, SL, 1))
    second = jnp.where(lane < SL, pltpu.roll(low, SL, 1), high)
    return first, second


BLOCKS = ((0, STEP), (STEP, ROWS))


def conv_forward(a_ref, w_ref, h_ref, rows, add):
    for start, size in BLOCKS:
        total = None
        for row in rows:
            for c in range(3):
                at = 16 * row + start
                part = dot_nt(a_ref[at : at + size, C * c : C * c + C], w_ref[3 * row + c])
                total = part if total is None else total + part
        h_ref[start : start + size, :] = total + h_ref[start : start + size, :] if add else total


def conv_back(d_ref, w_ref, h_ref):
    for start, size in BLOCKS:
        total = None
        for row in range(3):
            at = 16 * (2 - row) + start
            part = dot(d_ref[at : at + size, :], w_ref[3 * row : 3 * row + 3].reshape(3 * C, C))
            total = part if total is None else total + part
        h_ref[start : start + size, :] = total


def conv_weight(a_ref, turned, dw_ref, row):
    for c in range(3):
        total = None
        for m in range(2):
            at = 16 * row + STEP * m
            part = dot(turned[m], a_ref[at : at + ROWS, C * c : C * c + C])
            total = part if total is None else total + part
        dw_ref[3 * row + c] = total.astype(BF)


class Group:
    def __init__(self, links):
        self.links, self.at, self.rows = links, links.used, 0
        links.used += 1

    def remote(self, src, dst, device):
        links, rows = self.links, rows_in(src)
        if links.sending + rows > links.idle.shape[0]:
            links.ended.append((links.senders, links.sending))
            links.senders, links.sending = links.senders + 1, 0
        links.sending += rows
        self.rows += rows
        pltpu.make_async_remote_copy(
            src_ref=src, dst_ref=dst, send_sem=links.send.at[links.senders], recv_sem=links.recv.at[self.at],
            device_id=device, device_id_type=MESH).start()

    def wait(self):
        self.links.wait_rows(self.links.recv.at[self.at], self.rows)


class LocalGroup:
    def __init__(self, links):
        self.links, self.at, self.rows = links, links.local, 0
        links.local += 1

    def copy(self, src, dst):
        self.rows += rows_in(src)
        pltpu.make_async_copy(src, dst, self.links.own.at[self.at]).start()

    def wait(self):
        self.links.wait_rows(self.links.own.at[self.at], self.rows)


def rows_in(ref):
    size = ref.dtype.itemsize
    for n in ref.shape:
        size *= n
    return size // 256


class Links:
    def __init__(self, send, recv, own, idle):
        self.send, self.recv, self.own, self.idle = send, recv, own, idle
        self.used, self.local, self.senders, self.sending = 0, 0, 0, 0
        self.ended = []

    def wait_rows(self, semaphore, rows):
        view = self.idle.at[0:rows]
        pltpu.make_async_copy(view, view, semaphore).wait()

    def group(self, copies=()):
        group = Group(self)
        for src, dst, device in copies:
            group.remote(src, dst, device)
        return group

    def here(self, src, dst):
        copy = pltpu.make_async_copy(src, dst, self.own.at[self.local])
        self.local += 1
        copy.start()
        return copy

    def here_all(self, copies=()):
        group = LocalGroup(self)
        for src, dst in copies:
            group.copy(src, dst)
        return group

    def close(self):
        for at, rows in self.ended + [(self.senders, self.sending)]:
            self.wait_rows(self.send.at[at], rows)


def block_sizes(n_dp):
    team = min(8, n_dp)
    return team, n_dp // team


def aligned(start, size):
    return pl.ds(pl.multiple_of(start, size), size)


def reduction_scratch(taps, order, kind, teams):
    rows = SL * taps
    part = (1, 1, rows, 128)
    shapes = dict(rc=(2, taps, SL, C), s0=(2, 2, rows, 128), pc=part, rt=(teams,) + part)
    shapes.update({name: part for name in ("c0", "c1", "c2", "p0", "p1", "t0", "t1")})
    size = dict(y=2, x=2)
    for k, axis in enumerate(order):
        size[axis] = 1
        shapes[f"r{k}"] = shapes[f"s{k + 1}"] = (size["y"], size["x"], rows, 128)
    buffers = {name: pltpu.VMEM(shape, BF) for name, shape in shapes.items()}
    if kind is Chain:
        buffers.update(cs=pltpu.SemaphoreType.DMA((4,)))
    return buffers


class Reduction:
    def __init__(self, at, links, grad, out, work, order):
        self.at, self.links, self.grad, self.out, self.w, self.order = at, links, grad, out, work, order
        self.taps = grad.shape[0]
        self.size = dict(y=2, x=2, z=at.team // 2)
        self.stage = -1
        self.whole = dict(y=True, x=True)
        self.group = links.group([
            (grad.at[:, aligned(SL * (2 * y + 1 - at.core), SL), :], self.w.rc.at[y], at.sibling) for y in range(2)])

    def view(self, ref, axis, index):
        return ref.at[pl.ds(index, 1)] if axis == "y" else ref.at[:, pl.ds(index, 1)]

    def send(self):
        axis = self.order[self.stage]
        other = 1 - self.at.place[axis]
        current, arriving = getattr(self.w, f"s{self.stage}"), getattr(self.w, f"r{self.stage}")
        self.group = self.links.group([(self.view(current, axis, other), arriving, self.at.peer({axis: other}))])

    def collect(self):
        at, w = self.at, self.w
        self.group.wait()
        if self.stage < 0:
            for y in range(2):
                for t in range(self.taps):
                    mine = self.grad[t, aligned(SL * (2 * y + at.core), SL), :].astype(F32)
                    total = (mine + w.rc[y, t].astype(F32)).astype(BF)
                    for half in range(2):
                        w.s0[y, half, SL * t : SL * t + SL, :] = total[:, 128 * half : 128 * half + 128]
            return
        axis = self.order[self.stage]
        mine = self.view(getattr(w, f"s{self.stage}"), axis, at.place[axis])[...].astype(F32)
        total = mine + getattr(w, f"r{self.stage}")[...].astype(F32)
        getattr(w, f"s{self.stage + 1}")[...] = total.astype(BF)

    def across_teams(self, piece):
        at, w = self.at, self.w
        own = self.links.here(piece, w.rt.at[at.lead])
        group = self.links.group([
            (piece, w.rt.at[at.lead], at.device((at.lead + s) % at.teams * at.team + at.rank))
            for s in range(1, at.teams)])
        own.wait()
        group.wait()
        total = w.rt[0].astype(F32)
        for s in range(1, at.teams):
            total = total + w.rt[s].astype(F32)
        w.pc[...] = total.astype(BF)
        return w.pc

    def share(self, source):
        source = self.across_teams(source) if self.at.teams > 1 else source
        target = self.out.at[:, pl.ds(self.at.place["x"], 1)]
        self.at.results.copy(source, target)
        self.group = self.links.group([(source, target, self.at.peer(dict(x=1 - self.at.place["x"])))])

    def advance(self):
        last = len(self.order) - 1
        if self.stage <= last:
            self.collect()
        if self.stage < last:
            self.stage += 1
            self.send()
        else:
            self.along_z(self.stage - last, getattr(self.w, f"s{last + 1}"))
            self.stage += 1

    def finish(self):
        self.group.wait()


class Chain(Reduction):
    def copy(self, sent, got, src, dst, z):
        w = self.w
        return pltpu.make_async_remote_copy(
            src_ref=src, dst_ref=dst, send_sem=w.cs.at[sent], recv_sem=w.cs.at[2 + got],
            device_id=self.at.peer(dict(z=z)), device_id_type=MESH)

    def along_z(self, step, total):
        w, count = self.w, self.size["z"]
        long, alone = count == 4, count == 1
        if step == 0:
            z = self.at.place["z"]
            self.end = (z == 0) | (z == count - 1)
            self.inner = jnp.logical_not(self.end)
            self.inward = self.copy(0, 0, total, w.c0, jnp.where(z < 2, 1, 2))
            self.swap = self.copy(0, 1, w.c1, w.c2, count - 1 - z)
            self.outward = self.copy(1, 0, w.pc, w.pc, jnp.where(z < 2, 0, 3))
            if long:
                pl.when(self.end)(self.inward.start)
            else:
                w.c1[...] = total[...]
        elif step == 1:
            if long:
                @pl.when(self.inner)
                def _():
                    self.inward.wait_recv()
                    w.c1[...] = (total[...].astype(F32) + w.c0[...].astype(F32)).astype(BF)
                    self.swap.start()
            elif not alone:
                self.swap.start()
        elif step == 2:
            def join():
                self.swap.wait_recv()
                w.pc[...] = (w.c1[...].astype(F32) + w.c2[...].astype(F32)).astype(BF)

            if long:
                @pl.when(self.inner)
                def _():
                    join()
                    self.outward.start()
            elif alone:
                w.pc[...] = w.c1[...]
            else:
                join()
        else:
            if long:
                @pl.when(self.end)
                def _():
                    self.outward.wait_recv()
                    self.inward.wait_send()

                @pl.when(self.inner)
                def _():
                    self.swap.wait_send()
                    self.outward.wait_send()
            elif not alone:
                self.swap.wait_send()
            self.share(w.pc)


class Pairs(Reduction):
    def along_z(self, step, total):
        w, z = self.w, self.at.place["z"]
        partners = [z + 1 - 2 * (z % 2), (z + 2) % 4]
        partners[self.size["z"] // 2 :] = [None] * (2 - self.size["z"] // 2)
        if step == 0:
            self.held = total
        elif partners[step - 1] is not None:
            self.group.wait()
            total = self.held[...].astype(F32) + getattr(w, f"p{step - 1}")[...].astype(F32)
            self.held = getattr(w, f"t{step - 1}")
            self.held[...] = total.astype(BF)
        if step == len(partners):
            self.share(self.held)
        elif partners[step] is not None:
            self.group = self.links.group([
                (self.held, getattr(w, f"p{step}"), self.at.peer(dict(z=partners[step])))])


YX, XY = ("y", "x"), ("x", "y")
ITEMS = {
    "ga0": (4, XY, Chain), "gb0": (3, YX, Chain), "gb1": (3, XY, Chain), "gb2": (3, XY, Chain),
    "gc0": (4, XY, Pairs), "gc1": (3, XY, Pairs), "gc2": (2, YX, Pairs)}
SENDS, GROUPS_OF_COPIES = 8, 72
GAINS = ("gain1", "shift1", "gain2", "shift2", "gain3", "shift3")


def mega(n_dp, names, *refs):
    r = SimpleNamespace(**dict(zip(names, refs)))
    team, teams = block_sizes(n_dp)
    dp, chan = lax.axis_index("dp"), lax.axis_index("chan")
    core, y, bit = chan % 2, chan // 2, dp % 2
    sibling, across, corner = (dp, 2 * y + 1 - core), (dp, 2 * (1 - y) + core), (dp, 2 * (1 - y) + 1 - core)
    beside, oblique = (dp + 1 - 2 * bit, chan), (dp + 1 - 2 * bit, 2 * (1 - y) + core)
    quads = (sibling, across, corner)
    rank, lead = dp % team, dp // team
    own_place = dict(y=y, x=bit, z=rank // 2)

    def peer(place):
        place = {**own_place, **place}
        return (lead * team + 2 * place["z"] + place["x"], 2 * place["y"] + core)

    at = SimpleNamespace(core=core, sibling=sibling, team=team, teams=teams, rank=rank, lead=lead, place=own_place,
                         peer=peer, device=lambda p: (p, chan))
    links = Links(r.send, r.recv, r.own, r.idle)
    at.results = links.here_all()

    def others():
        return [(lax.rem(dp + s, n_dp), chan) for s in range(1, n_dp)]

    barrier = pltpu.get_barrier_semaphore()
    for device in quads + (oblique,) + tuple(others()):
        pl.semaphore_signal(barrier, inc=1, device_id=device, device_id_type=MESH)
    load_x, load_ts, load_table = links.here(r.x, r.xl), links.here(r.ts, r.tss), links.here(r.table, r.tab)
    for i, name in enumerate(GAINS):
        pltpu.make_async_copy(getattr(r, name), r.pin.at[i], r.gains).start()
    load_we, load_dy, load_cnt = links.here(r.we, r.wel), links.here(r.dy, r.dyl), links.here(r.cnt, r.cns)
    mine = aligned(SL * chan, SL)
    fill = links.here_all([
        (r.w1, r.w1g.at[:, mine, :]), (r.w2, r.w2g.at[:, mine, :]), (r.we, r.weg.at[:, mine, :]),
        (r.wq, r.wqg.at[0:3, mine, :]), (r.wo, r.wqg.at[3:4, mine, :])])

    def pack(src, dst):
        for k in range(CHAN):
            for half in range(2):
                rows = slice(128 * half, 128 * half + 128)
                both = jnp.concatenate([src[2 * k, rows, :].astype(F32), src[2 * k + 1, rows, :].astype(F32)], axis=1)
                dst[k, rows, :] = both.astype(BF)

    load_x.wait()
    pack(r.xl, r.xp)
    pltpu.make_async_copy(r.pin, r.pin, r.gains).wait()
    r.par[...] = jnp.zeros((8, 128), F32)
    for i in range(len(GAINS)):
        r.par[i : i + 1, 0:SL] = r.pin[i].astype(F32)
    pl.semaphore_wait(barrier, CHAN + n_dp - 1)

    part = 32 * bit
    far = SL * (2 * (1 - y) + core)

    class Share:
        def __init__(self, w, g, half):
            self.w, self.g, self.half = w, g, half
            self.from_sibling = links.group()
            rows = (part, 32) if half else (0, SL)
            self.over = links.group([
                (w.at[:, aligned(*rows), :], g.at[:, aligned(SL * chan + rows[0], rows[1]), :], across)])

        def own(self):
            self.from_sibling.remote(self.w, self.g.at[:, mine, :], sibling)

        def relay(self):
            self.over.wait()
            if self.half:
                piece = self.g.at[:, aligned(far + part, 32), :]
                self.around = links.group([(piece, piece, beside)])
            else:
                piece = self.g.at[:, aligned(far, SL), :]
            self.from_sibling.remote(piece, piece, sibling)

        def relay_again(self):
            self.around.wait()
            piece = self.g.at[:, aligned(far + 32 - part, 32), :]
            self.from_sibling.remote(piece, piece, sibling)

        def landed(self):
            self.from_sibling.wait()

    def rows3(ref, row):
        return ref.at[3 * row : 3 * row + 3]

    one = [Share(rows3(r.w1, row), rows3(r.w1g, row), True) for row in range(3)]
    for share in one:
        share.own()

    load_ts.wait()
    row8 = lax.broadcasted_iota(jnp.int32, (8, 128), 0)
    times = jnp.zeros((8, 128), F32)
    for i in range(8):
        times = jnp.where(row8 == i, r.tss[i].astype(F32), times)
    r.tl[...] = times
    r.ta[dp] = times
    steps = r.table.shape[0]
    load_table.wait()

    def embeddings(times):
        count = times.shape[0]
        wide = jnp.broadcast_to(times[:, 0:1], (count, steps))
        hot = jnp.where(wide == lax.broadcasted_iota(jnp.int32, (count, steps), 1).astype(F32), 1.0, 0.0)
        temb = dot(hot.astype(BF), r.tab[...])
        s = sigmoid(temb)
        return temb, s, (temb * s).astype(BF)

    _, _, tsil = embeddings(jnp.concatenate([times, times], axis=0))
    load_we.wait()
    r.el[...] = jnp.zeros((8, 128), F32)
    r.el[:, 0:SL] = dot_nt(tsil, r.wel[0])[0:8]
    r.eg[chan] = r.el[...]
    moves_x = links.group(
        [(r.xp.at[d[1]], r.xg.at[chan], d) for d in quads] + [(r.par, r.pg.at[chan], d) for d in quads])
    moves_emb = links.group([(r.el, r.eg.at[chan], d) for d in quads])
    r.xg[chan] = r.xp[chan]
    r.pg[chan] = r.par[...]
    at_row = lax.broadcasted_iota(jnp.int32, (C, C), 0) // (C // GROUPS)
    at_col = lax.broadcasted_iota(jnp.int32, (C, C), 1) // (C // GROUPS)
    r.bd[...] = jnp.where(at_row == at_col, 1.0, 0.0).astype(BF)
    for ref in (r.a1, r.a2, r.dd):
        for gap in range(3):
            ref[gap * STEP : gap * STEP + GAP, :] = jnp.zeros((GAP, 3 * C), BF)
    load_dy.wait()
    pack(r.dyl, r.dyp)
    r.dyg[chan] = r.dyp[chan]
    two = []
    for row in range(3):
        one[row].relay()
        two.append(Share(rows3(r.w2, row), rows3(r.w2g, row), row < 2))
        two[row].own()
    one[0].relay_again()
    out = [Share(r.wq, r.wqg.at[0:3], False), Share(r.wo, r.wqg.at[3:4], False)]
    for share in out:
        share.own()
    one[1].relay_again()
    moves_dy = links.group([(r.dyp.at[d[1]], r.dyg.at[chan], d) for d in quads])
    one[2].relay_again()
    mix = Share(r.we, r.weg, False)
    mix.own()
    moves_late = links.group([(r.tl, r.ta.at[dp], d) for d in others()])

    bd = r.bd[...]
    moves_x.wait()
    for b in range(2):
        first, _ = unpack(r.pg[2 * b], r.pg[2 * b + 1])
        r.pa[:, 128 * b : 128 * b + 128] = first
    par = r.pa[...]
    gain1, shift1, gain2, shift2, gain3, shift3 = [par[i : i + 1] for i in range(6)]

    def spread_out(src, at, dst, scale=None):
        for b in range(2):
            pair = unpack(src[2 * b, pl.ds(at, CH), :].astype(F32), src[2 * b + 1, pl.ds(at, CH), :].astype(F32))
            for m in range(2):
                value = pair[m] if scale is None else pair[m] * scale[m]
                dst[pl.ds(pl.multiple_of(at + m * ROWS, CH), CH), 128 * b : 128 * b + 128] = value.astype(dst.dtype)

    def open_x(i, held):
        spread_out(r.xg, chunk_at(i), r.xf)
        return held

    lax.fori_loop(0, ROWS // CH, open_x, 0)

    def rows_of(m, at):
        return pl.ds(pl.multiple_of(at + m * ROWS, CH), CH)

    def rows_gap(m, at):
        return pl.ds(pl.multiple_of(at + m * STEP, 16), CH)

    def to_shift(dst):
        def emit(m, at, u):
            write_shift(dst, m, at, u * sigmoid(u), True)
        return emit

    rstd1 = norm_forward(lambda m, at: r.xf[rows_of(m, at), :], r.n1, gain1, shift1, bd, to_shift(r.a1),
                         early=two[0].relay, midway=two[1].relay)
    fill.wait()

    for share in one:
        share.landed()
    conv_forward(r.a1, r.w1g, r.h, (0, 1, 2), False)
    moves_emb.wait()
    for b in range(2):
        first, _ = unpack(r.eg[2 * b], r.eg[2 * b + 1])
        r.emb[:, 128 * b : 128 * b + 128] = first
    emb = [r.emb[pl.ds(2 * chan + m, 1), :] for m in range(2)]
    rstd2 = norm_forward(lambda m, at: r.h[rows_gap(m, at), :] + emb[m], r.n2, gain2, shift2, bd, to_shift(r.a2),
                         midway=two[2].relay)
    two[0].relay_again()
    two[1].relay_again()
    two[0].landed()
    two[2].landed()
    conv_forward(r.a2, r.w2g, r.h, (0, 2), False)
    for share in out:
        share.relay()
    two[1].landed()
    conv_forward(r.a2, r.w2g, r.h, (1,), True)

    def load_resid(m, at):
        return r.xf[rows_of(m, at), :]

    def make_resid(m, at):
        value = r.xf[rows_of(m, at), :] + r.h[rows_gap(m, at), :]
        r.xf[rows_of(m, at), :] = value
        return value

    def to_a3(m, at, u):
        r.a3[rows_of(m, at), :] = u.astype(BF)

    rstd3 = norm_forward(load_resid, r.n3, gain3, shift3, bd, to_a3, first=make_resid)
    out[0].landed()
    for j, ref in enumerate((r.q, r.k, r.v)):
        ref[...] = dot_nt(r.a3[...], r.wqg[j]).astype(BF)
    load_cnt.wait()
    count = r.cns[0]
    live = [jnp.where(2 * chan + m < count, 1.0, 0.0).astype(F32) for m in range(2)]
    scale = C ** (-0.5)
    half = [slice(0, ROWS), slice(ROWS, 2 * ROWS)]
    for m in range(2):
        s = dot_nt(r.q[half[m], :], r.k[half[m], :]) * scale
        p = jnp.exp(s - jnp.max(s, axis=1, keepdims=True))
        p = p * (1.0 / jnp.sum(p, axis=1, keepdims=True))
        r.p[half[m], :] = p
        r.pb[half[m], :] = p.astype(BF)
        r.o[half[m], :] = dot(p.astype(BF), r.v[half[m], :]).astype(BF)

    moves_dy.wait()
    out[1].landed()

    def open_dy(i, held):
        spread_out(r.dyg, chunk_at(i), r.g, live)
        return held

    lax.fori_loop(0, ROWS // CH, open_dy, 0)
    for m in range(2):
        r.turn[m] = r.g[half[m], :].T
    r.dqo[3] = (dot(r.turn[0], r.o[half[0], :]) + dot(r.turn[1], r.o[half[1], :])).astype(BF)
    r.do[...] = dot(r.g[...], r.wqg[3]).astype(BF)
    for m in range(2):
        dp_m = dot_nt(r.do[half[m], :], r.v[half[m], :])
        p = r.p[half[m], :]
        ds = (p * (dp_m - jnp.sum(p * dp_m, axis=1, keepdims=True)) * scale).astype(BF)
        r.dv[half[m], :] = dot(r.pb[half[m], :].T, r.do[half[m], :]).astype(BF)
        r.dq[half[m], :] = dot(ds, r.k[half[m], :]).astype(BF)
        r.dk[half[m], :] = dot(ds.T, r.q[half[m], :]).astype(BF)
    for j, ref in enumerate((r.dq, r.dk, r.dv)):
        parts = [dot(ref[half[m], :].T, r.a3[half[m], :]) for m in range(2)]
        r.dqo[j] = (parts[0] + parts[1]).astype(BF)

    items = []

    def reduce(letter, grad):
        start = 0
        for name, (taps, order, kind) in ITEMS.items():
            if name[1] == letter:
                work = SimpleNamespace(**{k[4:]: getattr(r, k) for k in names if k.startswith(name + "_")})
                items.append(kind(at, links, grad.at[start : start + taps], getattr(r, name), work, order))
                start += taps

    def go(*which):
        for i in which:
            items[i].advance()

    reduce("a", r.dqo)
    for m in range(2):
        total = None
        for j, ref in enumerate((r.dq, r.dk, r.dv)):
            part_j = dot(ref[half[m], :], r.wqg[j])
            total = part_j if total is None else total + part_j
        r.h[m * STEP : m * STEP + ROWS, :] = total

    def to_dres(m, at, dv, held):
        value = r.g[rows_of(m, at), :].astype(F32) + dv
        r.dres[rows_of(m, at), :] = value
        write_shift(r.dd, m, at, value, False)
        return held

    passes(norm_back(r.h, r.n3, gain3, shift3, rstd3, bd, False, r.e, 4, to_dres))
    go(0)

    def turn():
        for m in range(2):
            r.turn[m] = r.dd[GAP + STEP * m : GAP + STEP * m + ROWS, C : 2 * C].T

    turn()
    for row in range(3):
        conv_weight(r.a2, r.turn, r.dw2, row)
    reduce("b", r.dw2)
    conv_back(r.dd, r.w2g, r.h)
    go(1, 2, 3)
    mix.relay()

    def to_dh1(m, at, dv, held):
        write_shift(r.dd, m, at, dv, False)
        return held + fold(dv)

    demb = passes(norm_back(r.h, r.n2, gain2, shift2, rstd2, bd, True, r.e, 2, to_dh1), zero_pair())
    for m in range(2):
        r.dm[chan, m : m + 1, :] = col(demb[m]).astype(BF).astype(F32)
    moves_dm = links.group([(r.dm.at[chan], r.dm.at[chan], d) for d in quads])
    turn()
    for row in range(3):
        conv_weight(r.a1, r.turn, r.dw1, row)
    reduce("c", r.dw1)
    r.big[...] = dot_nt(r.o[...], r.wqg[3])

    def pack_out(at, pair, dst):
        for b in range(2):
            even, odd = unpack(*(v[:, 128 * b : 128 * b + 128] for v in pair))
            dst[2 * b, pl.ds(at, CH), :] = even.astype(BF)
            dst[2 * b + 1, pl.ds(at, CH), :] = odd.astype(BF)

    def to_y(i, held):
        at = chunk_at(i)
        pack_out(at, [(load_resid(m, at) + r.big[rows_of(m, at), :]) * live[m] for m in range(2)], r.yp)
        return held

    lax.fori_loop(0, ROWS // CH, to_y, 0)

    def data_one():
        conv_back(r.dd, r.w1g, r.h)

    def norm_one():
        back1 = norm_back(r.h, r.n1, gain1, shift1, rstd1, bd, True, r.e, 0,
                          lambda m, at, dv, held: r.dres[rows_of(m, at), :] + dv)

        def to_maps(i, held):
            at = chunk_at(i)
            pack_out(at, [back1(m, at, 0) for m in range(2)], r.mp)
            return held

        lax.fori_loop(0, ROWS // CH, to_maps, 0)
        moves_dm.wait()
        for j in range(CHAN):
            r.dl[2 * j : 2 * j + 2, :] = r.dm[j, 0:2, :]
        r.ra[dp] = r.dl[...]
        for d in others():
            moves_late.remote(r.dl, r.ra.at[dp], d)
        for b in range(2):
            block = r.e[:, 128 * b : 128 * b + 128]
            r.es[2 * b] = block
            r.es[2 * b + 1] = pltpu.roll(block, SL, 1)
        r.er[chan] = r.es[chan]
        for d in quads:
            moves_e.remote(r.es.at[d[1]], r.er.at[chan], d)

    def send_maps():
        for src, dst in ((r.yp, r.yo), (r.mp, r.mo)):
            at.results.copy(src.at[chan], dst.at[chan])
            for d in quads:
                moves_out.remote(src.at[d[1]], dst.at[chan], d)

    def send_gains():
        moves_e.wait()
        r.et[...] = r.er[0] + r.er[1] + r.er[2] + r.er[3]
        at.results.copy(r.et, r.ext.at[dp])
        for d in others():
            moves_out.remote(r.et, r.ext.at[dp], d)

    def embedding():
        mix.landed()
        moves_late.wait()
        maps = 8 * n_dp
        temb, s, tsil = embeddings(r.ta[...].reshape(maps, 128))
        rows = r.ra[...].reshape(maps, C)
        r.rt[...] = rows.T
        r.dew[...] = dot(r.rt[mine, :].astype(BF), tsil)
        dtemb = dot(rows.astype(BF), r.weg[0]) * (s * (1.0 + temb * (1.0 - s)))
        high = dtemb.astype(BF)
        r.bw[0:maps, :] = high
        r.bw[maps:, :] = (dtemb - high.astype(F32)).astype(BF)
        for src, dst in ((r.dew, r.de), (r.bw, r.both), (r.ta, r.tall)):
            at.results.copy(src, dst)

    moves_e, moves_out = links.group(), links.group()
    go(0, 4, 5, 6)
    data_one()
    go(2, 1)
    norm_one()
    go(3, 0, 6, 4, 2, 3, 0, 5)
    send_maps()
    go(1)
    send_gains()
    go(6, 2, 4, 3, 5, 0, 1, 6)
    embedding()
    go(2, 4, 3, 5, 0, 1, 2, 6, 3, 1, 4, 5)
    for item in items:
        item.finish()
    at.results.wait()
    moves_out.wait()
    links.close()


def finish(n_dp, names, *refs):
    r = SimpleNamespace(**dict(zip(names, refs)))
    maps = 8 * n_dp
    steps = r.dt.shape[0]
    links = Links(None, None, r.own, None)
    items = list(ITEMS)
    load = {name: links.here(getattr(r, name), getattr(r, name + "_v"))
            for name in ["tall", "both", "yo", "mo", "de"] + items + ["ext"]}
    stores = []

    def out(src, dst):
        stores.append(links.here(src, dst))

    load["tall"].wait()
    load["both"].wait()
    lanes = r.tall_v[...].reshape(maps, 128).T[0:1, :]
    lanes = jnp.concatenate([lanes, lanes], axis=1)
    for start in range(0, steps, 256):
        size = min(256, steps - start)
        ids = lax.broadcasted_iota(jnp.int32, (size, 2 * maps), 0).astype(F32) + float(start)
        hot = jnp.where(ids == lanes, 1.0, 0.0).astype(BF)
        r.dt_v[start : start + size, :] = dot(hot, r.both_v[...])
        out(r.dt_v.at[start : start + size], r.dt.at[start : start + size])

    def unpack_maps(name, dst, dst_v):
        load[name].wait()
        src = getattr(r, name + "_v")
        for j in range(CHAN):
            block = src[j].astype(F32)
            dst_v[2 * j] = block[:, 0:SL].astype(BF)
            dst_v[2 * j + 1] = pltpu.roll(block, SL, 1)[:, 0:SL].astype(BF)
        out(dst_v, dst)

    def whole(name, dst_v, base, taps):
        src = getattr(r, name + "_v")
        for i, t in enumerate(taps):
            for half in range(2):
                dst_v[base + i, :, 128 * half : 128 * half + 128] = src[0, half, SL * t : SL * t + SL, :].astype(F32)

    unpack_maps("yo", r.y, r.y_v)
    unpack_maps("mo", r.dm, r.dm_v)
    load["de"].wait()
    out(r.de_v, r.de_out)
    load["ga0"].wait()
    whole("ga0", r.dq_v, 0, range(3))
    out(r.dq_v, r.dq)
    whole("ga0", r.do_v, 0, [3])
    out(r.do_v, r.do)
    for letter, dst_v, dst in (("b", r.d2_v, r.d2), ("c", r.d1_v, r.d1)):
        start = 0
        for name, (taps, _, _) in ITEMS.items():
            if name[1] == letter:
                load[name].wait()
                whole(name, dst_v, start, range(taps))
                out(dst_v.at[start : start + taps], dst.at[start : start + taps])
                start += taps
    load["ext"].wait()
    total = r.ext_v[0]
    for i in range(1, n_dp):
        total = total + r.ext_v[i]
    for i in range(6):
        r.gains_v[i] = total[i : i + 1, 0:SL]
        out(r.gains_v.at[i], getattr(r, f"e{i}"))
    for copy in stores:
        copy.wait()


def per_device(x_maps, timesteps, counts, emb_table, w_first, w_second, w_embed, w_qkv, w_out, gain_one, shift_one,
               gain_two, shift_two, gain_three, shift_three, cotangent, *, n_dp):
    team, teams = block_sizes(n_dp)
    slots, side, _, _ = x_maps.shape
    emb = w_embed.shape[0]
    steps = emb_table.shape[0]
    inputs = dict(
        x=x_maps.reshape(slots, side * side, SL), dy=cotangent.reshape(slots, side * side, SL),
        ts=timesteps, cnt=counts, table=emb_table,
        w1=jnp.swapaxes(w_first, 2, 3).reshape(9, SL, C), w2=jnp.swapaxes(w_second, 2, 3).reshape(9, SL, C),
        we=w_embed.T[None], wq=jnp.transpose(w_qkv, (1, 2, 0)), wo=w_out.T[None])
    gains = (gain_one, shift_one, gain_two, shift_two, gain_three, shift_three)
    inputs.update({name: v.reshape(1, SL) for name, v in zip(GAINS, gains)})
    anywhere = pl.BlockSpec(memory_space=pl.ANY)

    def of(shape, dtype):
        return jax.ShapeDtypeStruct(shape, dtype)

    maps = 8 * n_dp
    middle = dict(
        yo=of((CHAN, ROWS, 128), BF), mo=of((CHAN, ROWS, 128), BF), tall=of((n_dp, 8, 128), F32),
        ext=of((n_dp, 8, 128), F32), both=of((2 * maps, emb), BF), de=of((SL, emb), F32))
    middle.update({name: of((1, 2, SL * item[0], 128), BF) for name, item in ITEMS.items()})
    v = pltpu.VMEM
    maps2 = 2 * ROWS
    scratch = dict(
        xl=v((slots, ROWS, SL), BF), dyl=v((slots, ROWS, SL), BF), pin=v((len(GAINS), 1, SL), BF),
        tss=pltpu.SMEM((slots,), jnp.int32), cns=pltpu.SMEM((1,), jnp.int32), tab=v((steps, emb), BF),
        xp=v((CHAN, ROWS, 128), BF), dyp=v((CHAN, ROWS, 128), BF),
        xg=v((CHAN, ROWS, 128), BF), dyg=v((CHAN, ROWS, 128), BF),
        yp=v((CHAN, ROWS, 128), BF), mp=v((CHAN, ROWS, 128), BF),
        w1g=v((9, C, C), BF), w2g=v((9, C, C), BF), weg=v((1, C, emb), BF), wqg=v((4, C, C), BF),
        bd=v((C, C), BF), tl=v((8, 128), F32), ta=v((n_dp, 8, 128), F32), par=v((8, 128), F32),
        pg=v((CHAN, 8, 128), F32), pa=v((8, C), F32), emb=v((8, C), F32),
        wel=v((1, SL, emb), BF), el=v((8, 128), F32), eg=v((CHAN, 8, 128), F32),
        a1=v((TALL + 2 * GAP, 3 * C), BF), a2=v((TALL + 2 * GAP, 3 * C), BF), dd=v((TALL + 2 * GAP, 3 * C), BF),
        h=v((TALL, C), F32), xf=v((maps2, C), F32), n1=v((maps2, C), F32), n2=v((maps2, C), F32),
        n3=v((maps2, C), F32), dres=v((maps2, C), F32), big=v((maps2, C), F32), p=v((maps2, C), F32),
        e=v((8, C), F32), es=v((CHAN, 8, 128), F32), er=v((CHAN, 8, 128), F32), et=v((8, 128), F32),
        dm=v((CHAN, 8, C), F32), dl=v((8, C), F32), ra=v((n_dp, 8, C), F32), rt=v((C, maps), F32),
        dew=v((SL, emb), F32), bw=v((2 * maps, emb), BF), turn=v((2, ROWS, C), BF),
        dw1=v((9, C, C), BF), dw2=v((9, C, C), BF), dqo=v((4, C, C), BF))
    for name in ("a3", "q", "k", "v", "pb", "o", "g", "do", "dq", "dk", "dv"):
        scratch[name] = v((maps2, C), BF)
    for name, (taps, order, kind) in ITEMS.items():
        buffers = reduction_scratch(taps, order, kind, teams)
        scratch.update({name + "_" + k: b for k, b in buffers.items()})
    several = len(ITEMS) if teams > 1 else 0
    scratch.update(
        idle=v((4096, 128), BF), send=pltpu.SemaphoreType.DMA((SENDS + several,)),
        recv=pltpu.SemaphoreType.DMA((GROUPS_OF_COPIES + several,)), own=pltpu.SemaphoreType.DMA((9 + several,)),
        gains=pltpu.SemaphoreType.DMA(()))
    got = pl.pallas_call(
        functools.partial(mega, n_dp, list(inputs) + list(middle) + list(scratch)),
        out_shape=tuple(middle.values()),
        in_specs=[anywhere] * len(inputs),
        out_specs=(anywhere,) * len(middle),
        scratch_shapes=list(scratch.values()),
        compiler_params=pltpu.CompilerParams(collective_id=0, has_side_effects=True, vmem_limit_bytes=60 << 20),
        name="blocks",
    )(*inputs.values())
    results = dict(
        y=of((slots, ROWS, SL), BF), dm=of((slots, ROWS, SL), BF), dt=of((steps, emb), F32), d1=of((9, SL, C), F32),
        d2=of((9, SL, C), F32), de_out=of((SL, emb), F32), dq=of((3, SL, C), F32), do=of((1, SL, C), F32))
    results.update({f"e{i}": of((1, SL), F32) for i in range(6)})
    scratch = {name + "_v": v(o.shape, o.dtype) for name, o in middle.items()}
    scratch.update({name + "_v": v(o.shape, o.dtype) for name, o in results.items() if name[0] != "e"})
    scratch.update(gains_v=v((6, 1, SL), F32), own=pltpu.SemaphoreType.DMA((48,)))
    got = pl.pallas_call(
        functools.partial(finish, n_dp, list(middle) + list(results) + list(scratch)),
        out_shape=tuple(results.values()),
        in_specs=[anywhere] * len(middle),
        out_specs=(anywhere,) * len(results),
        scratch_shapes=list(scratch.values()),
        compiler_params=pltpu.CompilerParams(vmem_limit_bytes=60 << 20),
        name="finish",
    )(*got)
    got = dict(zip(results, got))
    return (
        got["y"].reshape(x_maps.shape), got["dm"].reshape(x_maps.shape), got["dt"],
        jnp.swapaxes(got["d1"].reshape(3, 3, SL, C), 2, 3), jnp.swapaxes(got["d2"].reshape(3, 3, SL, C), 2, 3),
        got["de_out"].T, jnp.transpose(got["dq"], (2, 0, 1)), got["do"].reshape(SL, C).T,
    ) + tuple(got[f"e{i}"].reshape(SL) for i in range(6))


def solution(mesh):
    weights = (P(None, None, None, "chan"), P(None, None, None, "chan"), P(None, "chan"), P(None, None, "chan"),
               P(None, "chan")) + (P("chan"),) * 6
    maps = P("dp", None, None, "chan")
    return jax.shard_map(
        functools.partial(per_device, n_dp=mesh.shape["dp"]), mesh=mesh,
        in_specs=(maps, P("dp"), P("dp"), P()) + weights + (maps,),
        out_specs=(maps, maps, P()) + weights, check_vma=False)
```

```python
import functools
from types import SimpleNamespace

import jax
import jax.numpy as jnp
from jax import lax
from jax.experimental import pallas as pl
from jax.experimental.pallas import tpu as pltpu
from jax.sharding import PartitionSpec as P

F32 = jnp.float32
BF = jnp.bfloat16
MESH = pl.DeviceIdType.MESH
EPS = 1e-06
GROUPS = 32
CHAN = 4
ROWS = 256
C = 256
SL = C // CHAN
GAP = 16
STEP = ROWS + GAP
TALL = 2 * ROWS + GAP
CH = 128
COUNT = ROWS * (C // GROUPS)


def dot(a, b):
    return jnp.dot(a, b, preferred_element_type=F32)


def dot_nt(a, b):
    return lax.dot_general(a, b, (((1,), (1,)), ((), ())), preferred_element_type=F32)


def sigmoid(u):
    return 0.5 * jnp.tanh(0.5 * u) + 0.5


def fold(v):
    return v.reshape(v.shape[0] // 8, 8, v.shape[1]).sum(axis=0)


def group_total(rows, bd):
    at = lax.broadcasted_iota(jnp.int32, (8, C), 0)
    stack = jnp.zeros((8, C), F32)
    for i, row in enumerate(rows):
        stack = jnp.where(at == i, row, stack)
    high = stack.astype(BF).astype(F32)
    rest = stack - high
    mid = rest.astype(BF).astype(F32)
    parts = jnp.concatenate([high, mid, rest - mid, jnp.zeros((8, C), F32)], axis=0)
    total = dot(parts.astype(BF), bd)
    total = total[0:8] + total[8:16] + total[16:24]
    return [total[i : i + 1] for i in range(len(rows))]


def chunk_at(i):
    return pl.multiple_of(i * CH, CH)


def passes(body, carry=None):
    carry = (0, 0) if carry is None else carry

    def step(i, held):
        return tuple(body(m, chunk_at(i), held[m]) for m in range(2))

    return lax.fori_loop(0, ROWS // CH, step, carry)


def zero_pair():
    return (jnp.zeros((8, C), F32), jnp.zeros((8, C), F32))


def col(v):
    return jnp.sum(v, axis=0, keepdims=True)


def write_shift(dst, m, at, value, forward):
    place = lax.broadcasted_iota(jnp.int32, (CH, C), 0) % 16
    before = jnp.where(place == 0, 0.0, pltpu.roll(value, 1, 0))
    after = jnp.where(place == 15, 0.0, pltpu.roll(value, CH - 1, 0))
    first, last = (before, after) if forward else (after, before)
    rows = pl.ds(pl.multiple_of(at + (GAP + m * STEP), 16), CH)
    dst[rows, 0:C] = first.astype(BF)
    dst[rows, C : 2 * C] = value.astype(BF)
    dst[rows, 2 * C : 3 * C] = last.astype(BF)


def norm_forward(load, n_ref, gain, shift, bd, emit, first=None, early=None, midway=None):
    def sums(m, at, held):
        return held + fold((first or load)(m, at))

    total = passes(sums, zero_pair())
    if early is not None:
        early()
    mean = group_total([col(t) for t in total], bd)
    mean = [v * (1.0 / COUNT) for v in mean]

    def squares(m, at, held):
        d = load(m, at) - mean[m]
        return held + fold(d * d)

    total = passes(squares, zero_pair())
    var = group_total([col(t) for t in total], bd)
    rstd = [lax.rsqrt(v * (1.0 / COUNT) + EPS) for v in var]
    if midway is not None:
        midway()

    def last(m, at, held):
        n = (load(m, at) - mean[m]) * rstd[m]
        n_ref[pl.ds(pl.multiple_of(at + m * ROWS, CH), CH), :] = n
        emit(m, at, n * gain + shift)
        return held

    passes(last)
    return rstd


def norm_back(d_ref, n_ref, gain, shift, rstd, bd, active, e_ref, e_at, emit):
    def rows(m, at):
        return pl.ds(pl.multiple_of(at + m * STEP, 16), CH)

    def first(m, at, held):
        d = d_ref[rows(m, at), :]
        n = n_ref[pl.ds(pl.multiple_of(at + m * ROWS, CH), CH), :]
        if active:
            u = n * gain + shift
            s = sigmoid(u)
            d = d * (s * (1.0 + u * (1.0 - s)))
            d_ref[rows(m, at), :] = d
        return (held[0] + fold(d), held[1] + fold(d * n))

    total = passes(first, (zero_pair(), zero_pair()))
    ones = [col(t[0]) for t in total]
    twos = [col(t[1]) for t in total]
    e_ref[e_at : e_at + 1, :] = twos[0] + twos[1]
    e_ref[e_at + 1 : e_at + 2, :] = ones[0] + ones[1]
    means = group_total([gain * v for v in ones + twos], bd)
    means = [v * (1.0 / COUNT) for v in means]

    def second(m, at, held):
        d = d_ref[rows(m, at), :]
        n = n_ref[pl.ds(pl.multiple_of(at + m * ROWS, CH), CH), :]
        return emit(m, at, rstd[m] * (d * gain - means[m] - n * means[2 + m]), held)

    return second


def unpack(low, high):
    lane = lax.broadcasted_iota(jnp.int32, low.shape, 1)
    first = jnp.where(lane < SL, low, pltpu.roll(high, SL, 1))
    second = jnp.where(lane < SL, pltpu.roll(low, SL, 1), high)
    return first, second


BLOCKS = ((0, STEP), (STEP, ROWS))


def conv_forward(a_ref, w_ref, h_ref, rows, add):
    for start, size in BLOCKS:
        total = None
        for row in rows:
            for c in range(3):
                at = 16 * row + start
                part = dot_nt(a_ref[at : at + size, C * c : C * c + C], w_ref[3 * row + c])
                total = part if total is None else total + part
        h_ref[start : start + size, :] = total + h_ref[start : start + size, :] if add else total


def conv_back(d_ref, w_ref, h_ref):
    for start, size in BLOCKS:
        total = None
        for row in range(3):
            at = 16 * (2 - row) + start
            part = dot(d_ref[at : at + size, :], w_ref[3 * row : 3 * row + 3].reshape(3 * C, C))
            total = part if total is None else total + part
        h_ref[start : start + size, :] = total


def conv_weight(a_ref, turned, dw_ref, row):
    for c in range(3):
        total = None
        for m in range(2):
            at = 16 * row + STEP * m
            part = dot(turned[m], a_ref[at : at + ROWS, C * c : C * c + C])
            total = part if total is None else total + part
        dw_ref[3 * row + c] = total.astype(BF)


class Group:
    def __init__(self, links):
        self.links, self.at, self.rows = links, links.used, 0
        links.used += 1

    def remote(self, src, dst, device):
        links, rows = self.links, rows_in(src)
        if links.sending + rows > links.idle.shape[0]:
            links.ended.append((links.senders, links.sending))
            links.senders, links.sending = links.senders + 1, 0
        links.sending += rows
        self.rows += rows
        pltpu.make_async_remote_copy(
            src_ref=src, dst_ref=dst, send_sem=links.send.at[links.senders], recv_sem=links.recv.at[self.at],
            device_id=device, device_id_type=MESH).start()

    def wait(self):
        self.links.wait_rows(self.links.recv.at[self.at], self.rows)


class LocalGroup:
    def __init__(self, links):
        self.links, self.at, self.rows = links, links.local, 0
        links.local += 1

    def copy(self, src, dst):
        self.rows += rows_in(src)
        pltpu.make_async_copy(src, dst, self.links.own.at[self.at]).start()

    def wait(self):
        self.links.wait_rows(self.links.own.at[self.at], self.rows)


def rows_in(ref):
    size = ref.dtype.itemsize
    for n in ref.shape:
        size *= n
    return size // 256


class Links:
    def __init__(self, send, recv, own, idle):
        self.send, self.recv, self.own, self.idle = send, recv, own, idle
        self.used, self.local, self.senders, self.sending = 0, 0, 0, 0
        self.ended = []

    def wait_rows(self, semaphore, rows):
        view = self.idle.at[0:rows]
        pltpu.make_async_copy(view, view, semaphore).wait()

    def group(self, copies=()):
        group = Group(self)
        for src, dst, device in copies:
            group.remote(src, dst, device)
        return group

    def here(self, src, dst):
        copy = pltpu.make_async_copy(src, dst, self.own.at[self.local])
        self.local += 1
        copy.start()
        return copy

    def here_all(self, copies=()):
        group = LocalGroup(self)
        for src, dst in copies:
            group.copy(src, dst)
        return group

    def close(self):
        for at, rows in self.ended + [(self.senders, self.sending)]:
            self.wait_rows(self.send.at[at], rows)


def block_sizes(n_dp):
    team = min(8, n_dp)
    return team, n_dp // team


def aligned(start, size):
    return pl.ds(pl.multiple_of(start, size), size)


def reduction_scratch(taps, order, kind, teams):
    rows = SL * taps
    part = (1, 1, rows, 128)
    shapes = dict(rc=(2, taps, SL, C), s0=(2, 2, rows, 128), pc=part, rt=(teams,) + part)
    shapes.update({name: part for name in ("c0", "c1", "c2", "p0", "p1", "t0", "t1")})
    size = dict(y=2, x=2)
    for k, axis in enumerate(order):
        size[axis] = 1
        shapes[f"r{k}"] = shapes[f"s{k + 1}"] = (size["y"], size["x"], rows, 128)
    buffers = {name: pltpu.VMEM(shape, BF) for name, shape in shapes.items()}
    if kind is Chain:
        buffers.update(cs=pltpu.SemaphoreType.DMA((4,)))
    return buffers


class Reduction:
    def __init__(self, at, links, grad, out, work, order):
        self.at, self.links, self.grad, self.out, self.w, self.order = at, links, grad, out, work, order
        self.taps = grad.shape[0]
        self.size = dict(y=2, x=2, z=at.team // 2)
        self.stage = -1
        self.whole = dict(y=True, x=True)
        self.group = links.group([
            (grad.at[:, aligned(SL * (2 * y + 1 - at.core), SL), :], self.w.rc.at[y], at.sibling) for y in range(2)])

    def view(self, ref, axis, index):
        return ref.at[pl.ds(index, 1)] if axis == "y" else ref.at[:, pl.ds(index, 1)]

    def send(self):
        axis = self.order[self.stage]
        other = 1 - self.at.place[axis]
        current, arriving = getattr(self.w, f"s{self.stage}"), getattr(self.w, f"r{self.stage}")
        self.group = self.links.group([(self.view(current, axis, other), arriving, self.at.peer({axis: other}))])

    def collect(self):
        at, w = self.at, self.w
        self.group.wait()
        if self.stage < 0:
            for y in range(2):
                for t in range(self.taps):
                    mine = self.grad[t, aligned(SL * (2 * y + at.core), SL), :].astype(F32)
                    total = (mine + w.rc[y, t].astype(F32)).astype(BF)
                    for half in range(2):
                        w.s0[y, half, SL * t : SL * t + SL, :] = total[:, 128 * half : 128 * half + 128]
            return
        axis = self.order[self.stage]
        mine = self.view(getattr(w, f"s{self.stage}"), axis, at.place[axis])[...].astype(F32)
        total = mine + getattr(w, f"r{self.stage}")[...].astype(F32)
        getattr(w, f"s{self.stage + 1}")[...] = total.astype(BF)

    def across_teams(self, piece):
        at, w = self.at, self.w
        own = self.links.here(piece, w.rt.at[at.lead])
        group = self.links.group([
            (piece, w.rt.at[at.lead], at.device((at.lead + s) % at.teams * at.team + at.rank))
            for s in range(1, at.teams)])
        own.wait()
        group.wait()
        total = w.rt[0].astype(F32)
        for s in range(1, at.teams):
            total = total + w.rt[s].astype(F32)
        w.pc[...] = total.astype(BF)
        return w.pc

    def share(self, source):
        source = self.across_teams(source) if self.at.teams > 1 else source
        target = self.out.at[:, pl.ds(self.at.place["x"], 1)]
        self.at.results.copy(source, target)
        self.group = self.links.group([(source, target, self.at.peer(dict(x=1 - self.at.place["x"])))])

    def advance(self):
        last = len(self.order) - 1
        if self.stage <= last:
            self.collect()
        if self.stage < last:
            self.stage += 1
            self.send()
        else:
            self.along_z(self.stage - last, getattr(self.w, f"s{last + 1}"))
            self.stage += 1

    def finish(self):
        self.group.wait()


class Chain(Reduction):
    def copy(self, sent, got, src, dst, z):
        w = self.w
        return pltpu.make_async_remote_copy(
            src_ref=src, dst_ref=dst, send_sem=w.cs.at[sent], recv_sem=w.cs.at[2 + got],
            device_id=self.at.peer(dict(z=z)), device_id_type=MESH)

    def along_z(self, step, total):
        w, count = self.w, self.size["z"]
        long, alone = count == 4, count == 1
        if step == 0:
            z = self.at.place["z"]
            self.end = (z == 0) | (z == count - 1)
            self.inner = jnp.logical_not(self.end)
            self.inward = self.copy(0, 0, total, w.c0, jnp.where(z < 2, 1, 2))
            self.swap = self.copy(0, 1, w.c1, w.c2, count - 1 - z)
            self.outward = self.copy(1, 0, w.pc, w.pc, jnp.where(z < 2, 0, 3))
            if long:
                pl.when(self.end)(self.inward.start)
            else:
                w.c1[...] = total[...]
        elif step == 1:
            if long:
                @pl.when(self.inner)
                def _():
                    self.inward.wait_recv()
                    w.c1[...] = (total[...].astype(F32) + w.c0[...].astype(F32)).astype(BF)
                    self.swap.start()
            elif not alone:
                self.swap.start()
        elif step == 2:
            def join():
                self.swap.wait_recv()
                w.pc[...] = (w.c1[...].astype(F32) + w.c2[...].astype(F32)).astype(BF)

            if long:
                @pl.when(self.inner)
                def _():
                    join()
                    self.outward.start()
            elif alone:
                w.pc[...] = w.c1[...]
            else:
                join()
        else:
            if long:
                @pl.when(self.end)
                def _():
                    self.outward.wait_recv()
                    self.inward.wait_send()

                @pl.when(self.inner)
                def _():
                    self.swap.wait_send()
                    self.outward.wait_send()
            elif not alone:
                self.swap.wait_send()
            self.share(w.pc)


class Pairs(Reduction):
    def along_z(self, step, total):
        w, z = self.w, self.at.place["z"]
        partners = [z + 1 - 2 * (z % 2), (z + 2) % 4]
        partners[self.size["z"] // 2 :] = [None] * (2 - self.size["z"] // 2)
        if step == 0:
            self.held = total
        elif partners[step - 1] is not None:
            self.group.wait()
            total = self.held[...].astype(F32) + getattr(w, f"p{step - 1}")[...].astype(F32)
            self.held = getattr(w, f"t{step - 1}")
            self.held[...] = total.astype(BF)
        if step == len(partners):
            self.share(self.held)
        elif partners[step] is not None:
            self.group = self.links.group([
                (self.held, getattr(w, f"p{step}"), self.at.peer(dict(z=partners[step])))])


YX, XY = ("y", "x"), ("x", "y")
ITEMS = {
    "ga0": (4, YX, Chain),
    "gb0": (3, YX, Chain),
    "gb1": (3, YX, Chain),
    "gb2": (3, XY, Chain),
    "gc0": (3, YX, Pairs),
    "gc1": (3, YX, Pairs),
    "gc2": (3, XY, Pairs),
}
SENDS, GROUPS_OF_COPIES = 8, 72
GAINS = ("gain1", "shift1", "gain2", "shift2", "gain3", "shift3")


def mega(n_dp, names, *refs):
    r = SimpleNamespace(**dict(zip(names, refs)))
    team, teams = block_sizes(n_dp)
    dp, chan = lax.axis_index("dp"), lax.axis_index("chan")
    core, y, bit = chan % 2, chan // 2, dp % 2
    sibling, across, corner = (dp, 2 * y + 1 - core), (dp, 2 * (1 - y) + core), (dp, 2 * (1 - y) + 1 - core)
    beside, oblique = (dp + 1 - 2 * bit, chan), (dp + 1 - 2 * bit, 2 * (1 - y) + core)
    quads = (sibling, across, corner)
    rank, lead = dp % team, dp // team
    own_place = dict(y=y, x=bit, z=rank // 2)

    def peer(place):
        place = {**own_place, **place}
        return (lead * team + 2 * place["z"] + place["x"], 2 * place["y"] + core)

    at = SimpleNamespace(core=core, sibling=sibling, team=team, teams=teams, rank=rank, lead=lead, place=own_place,
                         peer=peer, device=lambda p: (p, chan))
    links = Links(r.send, r.recv, r.own, r.idle)
    at.results = links.here_all()

    def others():
        return [(lax.rem(dp + s, n_dp), chan) for s in range(1, n_dp)]

    barrier = pltpu.get_barrier_semaphore()
    for device in quads + (oblique,) + tuple(others()):
        pl.semaphore_signal(barrier, inc=1, device_id=device, device_id_type=MESH)
    load_x, load_ts, load_table = links.here(r.x, r.xl), links.here(r.ts, r.tss), links.here(r.table, r.tab)
    for i, name in enumerate(GAINS):
        pltpu.make_async_copy(getattr(r, name), r.pin.at[i], r.gains).start()
    load_we, load_dy, load_cnt = links.here(r.we, r.wel), links.here(r.dy, r.dyl), links.here(r.cnt, r.cns)
    mine = aligned(SL * chan, SL)
    fill = links.here_all([
        (r.w1, r.w1g.at[:, mine, :]), (r.w2, r.w2g.at[:, mine, :]), (r.we, r.weg.at[:, mine, :]),
        (r.wq, r.wqg.at[0:3, mine, :]), (r.wo, r.wqg.at[3:4, mine, :])])

    def pack(src, dst):
        for k in range(CHAN):
            for half in range(2):
                rows = slice(128 * half, 128 * half + 128)
                both = jnp.concatenate([src[2 * k, rows, :].astype(F32), src[2 * k + 1, rows, :].astype(F32)], axis=1)
                dst[k, rows, :] = both.astype(BF)

    load_x.wait()
    pack(r.xl, r.xp)
    pltpu.make_async_copy(r.pin, r.pin, r.gains).wait()
    r.par[...] = jnp.zeros((8, 128), F32)
    for i in range(len(GAINS)):
        r.par[i : i + 1, 0:SL] = r.pin[i].astype(F32)
    pl.semaphore_wait(barrier, CHAN + n_dp - 1)

    part = 32 * bit
    far = SL * (2 * (1 - y) + core)

    class Share:
        def __init__(self, w, g, half):
            self.w, self.g, self.half = w, g, half
            self.from_sibling = links.group()
            rows = (part, 32) if half else (0, SL)
            self.over = links.group([
                (w.at[:, aligned(*rows), :], g.at[:, aligned(SL * chan + rows[0], rows[1]), :], across)])

        def own(self):
            self.from_sibling.remote(self.w, self.g.at[:, mine, :], sibling)

        def relay(self):
            self.over.wait()
            if self.half:
                piece = self.g.at[:, aligned(far + part, 32), :]
                self.around = links.group([(piece, piece, beside)])
            else:
                piece = self.g.at[:, aligned(far, SL), :]
            self.from_sibling.remote(piece, piece, sibling)

        def relay_again(self):
            self.around.wait()
            piece = self.g.at[:, aligned(far + 32 - part, 32), :]
            self.from_sibling.remote(piece, piece, sibling)

        def landed(self):
            self.from_sibling.wait()

    def rows3(ref, row):
        return ref.at[3 * row : 3 * row + 3]

    one = [Share(rows3(r.w1, row), rows3(r.w1g, row), True) for row in range(3)]
    for share in one:
        share.own()

    load_ts.wait()
    row8 = lax.broadcasted_iota(jnp.int32, (8, 128), 0)
    times = jnp.zeros((8, 128), F32)
    for i in range(8):
        times = jnp.where(row8 == i, r.tss[i].astype(F32), times)
    r.tl[...] = times
    r.ta[dp] = times
    steps = r.table.shape[0]
    load_table.wait()

    def embeddings(times):
        count = times.shape[0]
        wide = jnp.broadcast_to(times[:, 0:1], (count, steps))
        hot = jnp.where(wide == lax.broadcasted_iota(jnp.int32, (count, steps), 1).astype(F32), 1.0, 0.0)
        temb = dot(hot.astype(BF), r.tab[...])
        s = sigmoid(temb)
        return temb, s, (temb * s).astype(BF)

    _, _, tsil = embeddings(jnp.concatenate([times, times], axis=0))
    load_we.wait()
    r.el[...] = jnp.zeros((8, 128), F32)
    r.el[:, 0:SL] = dot_nt(tsil, r.wel[0])[0:8]
    r.eg[chan] = r.el[...]
    moves_x = links.group(
        [(r.xp.at[d[1]], r.xg.at[chan], d) for d in quads] + [(r.par, r.pg.at[chan], d) for d in quads])
    moves_emb = links.group([(r.el, r.eg.at[chan], d) for d in quads])
    r.xg[chan] = r.xp[chan]
    r.pg[chan] = r.par[...]
    at_row = lax.broadcasted_iota(jnp.int32, (C, C), 0) // (C // GROUPS)
    at_col = lax.broadcasted_iota(jnp.int32, (C, C), 1) // (C // GROUPS)
    r.bd[...] = jnp.where(at_row == at_col, 1.0, 0.0).astype(BF)
    for ref in (r.a1, r.a2, r.dd):
        for gap in range(3):
            ref[gap * STEP : gap * STEP + GAP, :] = jnp.zeros((GAP, 3 * C), BF)
    load_dy.wait()
    pack(r.dyl, r.dyp)
    r.dyg[chan] = r.dyp[chan]
    two = []
    for row in range(3):
        one[row].relay()
        two.append(Share(rows3(r.w2, row), rows3(r.w2g, row), row < 2))
        two[row].own()
    one[0].relay_again()
    out = [Share(r.wq, r.wqg.at[0:3], False), Share(r.wo, r.wqg.at[3:4], False)]
    for share in out:
        share.own()
    one[1].relay_again()
    moves_dy = links.group([(r.dyp.at[d[1]], r.dyg.at[chan], d) for d in quads])
    one[2].relay_again()
    mix = Share(r.we, r.weg, False)
    mix.own()
    moves_late = links.group([(r.tl, r.ta.at[dp], d) for d in others()])

    bd = r.bd[...]
    moves_x.wait()
    for b in range(2):
        first, _ = unpack(r.pg[2 * b], r.pg[2 * b + 1])
        r.pa[:, 128 * b : 128 * b + 128] = first
    par = r.pa[...]
    gain1, shift1, gain2, shift2, gain3, shift3 = [par[i : i + 1] for i in range(6)]

    def spread_out(src, at, dst, scale=None):
        for b in range(2):
            pair = unpack(src[2 * b, pl.ds(at, CH), :].astype(F32), src[2 * b + 1, pl.ds(at, CH), :].astype(F32))
            for m in range(2):
                value = pair[m] if scale is None else pair[m] * scale[m]
                dst[pl.ds(pl.multiple_of(at + m * ROWS, CH), CH), 128 * b : 128 * b + 128] = value.astype(dst.dtype)

    def open_x(i, held):
        spread_out(r.xg, chunk_at(i), r.xf)
        return held

    lax.fori_loop(0, ROWS // CH, open_x, 0)

    def rows_of(m, at):
        return pl.ds(pl.multiple_of(at + m * ROWS, CH), CH)

    def rows_gap(m, at):
        return pl.ds(pl.multiple_of(at + m * STEP, 16), CH)

    def to_shift(dst):
        def emit(m, at, u):
            write_shift(dst, m, at, u * sigmoid(u), True)
        return emit

    rstd1 = norm_forward(lambda m, at: r.xf[rows_of(m, at), :], r.n1, gain1, shift1, bd, to_shift(r.a1),
                         early=two[0].relay, midway=two[1].relay)
    fill.wait()

    for share in one:
        share.landed()
    conv_forward(r.a1, r.w1g, r.h, (0, 1, 2), False)
    moves_emb.wait()
    for b in range(2):
        first, _ = unpack(r.eg[2 * b], r.eg[2 * b + 1])
        r.emb[:, 128 * b : 128 * b + 128] = first
    emb = [r.emb[pl.ds(2 * chan + m, 1), :] for m in range(2)]
    rstd2 = norm_forward(lambda m, at: r.h[rows_gap(m, at), :] + emb[m], r.n2, gain2, shift2, bd, to_shift(r.a2),
                         midway=two[2].relay)
    two[0].relay_again()
    two[1].relay_again()
    two[0].landed()
    two[2].landed()
    conv_forward(r.a2, r.w2g, r.h, (0, 2), False)
    for share in out:
        share.relay()
    two[1].landed()
    conv_forward(r.a2, r.w2g, r.h, (1,), True)

    def load_resid(m, at):
        return r.xf[rows_of(m, at), :]

    def make_resid(m, at):
        value = r.xf[rows_of(m, at), :] + r.h[rows_gap(m, at), :]
        r.xf[rows_of(m, at), :] = value
        return value

    def to_a3(m, at, u):
        r.a3[rows_of(m, at), :] = u.astype(BF)

    rstd3 = norm_forward(load_resid, r.n3, gain3, shift3, bd, to_a3, first=make_resid)
    out[0].landed()
    for j, ref in enumerate((r.q, r.k, r.v)):
        ref[...] = dot_nt(r.a3[...], r.wqg[j]).astype(BF)
    load_cnt.wait()
    count = r.cns[0]
    live = [jnp.where(2 * chan + m < count, 1.0, 0.0).astype(F32) for m in range(2)]
    scale = C ** (-0.5)
    half = [slice(0, ROWS), slice(ROWS, 2 * ROWS)]
    for m in range(2):
        s = dot_nt(r.q[half[m], :], r.k[half[m], :]) * scale
        p = jnp.exp(s - jnp.max(s, axis=1, keepdims=True))
        p = p * (1.0 / jnp.sum(p, axis=1, keepdims=True))
        r.p[half[m], :] = p
        r.pb[half[m], :] = p.astype(BF)
        r.o[half[m], :] = dot(p.astype(BF), r.v[half[m], :]).astype(BF)

    moves_dy.wait()
    out[1].landed()

    def open_dy(i, held):
        spread_out(r.dyg, chunk_at(i), r.g, live)
        return held

    lax.fori_loop(0, ROWS // CH, open_dy, 0)
    for m in range(2):
        r.turn[m] = r.g[half[m], :].T
    r.dqo[3] = (dot(r.turn[0], r.o[half[0], :]) + dot(r.turn[1], r.o[half[1], :])).astype(BF)
    r.do[...] = dot(r.g[...], r.wqg[3]).astype(BF)
    for m in range(2):
        dp_m = dot_nt(r.do[half[m], :], r.v[half[m], :])
        p = r.p[half[m], :]
        ds = (p * (dp_m - jnp.sum(p * dp_m, axis=1, keepdims=True)) * scale).astype(BF)
        r.dv[half[m], :] = dot(r.pb[half[m], :].T, r.do[half[m], :]).astype(BF)
        r.dq[half[m], :] = dot(ds, r.k[half[m], :]).astype(BF)
        r.dk[half[m], :] = dot(ds.T, r.q[half[m], :]).astype(BF)
    for j, ref in enumerate((r.dq, r.dk, r.dv)):
        parts = [dot(ref[half[m], :].T, r.a3[half[m], :]) for m in range(2)]
        r.dqo[j] = (parts[0] + parts[1]).astype(BF)

    items = []

    def reduce(letter, grad):
        start = 0
        for name, (taps, order, kind) in ITEMS.items():
            if name[1] == letter:
                work = SimpleNamespace(**{k[4:]: getattr(r, k) for k in names if k.startswith(name + "_")})
                items.append(kind(at, links, grad.at[start : start + taps], getattr(r, name), work, order))
                start += taps

    def go(*which):
        for i in which:
            items[i].advance()

    reduce("a", r.dqo)
    for m in range(2):
        total = None
        for j, ref in enumerate((r.dq, r.dk, r.dv)):
            part_j = dot(ref[half[m], :], r.wqg[j])
            total = part_j if total is None else total + part_j
        r.h[m * STEP : m * STEP + ROWS, :] = total

    def to_dres(m, at, dv, held):
        value = r.g[rows_of(m, at), :].astype(F32) + dv
        r.dres[rows_of(m, at), :] = value
        write_shift(r.dd, m, at, value, False)
        return held

    passes(norm_back(r.h, r.n3, gain3, shift3, rstd3, bd, False, r.e, 4, to_dres))
    go(0)

    def turn():
        for m in range(2):
            r.turn[m] = r.dd[GAP + STEP * m : GAP + STEP * m + ROWS, C : 2 * C].T

    turn()
    for row in range(3):
        conv_weight(r.a2, r.turn, r.dw2, row)
    reduce("b", r.dw2)
    conv_back(r.dd, r.w2g, r.h)
    mix.relay()

    def to_dh1(m, at, dv, held):
        write_shift(r.dd, m, at, dv, False)
        return held + fold(dv)

    second = norm_back(r.h, r.n2, gain2, shift2, rstd2, bd, True, r.e, 2, to_dh1)
    go(1, 2, 3)
    demb = passes(second, zero_pair())
    for m in range(2):
        r.dm[chan, m : m + 1, :] = col(demb[m]).astype(BF).astype(F32)
    moves_dm = links.group([(r.dm.at[chan], r.dm.at[chan], d) for d in quads])
    turn()
    for row in range(3):
        conv_weight(r.a1, r.turn, r.dw1, row)
    reduce("c", r.dw1)
    r.big[...] = dot_nt(r.o[...], r.wqg[3])

    def pack_out(at, pair, dst):
        for b in range(2):
            even, odd = unpack(*(v[:, 128 * b : 128 * b + 128] for v in pair))
            dst[2 * b, pl.ds(at, CH), :] = even.astype(BF)
            dst[2 * b + 1, pl.ds(at, CH), :] = odd.astype(BF)

    def to_y(i, held):
        at = chunk_at(i)
        pack_out(at, [(load_resid(m, at) + r.big[rows_of(m, at), :]) * live[m] for m in range(2)], r.yp)
        return held

    lax.fori_loop(0, ROWS // CH, to_y, 0)

    def data_one():
        conv_back(r.dd, r.w1g, r.h)

    def norm_one():
        back1 = norm_back(r.h, r.n1, gain1, shift1, rstd1, bd, True, r.e, 0,
                          lambda m, at, dv, held: r.dres[rows_of(m, at), :] + dv)

        def to_maps(i, held):
            at = chunk_at(i)
            pack_out(at, [back1(m, at, 0) for m in range(2)], r.mp)
            return held

        lax.fori_loop(0, ROWS // CH, to_maps, 0)
        moves_dm.wait()
        for j in range(CHAN):
            r.dl[2 * j : 2 * j + 2, :] = r.dm[j, 0:2, :]
        r.ra[dp] = r.dl[...]
        for d in others():
            moves_late.remote(r.dl, r.ra.at[dp], d)
        for b in range(2):
            block = r.e[:, 128 * b : 128 * b + 128]
            r.es[2 * b] = block
            r.es[2 * b + 1] = pltpu.roll(block, SL, 1)
        r.er[chan] = r.es[chan]
        for d in quads:
            moves_e.remote(r.es.at[d[1]], r.er.at[chan], d)

    def send_maps():
        for src, dst in ((r.yp, r.yo), (r.mp, r.mo)):
            at.results.copy(src.at[chan], dst.at[chan])
            for d in quads:
                moves_out.remote(src.at[d[1]], dst.at[chan], d)

    def send_gains():
        moves_e.wait()
        r.et[...] = r.er[0] + r.er[1] + r.er[2] + r.er[3]
        at.results.copy(r.et, r.ext.at[dp])
        for d in others():
            moves_out.remote(r.et, r.ext.at[dp], d)

    def embedding():
        mix.landed()
        moves_late.wait()
        maps = 8 * n_dp
        temb, s, tsil = embeddings(r.ta[...].reshape(maps, 128))
        rows = r.ra[...].reshape(maps, C)
        r.rt[...] = rows.T
        r.dew[...] = dot(r.rt[mine, :].astype(BF), tsil)
        dtemb = dot(rows.astype(BF), r.weg[0]) * (s * (1.0 + temb * (1.0 - s)))
        high = dtemb.astype(BF)
        r.bw[0:maps, :] = high
        r.bw[maps:, :] = (dtemb - high.astype(F32)).astype(BF)
        for src, dst in ((r.dew, r.de), (r.bw, r.both), (r.ta, r.tall)):
            at.results.copy(src, dst)

    moves_e, moves_out = links.group(), links.group()
    go(0)
    data_one()
    go(6, 4, 5, 3, 1)
    norm_one()
    go(2, 0, 4, 6)
    send_maps()
    go(1, 5, 0, 2, 3)
    send_gains()
    go(4, 6, 1, 5, 2, 0, 3)
    embedding()
    go(4, 6, 1, 5, 2, 0, 3, 1, 4, 2, 3, 6, 5)
    for item in items:
        item.finish()
    at.results.wait()
    moves_out.wait()
    links.close()


def finish(n_dp, names, *refs):
    r = SimpleNamespace(**dict(zip(names, refs)))
    maps = 8 * n_dp
    steps = r.dt.shape[0]
    links = Links(None, None, r.own, None)
    items = list(ITEMS)
    load = {name: links.here(getattr(r, name), getattr(r, name + "_v"))
            for name in ["tall", "both", "yo", "mo", "de"] + items + ["ext"]}
    stores = []

    def out(src, dst):
        stores.append(links.here(src, dst))

    load["tall"].wait()
    load["both"].wait()
    lanes = r.tall_v[...].reshape(maps, 128).T[0:1, :]
    lanes = jnp.concatenate([lanes, lanes], axis=1)
    for start in range(0, steps, 256):
        size = min(256, steps - start)
        ids = lax.broadcasted_iota(jnp.int32, (size, 2 * maps), 0).astype(F32) + float(start)
        hot = jnp.where(ids == lanes, 1.0, 0.0).astype(BF)
        r.dt_v[start : start + size, :] = dot(hot, r.both_v[...])
        out(r.dt_v.at[start : start + size], r.dt.at[start : start + size])

    def unpack_maps(name, dst, dst_v):
        load[name].wait()
        src = getattr(r, name + "_v")
        for j in range(CHAN):
            block = src[j].astype(F32)
            dst_v[2 * j] = block[:, 0:SL].astype(BF)
            dst_v[2 * j + 1] = pltpu.roll(block, SL, 1)[:, 0:SL].astype(BF)
        out(dst_v, dst)

    def whole(name, dst_v, base, taps):
        src = getattr(r, name + "_v")
        for i, t in enumerate(taps):
            for half in range(2):
                dst_v[base + i, :, 128 * half : 128 * half + 128] = src[0, half, SL * t : SL * t + SL, :].astype(F32)

    unpack_maps("yo", r.y, r.y_v)
    unpack_maps("mo", r.dm, r.dm_v)
    load["de"].wait()
    out(r.de_v, r.de_out)
    load["ga0"].wait()
    whole("ga0", r.dq_v, 0, range(3))
    out(r.dq_v, r.dq)
    whole("ga0", r.do_v, 0, [3])
    out(r.do_v, r.do)
    for letter, dst_v, dst in (("b", r.d2_v, r.d2), ("c", r.d1_v, r.d1)):
        start = 0
        for name, (taps, _, _) in ITEMS.items():
            if name[1] == letter:
                load[name].wait()
                whole(name, dst_v, start, range(taps))
                out(dst_v.at[start : start + taps], dst.at[start : start + taps])
                start += taps
    load["ext"].wait()
    total = r.ext_v[0]
    for i in range(1, n_dp):
        total = total + r.ext_v[i]
    for i in range(6):
        r.gains_v[i] = total[i : i + 1, 0:SL]
        out(r.gains_v.at[i], getattr(r, f"e{i}"))
    for copy in stores:
        copy.wait()


def per_device(x_maps, timesteps, counts, emb_table, w_first, w_second, w_embed, w_qkv, w_out, gain_one, shift_one,
               gain_two, shift_two, gain_three, shift_three, cotangent, *, n_dp):
    team, teams = block_sizes(n_dp)
    slots, side, _, _ = x_maps.shape
    emb = w_embed.shape[0]
    steps = emb_table.shape[0]
    inputs = dict(
        x=x_maps.reshape(slots, side * side, SL), dy=cotangent.reshape(slots, side * side, SL),
        ts=timesteps, cnt=counts, table=emb_table,
        w1=jnp.swapaxes(w_first, 2, 3).reshape(9, SL, C), w2=jnp.swapaxes(w_second, 2, 3).reshape(9, SL, C),
        we=w_embed.T[None], wq=jnp.transpose(w_qkv, (1, 2, 0)), wo=w_out.T[None])
    gains = (gain_one, shift_one, gain_two, shift_two, gain_three, shift_three)
    inputs.update({name: v.reshape(1, SL) for name, v in zip(GAINS, gains)})
    anywhere = pl.BlockSpec(memory_space=pl.ANY)

    def of(shape, dtype):
        return jax.ShapeDtypeStruct(shape, dtype)

    maps = 8 * n_dp
    middle = dict(
        yo=of((CHAN, ROWS, 128), BF), mo=of((CHAN, ROWS, 128), BF), tall=of((n_dp, 8, 128), F32),
        ext=of((n_dp, 8, 128), F32), both=of((2 * maps, emb), BF), de=of((SL, emb), F32))
    middle.update({name: of((1, 2, SL * item[0], 128), BF) for name, item in ITEMS.items()})
    v = pltpu.VMEM
    maps2 = 2 * ROWS
    scratch = dict(
        xl=v((slots, ROWS, SL), BF), dyl=v((slots, ROWS, SL), BF), pin=v((len(GAINS), 1, SL), BF),
        tss=pltpu.SMEM((slots,), jnp.int32), cns=pltpu.SMEM((1,), jnp.int32), tab=v((steps, emb), BF),
        xp=v((CHAN, ROWS, 128), BF), dyp=v((CHAN, ROWS, 128), BF),
        xg=v((CHAN, ROWS, 128), BF), dyg=v((CHAN, ROWS, 128), BF),
        yp=v((CHAN, ROWS, 128), BF), mp=v((CHAN, ROWS, 128), BF),
        w1g=v((9, C, C), BF), w2g=v((9, C, C), BF), weg=v((1, C, emb), BF), wqg=v((4, C, C), BF),
        bd=v((C, C), BF), tl=v((8, 128), F32), ta=v((n_dp, 8, 128), F32), par=v((8, 128), F32),
        pg=v((CHAN, 8, 128), F32), pa=v((8, C), F32), emb=v((8, C), F32),
        wel=v((1, SL, emb), BF), el=v((8, 128), F32), eg=v((CHAN, 8, 128), F32),
        a1=v((TALL + 2 * GAP, 3 * C), BF), a2=v((TALL + 2 * GAP, 3 * C), BF), dd=v((TALL + 2 * GAP, 3 * C), BF),
        h=v((TALL, C), F32), xf=v((maps2, C), F32), n1=v((maps2, C), F32), n2=v((maps2, C), F32),
        n3=v((maps2, C), F32), dres=v((maps2, C), F32), big=v((maps2, C), F32), p=v((maps2, C), F32),
        e=v((8, C), F32), es=v((CHAN, 8, 128), F32), er=v((CHAN, 8, 128), F32), et=v((8, 128), F32),
        dm=v((CHAN, 8, C), F32), dl=v((8, C), F32), ra=v((n_dp, 8, C), F32), rt=v((C, maps), F32),
        dew=v((SL, emb), F32), bw=v((2 * maps, emb), BF), turn=v((2, ROWS, C), BF),
        dw1=v((9, C, C), BF), dw2=v((9, C, C), BF), dqo=v((4, C, C), BF))
    for name in ("a3", "q", "k", "v", "pb", "o", "g", "do", "dq", "dk", "dv"):
        scratch[name] = v((maps2, C), BF)
    for name, (taps, order, kind) in ITEMS.items():
        buffers = reduction_scratch(taps, order, kind, teams)
        scratch.update({name + "_" + k: b for k, b in buffers.items()})
    several = len(ITEMS) if teams > 1 else 0
    scratch.update(
        idle=v((4096, 128), BF), send=pltpu.SemaphoreType.DMA((SENDS + several,)),
        recv=pltpu.SemaphoreType.DMA((GROUPS_OF_COPIES + several,)), own=pltpu.SemaphoreType.DMA((9 + several,)),
        gains=pltpu.SemaphoreType.DMA(()))
    got = pl.pallas_call(
        functools.partial(mega, n_dp, list(inputs) + list(middle) + list(scratch)),
        out_shape=tuple(middle.values()),
        in_specs=[anywhere] * len(inputs),
        out_specs=(anywhere,) * len(middle),
        scratch_shapes=list(scratch.values()),
        compiler_params=pltpu.CompilerParams(collective_id=0, has_side_effects=True, vmem_limit_bytes=60 << 20),
        name="blocks",
    )(*inputs.values())
    results = dict(
        y=of((slots, ROWS, SL), BF), dm=of((slots, ROWS, SL), BF), dt=of((steps, emb), F32), d1=of((9, SL, C), F32),
        d2=of((9, SL, C), F32), de_out=of((SL, emb), F32), dq=of((3, SL, C), F32), do=of((1, SL, C), F32))
    results.update({f"e{i}": of((1, SL), F32) for i in range(6)})
    scratch = {name + "_v": v(o.shape, o.dtype) for name, o in middle.items()}
    scratch.update({name + "_v": v(o.shape, o.dtype) for name, o in results.items() if name[0] != "e"})
    scratch.update(gains_v=v((6, 1, SL), F32), own=pltpu.SemaphoreType.DMA((48,)))
    got = pl.pallas_call(
        functools.partial(finish, n_dp, list(middle) + list(results) + list(scratch)),
        out_shape=tuple(results.values()),
        in_specs=[anywhere] * len(middle),
        out_specs=(anywhere,) * len(results),
        scratch_shapes=list(scratch.values()),
        compiler_params=pltpu.CompilerParams(vmem_limit_bytes=60 << 20),
        name="finish",
    )(*got)
    got = dict(zip(results, got))
    return (
        got["y"].reshape(x_maps.shape), got["dm"].reshape(x_maps.shape), got["dt"],
        jnp.swapaxes(got["d1"].reshape(3, 3, SL, C), 2, 3), jnp.swapaxes(got["d2"].reshape(3, 3, SL, C), 2, 3),
        got["de_out"].T, jnp.transpose(got["dq"], (2, 0, 1)), got["do"].reshape(SL, C).T,
    ) + tuple(got[f"e{i}"].reshape(SL) for i in range(6))


def solution(mesh):
    weights = (P(None, None, None, "chan"), P(None, None, None, "chan"), P(None, "chan"), P(None, None, "chan"),
               P(None, "chan")) + (P("chan"),) * 6
    maps = P("dp", None, None, "chan")
    return jax.shard_map(
        functools.partial(per_device, n_dp=mesh.shape["dp"]), mesh=mesh,
        in_specs=(maps, P("dp"), P("dp"), P()) + weights + (maps,),
        out_specs=(maps, maps, P()) + weights, check_vma=False)
```

```python
import functools
from types import SimpleNamespace

import jax
import jax.numpy as jnp
from jax import lax
from jax.experimental import pallas as pl
from jax.experimental.pallas import tpu as pltpu
from jax.sharding import PartitionSpec as P

F32 = jnp.float32
BF = jnp.bfloat16
MESH = pl.DeviceIdType.MESH
EPS = 1e-06
GROUPS = 32
CHAN = 4
ROWS = 256
C = 256
SL = C // CHAN
GAP = 16
STEP = ROWS + GAP
TALL = 2 * ROWS + GAP
CH = 128
COUNT = ROWS * (C // GROUPS)


def dot(a, b):
    return jnp.dot(a, b, preferred_element_type=F32)


def dot_nt(a, b):
    return lax.dot_general(a, b, (((1,), (1,)), ((), ())), preferred_element_type=F32)


def sigmoid(u):
    return 0.5 * jnp.tanh(0.5 * u) + 0.5


def fold(v):
    return v.reshape(v.shape[0] // 8, 8, v.shape[1]).sum(axis=0)


def group_total(rows, bd):
    at = lax.broadcasted_iota(jnp.int32, (8, C), 0)
    stack = jnp.zeros((8, C), F32)
    for i, row in enumerate(rows):
        stack = jnp.where(at == i, row, stack)
    high = stack.astype(BF).astype(F32)
    rest = stack - high
    mid = rest.astype(BF).astype(F32)
    parts = jnp.concatenate([high, mid, rest - mid, jnp.zeros((8, C), F32)], axis=0)
    total = dot(parts.astype(BF), bd)
    total = total[0:8] + total[8:16] + total[16:24]
    return [total[i : i + 1] for i in range(len(rows))]


def chunk_at(i):
    return pl.multiple_of(i * CH, CH)


def passes(body, carry=None):
    carry = (0, 0) if carry is None else carry

    def step(i, held):
        return tuple(body(m, chunk_at(i), held[m]) for m in range(2))

    return lax.fori_loop(0, ROWS // CH, step, carry)


def zero_pair():
    return (jnp.zeros((8, C), F32), jnp.zeros((8, C), F32))


def col(v):
    return jnp.sum(v, axis=0, keepdims=True)


def write_shift(dst, m, at, value, forward):
    place = lax.broadcasted_iota(jnp.int32, (CH, C), 0) % 16
    before = jnp.where(place == 0, 0.0, pltpu.roll(value, 1, 0))
    after = jnp.where(place == 15, 0.0, pltpu.roll(value, CH - 1, 0))
    first, last = (before, after) if forward else (after, before)
    rows = pl.ds(pl.multiple_of(at + (GAP + m * STEP), 16), CH)
    dst[rows, 0:C] = first.astype(BF)
    dst[rows, C : 2 * C] = value.astype(BF)
    dst[rows, 2 * C : 3 * C] = last.astype(BF)


def norm_forward(load, n_ref, gain, shift, bd, emit, first=None, early=None, midway=None):
    sums = []
    for at in range(0, ROWS, CH):
        for m in range(2):
            value = (first or load)(m, at)
            if at == 0:
                near = col(value[0:32]) * (1.0 / 32)
                sums.append([near, zero_pair()[0], zero_pair()[0]])
            d = value - sums[m][0]
            sums[m][1] = sums[m][1] + fold(d)
            sums[m][2] = sums[m][2] + fold(d * d)
    if early is not None:
        early()
    ones = [col(t[1]) for t in sums]
    middle = [t[0] + one * (1.0 / ROWS) for t, one in zip(sums, ones)]
    mean = [v * (GROUPS / C) for v in group_total(middle, bd)]
    spread = [
        col(t[2]) - one * one * (1.0 / ROWS) + ROWS * (mid - mu) * (mid - mu)
        for t, one, mid, mu in zip(sums, ones, middle, mean)]
    rstd = [lax.rsqrt(v * (1.0 / COUNT) + EPS) for v in group_total(spread, bd)]
    if midway is not None:
        midway()

    def last(m, at, held):
        n = (load(m, at) - mean[m]) * rstd[m]
        n_ref[pl.ds(pl.multiple_of(at + m * ROWS, CH), CH), :] = n
        emit(m, at, n * gain + shift)
        return held

    passes(last)
    return rstd


def norm_back(d_ref, n_ref, gain, shift, rstd, bd, active, e_ref, e_at, emit):
    def rows(m, at):
        return pl.ds(pl.multiple_of(at + m * STEP, 16), CH)

    def first(m, at, held):
        d = d_ref[rows(m, at), :]
        n = n_ref[pl.ds(pl.multiple_of(at + m * ROWS, CH), CH), :]
        if active:
            u = n * gain + shift
            s = sigmoid(u)
            d = d * (s * (1.0 + u * (1.0 - s)))
            d_ref[rows(m, at), :] = d
        return (held[0] + fold(d), held[1] + fold(d * n))

    total = passes(first, (zero_pair(), zero_pair()))
    ones = [col(t[0]) for t in total]
    twos = [col(t[1]) for t in total]
    e_ref[e_at : e_at + 1, :] = twos[0] + twos[1]
    e_ref[e_at + 1 : e_at + 2, :] = ones[0] + ones[1]
    means = group_total([gain * v for v in ones + twos], bd)
    means = [v * (1.0 / COUNT) for v in means]

    def second(m, at, held):
        d = d_ref[rows(m, at), :]
        n = n_ref[pl.ds(pl.multiple_of(at + m * ROWS, CH), CH), :]
        return emit(m, at, rstd[m] * (d * gain - means[m] - n * means[2 + m]), held)

    return second


def unpack(low, high):
    lane = lax.broadcasted_iota(jnp.int32, low.shape, 1)
    first = jnp.where(lane < SL, low, pltpu.roll(high, SL, 1))
    second = jnp.where(lane < SL, pltpu.roll(low, SL, 1), high)
    return first, second


BLOCKS = ((0, STEP), (STEP, ROWS))


def conv_forward(a_ref, w_ref, h_ref, rows):
    for start, size in BLOCKS:
        total = None
        for row in rows:
            for c in range(3):
                at = 16 * row + start
                part = dot_nt(a_ref[at : at + size, C * c : C * c + C], w_ref[3 * row + c])
                total = part if total is None else total + part
        h_ref[start : start + size, :] = total


def conv_back(d_ref, w_ref, h_ref):
    for start, size in BLOCKS:
        total = None
        for row in range(3):
            at = 16 * (2 - row) + start
            part = dot(d_ref[at : at + size, :], w_ref[3 * row : 3 * row + 3].reshape(3 * C, C))
            total = part if total is None else total + part
        h_ref[start : start + size, :] = total


def conv_weight(a_ref, turned, dw_ref, row):
    for c in range(3):
        total = None
        for m in range(2):
            at = 16 * row + STEP * m
            part = dot(turned[m], a_ref[at : at + ROWS, C * c : C * c + C])
            total = part if total is None else total + part
        dw_ref[3 * row + c] = total.astype(BF)


class Group:
    def __init__(self, links):
        self.links, self.at, self.rows = links, links.used, 0
        links.used += 1

    def remote(self, src, dst, device):
        self.plan(src, dst, device)()

    def plan(self, src, dst, device):
        links, rows = self.links, rows_in(src)
        if links.sending + rows > links.idle.shape[0]:
            links.ended.append((links.senders, links.sending))
            links.senders, links.sending = links.senders + 1, 0
        links.sending += rows
        self.rows += rows
        sender = links.send.at[links.senders]
        return lambda: pltpu.make_async_remote_copy(
            src_ref=src, dst_ref=dst, send_sem=sender, recv_sem=links.recv.at[self.at],
            device_id=device, device_id_type=MESH).start()

    def wait(self):
        self.links.wait_rows(self.links.recv.at[self.at], self.rows)


class LocalGroup:
    def __init__(self, links):
        self.links, self.at, self.rows = links, links.local, 0
        links.local += 1

    def copy(self, src, dst):
        self.rows += rows_in(src)
        pltpu.make_async_copy(src, dst, self.links.own.at[self.at]).start()

    def wait(self):
        self.links.wait_rows(self.links.own.at[self.at], self.rows)


def rows_in(ref):
    size = ref.dtype.itemsize
    for n in ref.shape:
        size *= n
    return size // 256


class Links:
    def __init__(self, send, recv, own, idle):
        self.send, self.recv, self.own, self.idle = send, recv, own, idle
        self.used, self.local, self.senders, self.sending = 0, 0, 0, 0
        self.ended = []

    def wait_rows(self, semaphore, rows):
        view = self.idle.at[0:rows]
        pltpu.make_async_copy(view, view, semaphore).wait()

    def group(self, copies=()):
        group = Group(self)
        for src, dst, device in copies:
            group.remote(src, dst, device)
        return group

    def here(self, src, dst):
        copy = pltpu.make_async_copy(src, dst, self.own.at[self.local])
        self.local += 1
        copy.start()
        return copy

    def here_all(self, copies=()):
        group = LocalGroup(self)
        for src, dst in copies:
            group.copy(src, dst)
        return group

    def close(self):
        for at, rows in self.ended + [(self.senders, self.sending)]:
            self.wait_rows(self.send.at[at], rows)


def block_sizes(n_dp):
    team = min(8, n_dp)
    return team, n_dp // team


def aligned(start, size):
    return pl.ds(pl.multiple_of(start, size), size)


def reduction_scratch(taps, order, kind, teams):
    rows = SL * taps
    part = (1, 1, rows, 128)
    shapes = dict(rc=(2, taps, SL, C), s0=(2, 2, rows, 128), pc=part, rt=(teams,) + part)
    shapes.update({name: part for name in ("c0", "c1", "c2", "p0", "p1", "t0", "t1")})
    size = dict(y=2, x=2)
    for k, axis in enumerate(order):
        size[axis] = 1
        shapes[f"r{k}"] = shapes[f"s{k + 1}"] = (size["y"], size["x"], rows, 128)
    buffers = {name: pltpu.VMEM(shape, BF) for name, shape in shapes.items()}
    if kind is Chain:
        buffers.update(cs=pltpu.SemaphoreType.DMA((4,)))
    return buffers


class Reduction:
    def __init__(self, at, links, grad, out, work, order):
        self.at, self.links, self.grad, self.out, self.w, self.order = at, links, grad, out, work, order
        self.taps = grad.shape[0]
        self.size = dict(y=2, x=2, z=at.team // 2)
        self.stage = -1
        self.whole = dict(y=True, x=True)
        self.group = links.group([
            (grad.at[:, aligned(SL * (2 * y + 1 - at.core), SL), :], self.w.rc.at[y], at.sibling) for y in range(2)])

    def view(self, ref, axis, index):
        return ref.at[pl.ds(index, 1)] if axis == "y" else ref.at[:, pl.ds(index, 1)]

    def send(self):
        axis = self.order[self.stage]
        other = 1 - self.at.place[axis]
        current, arriving = getattr(self.w, f"s{self.stage}"), getattr(self.w, f"r{self.stage}")
        self.group = self.links.group([(self.view(current, axis, other), arriving, self.at.peer({axis: other}))])

    def collect(self):
        at, w = self.at, self.w
        self.group.wait()
        if self.stage < 0:
            for y in range(2):
                for t in range(self.taps):
                    mine = self.grad[t, aligned(SL * (2 * y + at.core), SL), :].astype(F32)
                    total = (mine + w.rc[y, t].astype(F32)).astype(BF)
                    for half in range(2):
                        w.s0[y, half, SL * t : SL * t + SL, :] = total[:, 128 * half : 128 * half + 128]
            return
        axis = self.order[self.stage]
        mine = self.view(getattr(w, f"s{self.stage}"), axis, at.place[axis])[...].astype(F32)
        total = mine + getattr(w, f"r{self.stage}")[...].astype(F32)
        getattr(w, f"s{self.stage + 1}")[...] = total.astype(BF)

    def across_teams(self, piece):
        at, w = self.at, self.w
        own = self.links.here(piece, w.rt.at[at.lead])
        group = self.links.group([
            (piece, w.rt.at[at.lead], at.device((at.lead + s) % at.teams * at.team + at.rank))
            for s in range(1, at.teams)])
        own.wait()
        group.wait()
        total = w.rt[0].astype(F32)
        for s in range(1, at.teams):
            total = total + w.rt[s].astype(F32)
        w.pc[...] = total.astype(BF)
        return w.pc

    def share(self, source):
        source = self.across_teams(source) if self.at.teams > 1 else source
        target = self.out.at[:, pl.ds(self.at.place["x"], 1)]
        self.at.results.copy(source, target)
        self.group = self.links.group([(source, target, self.at.peer(dict(x=1 - self.at.place["x"])))])

    def advance(self):
        last = len(self.order) - 1
        if self.stage <= last:
            self.collect()
        if self.stage < last:
            self.stage += 1
            self.send()
        else:
            self.along_z(self.stage - last, getattr(self.w, f"s{last + 1}"))
            self.stage += 1

    def finish(self):
        self.group.wait()


class Chain(Reduction):
    def copy(self, sent, got, src, dst, z):
        w = self.w
        return pltpu.make_async_remote_copy(
            src_ref=src, dst_ref=dst, send_sem=w.cs.at[sent], recv_sem=w.cs.at[2 + got],
            device_id=self.at.peer(dict(z=z)), device_id_type=MESH)

    def along_z(self, step, total):
        w, count = self.w, self.size["z"]
        long, alone = count == 4, count == 1
        if step == 0:
            z = self.at.place["z"]
            self.end = (z == 0) | (z == count - 1)
            self.inner = jnp.logical_not(self.end)
            self.inward = self.copy(0, 0, total, w.c0, jnp.where(z < 2, 1, 2))
            self.swap = self.copy(0, 1, w.c1, w.c2, count - 1 - z)
            self.outward = self.copy(1, 0, w.pc, w.pc, jnp.where(z < 2, 0, 3))
            if long:
                pl.when(self.end)(self.inward.start)
            else:
                w.c1[...] = total[...]
        elif step == 1:
            if long:
                @pl.when(self.inner)
                def _():
                    self.inward.wait_recv()
                    w.c1[...] = (total[...].astype(F32) + w.c0[...].astype(F32)).astype(BF)
                    self.swap.start()
            elif not alone:
                self.swap.start()
        elif step == 2:
            def join():
                self.swap.wait_recv()
                w.pc[...] = (w.c1[...].astype(F32) + w.c2[...].astype(F32)).astype(BF)

            if long:
                @pl.when(self.inner)
                def _():
                    join()
                    self.outward.start()
            elif alone:
                w.pc[...] = w.c1[...]
            else:
                join()
        else:
            if long:
                @pl.when(self.end)
                def _():
                    self.outward.wait_recv()
                    self.inward.wait_send()

                @pl.when(self.inner)
                def _():
                    self.swap.wait_send()
                    self.outward.wait_send()
            elif not alone:
                self.swap.wait_send()
            self.share(w.pc)


class Pairs(Reduction):
    def along_z(self, step, total):
        w, z = self.w, self.at.place["z"]
        partners = [z + 1 - 2 * (z % 2), (z + 2) % 4]
        partners[self.size["z"] // 2 :] = [None] * (2 - self.size["z"] // 2)
        if step == 0:
            self.held = total
        elif partners[step - 1] is not None:
            self.group.wait()
            total = self.held[...].astype(F32) + getattr(w, f"p{step - 1}")[...].astype(F32)
            self.held = getattr(w, f"t{step - 1}")
            self.held[...] = total.astype(BF)
        if step == len(partners):
            self.share(self.held)
        elif partners[step] is not None:
            self.group = self.links.group([
                (self.held, getattr(w, f"p{step}"), self.at.peer(dict(z=partners[step])))])


YX, XY = ("y", "x"), ("x", "y")
ITEMS = {
    "ga0": (4, YX, Chain),
    "gb0": (3, YX, Chain),
    "gb1": (3, YX, Chain),
    "gb2": (3, XY, Chain),
    "gc0": (3, YX, Pairs),
    "gc1": (3, YX, Pairs),
    "gc2": (3, XY, Pairs),
}
SENDS, GROUPS_OF_COPIES = 8, 72
GAINS = ("gain1", "shift1", "gain2", "shift2", "gain3", "shift3")


def mega(n_dp, names, *refs):
    r = SimpleNamespace(**dict(zip(names, refs)))
    team, teams = block_sizes(n_dp)
    dp, chan = lax.axis_index("dp"), lax.axis_index("chan")
    core, y, bit = chan % 2, chan // 2, dp % 2
    sibling, across, corner = (dp, 2 * y + 1 - core), (dp, 2 * (1 - y) + core), (dp, 2 * (1 - y) + 1 - core)
    beside, oblique = (dp + 1 - 2 * bit, chan), (dp + 1 - 2 * bit, 2 * (1 - y) + core)
    quads = (sibling, across, corner)
    rank, lead = dp % team, dp // team
    own_place = dict(y=y, x=bit, z=rank // 2)

    def peer(place):
        place = {**own_place, **place}
        return (lead * team + 2 * place["z"] + place["x"], 2 * place["y"] + core)

    at = SimpleNamespace(core=core, sibling=sibling, team=team, teams=teams, rank=rank, lead=lead, place=own_place,
                         peer=peer, device=lambda p: (p, chan))
    links = Links(r.send, r.recv, r.own, r.idle)
    at.results = links.here_all()

    def others():
        return [(lax.rem(dp + s, n_dp), chan) for s in range(1, n_dp)]

    barrier = pltpu.get_barrier_semaphore()
    for device in quads + (oblique,) + tuple(others()):
        pl.semaphore_signal(barrier, inc=1, device_id=device, device_id_type=MESH)
    load_x, load_ts, load_table = links.here(r.x, r.xl), links.here(r.ts, r.tss), links.here(r.table, r.tab)
    for i, name in enumerate(GAINS):
        pltpu.make_async_copy(getattr(r, name), r.pin.at[i], r.gains).start()
    load_we, load_dy, load_cnt = links.here(r.we, r.wel), links.here(r.dy, r.dyl), links.here(r.cnt, r.cns)
    mine = aligned(SL * chan, SL)
    fill = links.here_all([
        (r.w1, r.w1g.at[:, mine, :]), (r.w2, r.w2g.at[:, mine, :]), (r.we, r.weg.at[:, mine, :]),
        (r.wq, r.wqg.at[0:3, mine, :]), (r.wo, r.wqg.at[3:4, mine, :])])

    def pack(src, dst):
        for k in range(CHAN):
            for half in range(2):
                rows = slice(128 * half, 128 * half + 128)
                both = jnp.concatenate([src[2 * k, rows, :].astype(F32), src[2 * k + 1, rows, :].astype(F32)], axis=1)
                dst[k, rows, :] = both.astype(BF)

    load_x.wait()
    pack(r.xl, r.xp)
    pltpu.make_async_copy(r.pin, r.pin, r.gains).wait()
    r.par[...] = jnp.zeros((8, 128), F32)
    for i in range(len(GAINS)):
        r.par[i : i + 1, 0:SL] = r.pin[i].astype(F32)
    pl.semaphore_wait(barrier, CHAN + n_dp - 1)

    far = SL * (2 * (1 - y) + core)
    low = (dp // 2) % 2
    above = (dp + 2 - 4 * low, chan) if n_dp > 2 else None

    class Share:
        def __init__(self, w, g, parts, later=None):
            self.w, self.g, self.parts = w, g, parts if n_dp > 2 else min(parts, 2)
            self.from_sibling = links.group()
            self.size = SL // self.parts
            self.part = {1: 0, 2: 32 * bit, 4: 32 * low + 16 * bit}[self.parts]
            self.over = links.group()
            start = self.over.plan(
                w.at[:, aligned(self.part, self.size), :], g.at[:, aligned(SL * chan + self.part, self.size), :], across)
            if later is None:
                start()
            else:
                later.append(start)

        def own(self):
            self.from_sibling.remote(self.w, self.g.at[:, mine, :], sibling)

        def piece(self, start, size):
            return self.g.at[:, aligned(far + start, size), :]

        def to_sibling(self, start, size):
            piece = self.piece(start, size)
            self.from_sibling.remote(piece, piece, sibling)

        def relay(self):
            self.over.wait()
            piece = self.piece(self.part, self.size)
            if self.parts > 1:
                self.around = links.group([(piece, piece, beside)])
            if self.parts < 4:
                self.to_sibling(self.part, self.size)

        def relay_up(self):
            if self.parts == 4:
                self.around.wait()
                piece = self.piece(32 * low, 32)
                self.around = links.group([(piece, piece, above)])
                self.to_sibling(32 * low, 32)

        def relay_again(self):
            self.around.wait()
            self.to_sibling(32 - 32 * (low if self.parts == 4 else bit), 32)

        def landed(self):
            self.from_sibling.wait()

    def rows3(ref, row):
        return ref.at[3 * row : 3 * row + 3]

    one = [Share(rows3(r.w1, row), rows3(r.w1g, row), 2 if row == 2 else 4) for row in range(3)]
    for share in one:
        share.own()
    later = []
    two = [Share(rows3(r.w2, row), rows3(r.w2g, row), 4, later) for row in range(2)]
    for share in two:
        share.own()

    load_ts.wait()
    row8 = lax.broadcasted_iota(jnp.int32, (8, 128), 0)
    times = jnp.zeros((8, 128), F32)
    for i in range(8):
        times = jnp.where(row8 == i, r.tss[i].astype(F32), times)
    r.tl[...] = times
    r.ta[dp] = times
    steps = r.table.shape[0]
    load_table.wait()

    def embeddings(times):
        count = times.shape[0]
        wide = jnp.broadcast_to(times[:, 0:1], (count, steps))
        hot = jnp.where(wide == lax.broadcasted_iota(jnp.int32, (count, steps), 1).astype(F32), 1.0, 0.0)
        temb = dot(hot.astype(BF), r.tab[...])
        s = sigmoid(temb)
        return temb, s, (temb * s).astype(BF)

    _, _, tsil = embeddings(jnp.concatenate([times, times], axis=0))
    load_we.wait()
    r.el[...] = jnp.zeros((8, 128), F32)
    r.el[:, 0:SL] = dot_nt(tsil, r.wel[0])[0:8]
    r.eg[chan] = r.el[...]
    moves_x, moves_emb = links.group(), links.group()
    later += [moves_x.plan(r.xp.at[d[1]], r.xg.at[chan], d) for d in quads]
    later += [moves_x.plan(r.par, r.pg.at[chan], d) for d in quads]
    later += [moves_emb.plan(r.el, r.eg.at[chan], d) for d in quads]

    def start_later():
        for start in later:
            start()

    pl.when(core == 0)(start_later)
    r.xg[chan] = r.xp[chan]
    r.pg[chan] = r.par[...]
    at_row = lax.broadcasted_iota(jnp.int32, (C, C), 0) // (C // GROUPS)
    at_col = lax.broadcasted_iota(jnp.int32, (C, C), 1) // (C // GROUPS)
    r.bd[...] = jnp.where(at_row == at_col, 1.0, 0.0).astype(BF)
    for ref in (r.a1, r.a2, r.dd):
        for gap in range(3):
            ref[gap * STEP : gap * STEP + GAP, :] = jnp.zeros((GAP, 3 * C), BF)
    load_dy.wait()
    pack(r.dyl, r.dyp)
    r.dyg[chan] = r.dyp[chan]
    for share in one:
        share.relay()
    pl.when(core == 1)(start_later)
    two.append(Share(rows3(r.w2, 2), rows3(r.w2g, 2), 1))
    two[2].own()
    one[0].relay_up()
    two[0].relay()
    one[1].relay_up()
    out = [Share(r.wq, r.wqg.at[0:3], 1), Share(r.wo, r.wqg.at[3:4], 1)]
    for share in out:
        share.own()
    two[1].relay()
    one[2].relay_again()
    two[0].relay_up()
    moves_dy = links.group([(r.dyp.at[d[1]], r.dyg.at[chan], d) for d in quads])
    mix = Share(r.we, r.weg, 1)
    mix.own()
    moves_late = links.group([(r.tl, r.ta.at[dp], d) for d in others()])
    one[0].relay_again()
    two[1].relay_up()

    bd = r.bd[...]
    moves_x.wait()
    one[1].relay_again()
    for b in range(2):
        first, _ = unpack(r.pg[2 * b], r.pg[2 * b + 1])
        r.pa[:, 128 * b : 128 * b + 128] = first
    par = r.pa[...]
    gain1, shift1, gain2, shift2, gain3, shift3 = [par[i : i + 1] for i in range(6)]

    def spread_out(src, at, dst, scale=None):
        for b in range(2):
            pair = unpack(src[2 * b, pl.ds(at, CH), :].astype(F32), src[2 * b + 1, pl.ds(at, CH), :].astype(F32))
            for m in range(2):
                value = pair[m] if scale is None else pair[m] * scale[m]
                dst[pl.ds(pl.multiple_of(at + m * ROWS, CH), CH), 128 * b : 128 * b + 128] = value.astype(dst.dtype)

    def rows_of(m, at):
        return pl.ds(pl.multiple_of(at + m * ROWS, CH), CH)

    def rows_gap(m, at):
        return pl.ds(pl.multiple_of(at + m * STEP, 16), CH)

    def to_shift(dst):
        def emit(m, at, u):
            write_shift(dst, m, at, u * sigmoid(u), True)
        return emit

    def open_x(m, at):
        if m == 0:
            spread_out(r.xg, at, r.xf)
        return r.xf[rows_of(m, at), :]

    rstd1 = norm_forward(lambda m, at: r.xf[rows_of(m, at), :], r.n1, gain1, shift1, bd, to_shift(r.a1), first=open_x)
    fill.wait()

    for share in one:
        share.landed()
    conv_forward(r.a1, r.w1g, r.h, (0, 1, 2))
    two[0].relay_again()
    moves_emb.wait()
    for b in range(2):
        first, _ = unpack(r.eg[2 * b], r.eg[2 * b + 1])
        r.emb[:, 128 * b : 128 * b + 128] = first
    emb = [r.emb[pl.ds(2 * chan + m, 1), :] for m in range(2)]
    rstd2 = norm_forward(lambda m, at: r.h[rows_gap(m, at), :] + emb[m], r.n2, gain2, shift2, bd, to_shift(r.a2),
                         early=two[2].relay, midway=two[1].relay_again)
    out[0].relay()
    for share in two:
        share.landed()
    conv_forward(r.a2, r.w2g, r.h, (0, 1, 2))
    out[1].relay()

    def load_resid(m, at):
        return r.xf[rows_of(m, at), :]

    def make_resid(m, at):
        value = r.xf[rows_of(m, at), :] + r.h[rows_gap(m, at), :]
        r.xf[rows_of(m, at), :] = value
        return value

    def to_a3(m, at, u):
        r.a3[rows_of(m, at), :] = u.astype(BF)

    rstd3 = norm_forward(load_resid, r.n3, gain3, shift3, bd, to_a3, first=make_resid)
    out[0].landed()
    for j, ref in enumerate((r.q, r.k, r.v)):
        ref[...] = dot_nt(r.a3[...], r.wqg[j]).astype(BF)
    load_cnt.wait()
    count = r.cns[0]
    live = [jnp.where(2 * chan + m < count, 1.0, 0.0).astype(F32) for m in range(2)]
    scale = C ** (-0.5)
    half = [slice(0, ROWS), slice(ROWS, 2 * ROWS)]
    for m in range(2):
        s = dot_nt(r.q[half[m], :], r.k[half[m], :]) * scale
        p = jnp.exp(s - jnp.max(s, axis=1, keepdims=True))
        p = p * (1.0 / jnp.sum(p, axis=1, keepdims=True))
        r.p[half[m], :] = p
        r.pb[half[m], :] = p.astype(BF)
        r.o[half[m], :] = dot(p.astype(BF), r.v[half[m], :]).astype(BF)

    moves_dy.wait()
    out[1].landed()

    def open_dy(i, held):
        spread_out(r.dyg, chunk_at(i), r.g, live)
        return held

    lax.fori_loop(0, ROWS // CH, open_dy, 0)
    for m in range(2):
        r.turn[m] = r.g[half[m], :].T
    r.dqo[3] = (dot(r.turn[0], r.o[half[0], :]) + dot(r.turn[1], r.o[half[1], :])).astype(BF)
    r.do[...] = dot(r.g[...], r.wqg[3]).astype(BF)
    for m in range(2):
        dp_m = dot_nt(r.do[half[m], :], r.v[half[m], :])
        p = r.p[half[m], :]
        ds = (p * (dp_m - jnp.sum(p * dp_m, axis=1, keepdims=True)) * scale).astype(BF)
        r.dv[half[m], :] = dot(r.pb[half[m], :].T, r.do[half[m], :]).astype(BF)
        r.dq[half[m], :] = dot(ds, r.k[half[m], :]).astype(BF)
        r.dk[half[m], :] = dot(ds.T, r.q[half[m], :]).astype(BF)
    for j, ref in enumerate((r.dq, r.dk, r.dv)):
        parts = [dot(ref[half[m], :].T, r.a3[half[m], :]) for m in range(2)]
        r.dqo[j] = (parts[0] + parts[1]).astype(BF)

    items = []

    def reduce(letter, grad):
        start = 0
        for name, (taps, order, kind) in ITEMS.items():
            if name[1] == letter:
                work = SimpleNamespace(**{k[4:]: getattr(r, k) for k in names if k.startswith(name + "_")})
                items.append(kind(at, links, grad.at[start : start + taps], getattr(r, name), work, order))
                start += taps

    def go(*which):
        for i in which:
            items[i].advance()

    reduce("a", r.dqo)
    for m in range(2):
        total = None
        for j, ref in enumerate((r.dq, r.dk, r.dv)):
            part_j = dot(ref[half[m], :], r.wqg[j])
            total = part_j if total is None else total + part_j
        r.h[m * STEP : m * STEP + ROWS, :] = total

    def to_dres(m, at, dv, held):
        value = r.g[rows_of(m, at), :].astype(F32) + dv
        r.dres[rows_of(m, at), :] = value
        write_shift(r.dd, m, at, value, False)
        return held

    passes(norm_back(r.h, r.n3, gain3, shift3, rstd3, bd, False, r.e, 4, to_dres))
    go(0)

    def turn():
        for m in range(2):
            r.turn[m] = r.dd[GAP + STEP * m : GAP + STEP * m + ROWS, C : 2 * C].T

    turn()
    for row in range(3):
        conv_weight(r.a2, r.turn, r.dw2, row)
    reduce("b", r.dw2)
    conv_back(r.dd, r.w2g, r.h)
    mix.relay()

    def to_dh1(m, at, dv, held):
        write_shift(r.dd, m, at, dv, False)
        return held + fold(dv)

    second = norm_back(r.h, r.n2, gain2, shift2, rstd2, bd, True, r.e, 2, to_dh1)
    go(1, 2, 3)
    demb = passes(second, zero_pair())
    for m in range(2):
        r.dm[chan, m : m + 1, :] = col(demb[m]).astype(BF).astype(F32)
    moves_dm = links.group([(r.dm.at[chan], r.dm.at[chan], d) for d in quads])
    turn()
    for row in range(3):
        conv_weight(r.a1, r.turn, r.dw1, row)
    reduce("c", r.dw1)
    r.big[...] = dot_nt(r.o[...], r.wqg[3])

    def pack_out(at, pair, dst):
        for b in range(2):
            even, odd = unpack(*(v[:, 128 * b : 128 * b + 128] for v in pair))
            dst[2 * b, pl.ds(at, CH), :] = even.astype(BF)
            dst[2 * b + 1, pl.ds(at, CH), :] = odd.astype(BF)

    def to_y(i, held):
        at = chunk_at(i)
        pack_out(at, [(load_resid(m, at) + r.big[rows_of(m, at), :]) * live[m] for m in range(2)], r.yp)
        return held

    lax.fori_loop(0, ROWS // CH, to_y, 0)

    def data_one():
        conv_back(r.dd, r.w1g, r.h)

    def norm_one():
        back1 = norm_back(r.h, r.n1, gain1, shift1, rstd1, bd, True, r.e, 0,
                          lambda m, at, dv, held: r.dres[rows_of(m, at), :] + dv)

        def to_maps(i, held):
            at = chunk_at(i)
            pack_out(at, [back1(m, at, 0) for m in range(2)], r.mp)
            return held

        lax.fori_loop(0, ROWS // CH, to_maps, 0)
        moves_dm.wait()
        for j in range(CHAN):
            r.dl[2 * j : 2 * j + 2, :] = r.dm[j, 0:2, :]
        r.ra[dp] = r.dl[...]
        for d in others():
            moves_late.remote(r.dl, r.ra.at[dp], d)
        for b in range(2):
            block = r.e[:, 128 * b : 128 * b + 128]
            r.es[2 * b] = block
            r.es[2 * b + 1] = pltpu.roll(block, SL, 1)
        r.er[chan] = r.es[chan]
        for d in quads:
            moves_e.remote(r.es.at[d[1]], r.er.at[chan], d)

    def send_maps():
        for src, dst in ((r.yp, r.yo), (r.mp, r.mo)):
            at.results.copy(src.at[chan], dst.at[chan])
            for d in quads:
                moves_out.remote(src.at[d[1]], dst.at[chan], d)

    def send_gains():
        moves_e.wait()
        r.et[...] = r.er[0] + r.er[1] + r.er[2] + r.er[3]
        at.results.copy(r.et, r.ext.at[dp])
        for d in others():
            moves_out.remote(r.et, r.ext.at[dp], d)

    def embedding():
        mix.landed()
        moves_late.wait()
        maps = 8 * n_dp
        temb, s, tsil = embeddings(r.ta[...].reshape(maps, 128))
        rows = r.ra[...].reshape(maps, C)
        r.rt[...] = rows.T
        r.dew[...] = dot(r.rt[mine, :].astype(BF), tsil)
        dtemb = dot(rows.astype(BF), r.weg[0]) * (s * (1.0 + temb * (1.0 - s)))
        high = dtemb.astype(BF)
        r.bw[0:maps, :] = high
        r.bw[maps:, :] = (dtemb - high.astype(F32)).astype(BF)
        for src, dst in ((r.dew, r.de), (r.bw, r.both), (r.ta, r.tall)):
            at.results.copy(src, dst)

    moves_e, moves_out = links.group(), links.group()
    go(0)
    data_one()
    go(6, 4, 5, 3, 1)
    norm_one()
    go(2, 0, 4, 6)
    send_maps()
    go(1, 5, 0, 2, 3)
    send_gains()
    go(4, 6, 1, 5, 2, 0, 3)
    embedding()
    go(4, 6, 1, 5, 2, 0, 3, 1, 4, 2, 3, 6, 5)
    for item in items:
        item.finish()
    at.results.wait()
    moves_out.wait()
    links.close()


def finish(n_dp, names, *refs):
    r = SimpleNamespace(**dict(zip(names, refs)))
    maps = 8 * n_dp
    steps = r.dt.shape[0]
    links = Links(None, None, r.own, None)
    items = list(ITEMS)
    load = {name: links.here(getattr(r, name), getattr(r, name + "_v"))
            for name in ["tall", "both", "yo", "mo", "de"] + items + ["ext"]}
    stores = []

    def out(src, dst):
        stores.append(links.here(src, dst))

    load["tall"].wait()
    load["both"].wait()
    lanes = r.tall_v[...].reshape(maps, 128).T[0:1, :]
    lanes = jnp.concatenate([lanes, lanes], axis=1)
    for start in range(0, steps, 256):
        size = min(256, steps - start)
        ids = lax.broadcasted_iota(jnp.int32, (size, 2 * maps), 0).astype(F32) + float(start)
        hot = jnp.where(ids == lanes, 1.0, 0.0).astype(BF)
        r.dt_v[start : start + size, :] = dot(hot, r.both_v[...])
        out(r.dt_v.at[start : start + size], r.dt.at[start : start + size])

    def unpack_maps(name, dst, dst_v):
        load[name].wait()
        src = getattr(r, name + "_v")
        for j in range(CHAN):
            block = src[j].astype(F32)
            dst_v[2 * j] = block[:, 0:SL].astype(BF)
            dst_v[2 * j + 1] = pltpu.roll(block, SL, 1)[:, 0:SL].astype(BF)
        out(dst_v, dst)

    def whole(name, dst_v, base, taps):
        src = getattr(r, name + "_v")
        for i, t in enumerate(taps):
            for half in range(2):
                dst_v[base + i, :, 128 * half : 128 * half + 128] = src[0, half, SL * t : SL * t + SL, :].astype(F32)

    unpack_maps("yo", r.y, r.y_v)
    unpack_maps("mo", r.dm, r.dm_v)
    load["de"].wait()
    out(r.de_v, r.de_out)
    load["ga0"].wait()
    whole("ga0", r.dq_v, 0, range(3))
    out(r.dq_v, r.dq)
    whole("ga0", r.do_v, 0, [3])
    out(r.do_v, r.do)
    for letter, dst_v, dst in (("b", r.d2_v, r.d2), ("c", r.d1_v, r.d1)):
        start = 0
        for name, (taps, _, _) in ITEMS.items():
            if name[1] == letter:
                load[name].wait()
                whole(name, dst_v, start, range(taps))
                out(dst_v.at[start : start + taps], dst.at[start : start + taps])
                start += taps
    load["ext"].wait()
    total = r.ext_v[0]
    for i in range(1, n_dp):
        total = total + r.ext_v[i]
    for i in range(6):
        r.gains_v[i] = total[i : i + 1, 0:SL]
        out(r.gains_v.at[i], getattr(r, f"e{i}"))
    for copy in stores:
        copy.wait()


def per_device(x_maps, timesteps, counts, emb_table, w_first, w_second, w_embed, w_qkv, w_out, gain_one, shift_one,
               gain_two, shift_two, gain_three, shift_three, cotangent, *, n_dp):
    team, teams = block_sizes(n_dp)
    slots, side, _, _ = x_maps.shape
    emb = w_embed.shape[0]
    steps = emb_table.shape[0]
    inputs = dict(
        x=x_maps.reshape(slots, side * side, SL), dy=cotangent.reshape(slots, side * side, SL),
        ts=timesteps, cnt=counts, table=emb_table,
        w1=jnp.swapaxes(w_first, 2, 3).reshape(9, SL, C), w2=jnp.swapaxes(w_second, 2, 3).reshape(9, SL, C),
        we=w_embed.T[None], wq=jnp.transpose(w_qkv, (1, 2, 0)), wo=w_out.T[None])
    gains = (gain_one, shift_one, gain_two, shift_two, gain_three, shift_three)
    inputs.update({name: v.reshape(1, SL) for name, v in zip(GAINS, gains)})
    anywhere = pl.BlockSpec(memory_space=pl.ANY)

    def of(shape, dtype):
        return jax.ShapeDtypeStruct(shape, dtype)

    maps = 8 * n_dp
    middle = dict(
        yo=of((CHAN, ROWS, 128), BF), mo=of((CHAN, ROWS, 128), BF), tall=of((n_dp, 8, 128), F32),
        ext=of((n_dp, 8, 128), F32), both=of((2 * maps, emb), BF), de=of((SL, emb), F32))
    middle.update({name: of((1, 2, SL * item[0], 128), BF) for name, item in ITEMS.items()})
    v = pltpu.VMEM
    maps2 = 2 * ROWS
    scratch = dict(
        xl=v((slots, ROWS, SL), BF), dyl=v((slots, ROWS, SL), BF), pin=v((len(GAINS), 1, SL), BF),
        tss=pltpu.SMEM((slots,), jnp.int32), cns=pltpu.SMEM((1,), jnp.int32), tab=v((steps, emb), BF),
        xp=v((CHAN, ROWS, 128), BF), dyp=v((CHAN, ROWS, 128), BF),
        xg=v((CHAN, ROWS, 128), BF), dyg=v((CHAN, ROWS, 128), BF),
        yp=v((CHAN, ROWS, 128), BF), mp=v((CHAN, ROWS, 128), BF),
        w1g=v((9, C, C), BF), w2g=v((9, C, C), BF), weg=v((1, C, emb), BF), wqg=v((4, C, C), BF),
        bd=v((C, C), BF), tl=v((8, 128), F32), ta=v((n_dp, 8, 128), F32), par=v((8, 128), F32),
        pg=v((CHAN, 8, 128), F32), pa=v((8, C), F32), emb=v((8, C), F32),
        wel=v((1, SL, emb), BF), el=v((8, 128), F32), eg=v((CHAN, 8, 128), F32),
        a1=v((TALL + 2 * GAP, 3 * C), BF), a2=v((TALL + 2 * GAP, 3 * C), BF), dd=v((TALL + 2 * GAP, 3 * C), BF),
        h=v((TALL, C), F32), xf=v((maps2, C), F32), n1=v((maps2, C), F32), n2=v((maps2, C), F32),
        n3=v((maps2, C), F32), dres=v((maps2, C), F32), big=v((maps2, C), F32), p=v((maps2, C), F32),
        e=v((8, C), F32), es=v((CHAN, 8, 128), F32), er=v((CHAN, 8, 128), F32), et=v((8, 128), F32),
        dm=v((CHAN, 8, C), F32), dl=v((8, C), F32), ra=v((n_dp, 8, C), F32), rt=v((C, maps), F32),
        dew=v((SL, emb), F32), bw=v((2 * maps, emb), BF), turn=v((2, ROWS, C), BF),
        dw1=v((9, C, C), BF), dw2=v((9, C, C), BF), dqo=v((4, C, C), BF))
    for name in ("a3", "q", "k", "v", "pb", "o", "g", "do", "dq", "dk", "dv"):
        scratch[name] = v((maps2, C), BF)
    for name, (taps, order, kind) in ITEMS.items():
        buffers = reduction_scratch(taps, order, kind, teams)
        scratch.update({name + "_" + k: b for k, b in buffers.items()})
    several = len(ITEMS) if teams > 1 else 0
    scratch.update(
        idle=v((4096, 128), BF), send=pltpu.SemaphoreType.DMA((SENDS + several,)),
        recv=pltpu.SemaphoreType.DMA((GROUPS_OF_COPIES + several,)), own=pltpu.SemaphoreType.DMA((9 + several,)),
        gains=pltpu.SemaphoreType.DMA(()))
    got = pl.pallas_call(
        functools.partial(mega, n_dp, list(inputs) + list(middle) + list(scratch)),
        out_shape=tuple(middle.values()),
        in_specs=[anywhere] * len(inputs),
        out_specs=(anywhere,) * len(middle),
        scratch_shapes=list(scratch.values()),
        compiler_params=pltpu.CompilerParams(collective_id=0, has_side_effects=True, vmem_limit_bytes=60 << 20),
        name="blocks",
    )(*inputs.values())
    results = dict(
        y=of((slots, ROWS, SL), BF), dm=of((slots, ROWS, SL), BF), dt=of((steps, emb), F32), d1=of((9, SL, C), F32),
        d2=of((9, SL, C), F32), de_out=of((SL, emb), F32), dq=of((3, SL, C), F32), do=of((1, SL, C), F32))
    results.update({f"e{i}": of((1, SL), F32) for i in range(6)})
    scratch = {name + "_v": v(o.shape, o.dtype) for name, o in middle.items()}
    scratch.update({name + "_v": v(o.shape, o.dtype) for name, o in results.items() if name[0] != "e"})
    scratch.update(gains_v=v((6, 1, SL), F32), own=pltpu.SemaphoreType.DMA((48,)))
    got = pl.pallas_call(
        functools.partial(finish, n_dp, list(middle) + list(results) + list(scratch)),
        out_shape=tuple(results.values()),
        in_specs=[anywhere] * len(middle),
        out_specs=(anywhere,) * len(results),
        scratch_shapes=list(scratch.values()),
        compiler_params=pltpu.CompilerParams(vmem_limit_bytes=60 << 20),
        name="finish",
    )(*got)
    got = dict(zip(results, got))
    return (
        got["y"].reshape(x_maps.shape), got["dm"].reshape(x_maps.shape), got["dt"],
        jnp.swapaxes(got["d1"].reshape(3, 3, SL, C), 2, 3), jnp.swapaxes(got["d2"].reshape(3, 3, SL, C), 2, 3),
        got["de_out"].T, jnp.transpose(got["dq"], (2, 0, 1)), got["do"].reshape(SL, C).T,
    ) + tuple(got[f"e{i}"].reshape(SL) for i in range(6))


def solution(mesh):
    weights = (P(None, None, None, "chan"), P(None, None, None, "chan"), P(None, "chan"), P(None, None, "chan"),
               P(None, "chan")) + (P("chan"),) * 6
    maps = P("dp", None, None, "chan")
    return jax.shard_map(
        functools.partial(per_device, n_dp=mesh.shape["dp"]), mesh=mesh,
        in_specs=(maps, P("dp"), P("dp"), P()) + weights + (maps,),
        out_specs=(maps, maps, P()) + weights, check_vma=False)
```

```python
import functools
from types import SimpleNamespace

import jax
import jax.numpy as jnp
from jax import lax
from jax.experimental import pallas as pl
from jax.experimental.pallas import tpu as pltpu
from jax.sharding import PartitionSpec as P

F32 = jnp.float32
BF = jnp.bfloat16
MESH = pl.DeviceIdType.MESH
EPS = 1e-06
GROUPS = 32
CHAN = 4
ROWS = 256
C = 256
SL = C // CHAN
GAP = 16
STEP = ROWS + GAP
TALL = 2 * ROWS + GAP
CH = 128
COUNT = ROWS * (C // GROUPS)


def dot(a, b):
    return jnp.dot(a, b, preferred_element_type=F32)


def dot_nt(a, b):
    return lax.dot_general(a, b, (((1,), (1,)), ((), ())), preferred_element_type=F32)


def sigmoid(u):
    return 0.5 * jnp.tanh(0.5 * u) + 0.5


def fold(v):
    return v.reshape(v.shape[0] // 8, 8, v.shape[1]).sum(axis=0)


def group_total(rows, bd):
    at = lax.broadcasted_iota(jnp.int32, (8, C), 0)
    stack = jnp.zeros((8, C), F32)
    for i, row in enumerate(rows):
        stack = jnp.where(at == i, row, stack)
    high = stack.astype(BF).astype(F32)
    rest = stack - high
    mid = rest.astype(BF).astype(F32)
    parts = jnp.concatenate([high, mid, rest - mid, jnp.zeros((8, C), F32)], axis=0)
    total = dot(parts.astype(BF), bd)
    total = total[0:8] + total[8:16] + total[16:24]
    return [total[i : i + 1] for i in range(len(rows))]


def chunk_at(i):
    return pl.multiple_of(i * CH, CH)


def passes(body, carry=None):
    carry = (0, 0) if carry is None else carry

    def step(i, held):
        return tuple(body(m, chunk_at(i), held[m]) for m in range(2))

    return lax.fori_loop(0, ROWS // CH, step, carry)


def zero_pair():
    return (jnp.zeros((8, C), F32), jnp.zeros((8, C), F32))


def col(v):
    return jnp.sum(v, axis=0, keepdims=True)


def write_shift(dst, m, at, value, forward):
    place = lax.broadcasted_iota(jnp.int32, (CH, C), 0) % 16
    before = jnp.where(place == 0, 0.0, pltpu.roll(value, 1, 0))
    after = jnp.where(place == 15, 0.0, pltpu.roll(value, CH - 1, 0))
    first, last = (before, after) if forward else (after, before)
    rows = pl.ds(pl.multiple_of(at + (GAP + m * STEP), 16), CH)
    dst[rows, 0:C] = first.astype(BF)
    dst[rows, C : 2 * C] = value.astype(BF)
    dst[rows, 2 * C : 3 * C] = last.astype(BF)


def norm_forward(load, n_ref, gain, shift, bd, emit, first=None, early=None, midway=None):
    sums = []
    for at in range(0, ROWS, CH):
        for m in range(2):
            value = (first or load)(m, at)
            if at == 0:
                near = col(value[0:32]) * (1.0 / 32)
                sums.append([near, zero_pair()[0], zero_pair()[0]])
            d = value - sums[m][0]
            sums[m][1] = sums[m][1] + fold(d)
            sums[m][2] = sums[m][2] + fold(d * d)
    if early is not None:
        early()
    ones = [col(t[1]) for t in sums]
    middle = [t[0] + one * (1.0 / ROWS) for t, one in zip(sums, ones)]
    mean = [v * (GROUPS / C) for v in group_total(middle, bd)]
    spread = [
        col(t[2]) - one * one * (1.0 / ROWS) + ROWS * (mid - mu) * (mid - mu)
        for t, one, mid, mu in zip(sums, ones, middle, mean)]
    rstd = [lax.rsqrt(v * (1.0 / COUNT) + EPS) for v in group_total(spread, bd)]
    if midway is not None:
        midway()

    def last(m, at, held):
        n = (load(m, at) - mean[m]) * rstd[m]
        n_ref[pl.ds(pl.multiple_of(at + m * ROWS, CH), CH), :] = n
        emit(m, at, n * gain + shift)
        return held

    passes(last)
    return rstd


def norm_back(d_ref, n_ref, gain, shift, rstd, bd, active, e_ref, e_at, emit):
    def rows(m, at):
        return pl.ds(pl.multiple_of(at + m * STEP, 16), CH)

    def first(m, at, held):
        d = d_ref[rows(m, at), :]
        n = n_ref[pl.ds(pl.multiple_of(at + m * ROWS, CH), CH), :]
        if active:
            u = n * gain + shift
            s = sigmoid(u)
            d = d * (s * (1.0 + u * (1.0 - s)))
            d_ref[rows(m, at), :] = d
        return (held[0] + fold(d), held[1] + fold(d * n))

    total = passes(first, (zero_pair(), zero_pair()))
    ones = [col(t[0]) for t in total]
    twos = [col(t[1]) for t in total]
    e_ref[e_at : e_at + 1, :] = twos[0] + twos[1]
    e_ref[e_at + 1 : e_at + 2, :] = ones[0] + ones[1]
    means = group_total([gain * v for v in ones + twos], bd)
    means = [v * (1.0 / COUNT) for v in means]

    def second(m, at, held):
        d = d_ref[rows(m, at), :]
        n = n_ref[pl.ds(pl.multiple_of(at + m * ROWS, CH), CH), :]
        return emit(m, at, rstd[m] * (d * gain - means[m] - n * means[2 + m]), held)

    return second


def unpack(low, high):
    lane = lax.broadcasted_iota(jnp.int32, low.shape, 1)
    first = jnp.where(lane < SL, low, pltpu.roll(high, SL, 1))
    second = jnp.where(lane < SL, pltpu.roll(low, SL, 1), high)
    return first, second


BLOCKS = ((0, STEP), (STEP, ROWS))


def conv_forward(a_ref, w_ref, h_ref, rows):
    for start, size in BLOCKS:
        total = None
        for row in rows:
            for c in range(3):
                at = 16 * row + start
                part = dot_nt(a_ref[at : at + size, C * c : C * c + C], w_ref[3 * row + c])
                total = part if total is None else total + part
        h_ref[start : start + size, :] = total


def conv_back(d_ref, w_ref, h_ref):
    for start, size in BLOCKS:
        total = None
        for row in range(3):
            at = 16 * (2 - row) + start
            part = dot(d_ref[at : at + size, :], w_ref[3 * row : 3 * row + 3].reshape(3 * C, C))
            total = part if total is None else total + part
        h_ref[start : start + size, :] = total


def conv_weight(a_ref, turned, dw_ref, row):
    for c in range(3):
        total = None
        for m in range(2):
            at = 16 * row + STEP * m
            part = dot(turned[m], a_ref[at : at + ROWS, C * c : C * c + C])
            total = part if total is None else total + part
        dw_ref[3 * row + c] = total.astype(BF)


class Group:
    def __init__(self, links):
        self.links, self.at, self.rows = links, links.used, 0
        links.used += 1

    def remote(self, src, dst, device):
        self.plan(src, dst, device)()

    def plan(self, src, dst, device):
        links, rows = self.links, rows_in(src)
        if links.sending + rows > links.idle.shape[0]:
            links.ended.append((links.senders, links.sending))
            links.senders, links.sending = links.senders + 1, 0
        links.sending += rows
        self.rows += rows
        sender = links.send.at[links.senders]
        return lambda: pltpu.make_async_remote_copy(
            src_ref=src, dst_ref=dst, send_sem=sender, recv_sem=links.recv.at[self.at],
            device_id=device, device_id_type=MESH).start()

    def wait(self):
        self.links.wait_rows(self.links.recv.at[self.at], self.rows)


class LocalGroup:
    def __init__(self, links):
        self.links, self.at, self.rows = links, links.local, 0
        links.local += 1

    def copy(self, src, dst):
        self.rows += rows_in(src)
        pltpu.make_async_copy(src, dst, self.links.own.at[self.at]).start()

    def wait(self):
        self.links.wait_rows(self.links.own.at[self.at], self.rows)


def rows_in(ref):
    size = ref.dtype.itemsize
    for n in ref.shape:
        size *= n
    return size // 256


class Links:
    def __init__(self, send, recv, own, idle):
        self.send, self.recv, self.own, self.idle = send, recv, own, idle
        self.used, self.local, self.senders, self.sending = 0, 0, 0, 0
        self.ended = []

    def wait_rows(self, semaphore, rows):
        view = self.idle.at[0:rows]
        pltpu.make_async_copy(view, view, semaphore).wait()

    def group(self, copies=()):
        group = Group(self)
        for src, dst, device in copies:
            group.remote(src, dst, device)
        return group

    def here(self, src, dst):
        copy = pltpu.make_async_copy(src, dst, self.own.at[self.local])
        self.local += 1
        copy.start()
        return copy

    def here_all(self, copies=()):
        group = LocalGroup(self)
        for src, dst in copies:
            group.copy(src, dst)
        return group

    def close(self):
        for at, rows in self.ended + [(self.senders, self.sending)]:
            self.wait_rows(self.send.at[at], rows)


def block_sizes(n_dp):
    team = min(8, n_dp)
    return team, n_dp // team


def aligned(start, size):
    return pl.ds(pl.multiple_of(start, size), size)


def reduction_scratch(taps, order, kind, teams):
    rows = SL * taps
    part = (1, 1, rows, 128)
    shapes = dict(rc=(2, taps, SL, C), s0=(2, 2, rows, 128), pc=part, rt=(teams,) + part)
    shapes.update({name: part for name in ("c0", "c1", "c2", "p0", "p1", "t0", "t1")})
    size = dict(y=2, x=2)
    for k, axis in enumerate(order):
        size[axis] = 1
        shapes[f"r{k}"] = shapes[f"s{k + 1}"] = (size["y"], size["x"], rows, 128)
    buffers = {name: pltpu.VMEM(shape, BF) for name, shape in shapes.items()}
    if kind is Chain:
        buffers.update(cs=pltpu.SemaphoreType.DMA((4,)))
    return buffers


class Reduction:
    def __init__(self, at, links, grad, out, work, order):
        self.at, self.links, self.grad, self.out, self.w, self.order = at, links, grad, out, work, order
        self.taps = grad.shape[0]
        self.size = dict(y=2, x=2, z=at.team // 2)
        self.stage = -1
        self.whole = dict(y=True, x=True)
        self.group = links.group([
            (grad.at[:, aligned(SL * (2 * y + 1 - at.core), SL), :], self.w.rc.at[y], at.sibling) for y in range(2)])

    def view(self, ref, axis, index):
        return ref.at[pl.ds(index, 1)] if axis == "y" else ref.at[:, pl.ds(index, 1)]

    def send(self):
        axis = self.order[self.stage]
        other = 1 - self.at.place[axis]
        current, arriving = getattr(self.w, f"s{self.stage}"), getattr(self.w, f"r{self.stage}")
        self.group = self.links.group([(self.view(current, axis, other), arriving, self.at.peer({axis: other}))])

    def collect(self):
        at, w = self.at, self.w
        self.group.wait()
        if self.stage < 0:
            for y in range(2):
                for t in range(self.taps):
                    mine = self.grad[t, aligned(SL * (2 * y + at.core), SL), :].astype(F32)
                    total = (mine + w.rc[y, t].astype(F32)).astype(BF)
                    for half in range(2):
                        w.s0[y, half, SL * t : SL * t + SL, :] = total[:, 128 * half : 128 * half + 128]
            return
        axis = self.order[self.stage]
        mine = self.view(getattr(w, f"s{self.stage}"), axis, at.place[axis])[...].astype(F32)
        total = mine + getattr(w, f"r{self.stage}")[...].astype(F32)
        getattr(w, f"s{self.stage + 1}")[...] = total.astype(BF)

    def across_teams(self, piece):
        at, w = self.at, self.w
        own = self.links.here(piece, w.rt.at[at.lead])
        group = self.links.group([
            (piece, w.rt.at[at.lead], at.device((at.lead + s) % at.teams * at.team + at.rank))
            for s in range(1, at.teams)])
        own.wait()
        group.wait()
        total = w.rt[0].astype(F32)
        for s in range(1, at.teams):
            total = total + w.rt[s].astype(F32)
        w.pc[...] = total.astype(BF)
        return w.pc

    def share(self, source):
        source = self.across_teams(source) if self.at.teams > 1 else source
        target = self.out.at[:, pl.ds(self.at.place["x"], 1)]
        self.at.results.copy(source, target)
        self.group = self.links.group([(source, target, self.at.peer(dict(x=1 - self.at.place["x"])))])

    def advance(self):
        last = len(self.order) - 1
        if self.stage <= last:
            self.collect()
        if self.stage < last:
            self.stage += 1
            self.send()
        else:
            self.along_z(self.stage - last, getattr(self.w, f"s{last + 1}"))
            self.stage += 1

    def finish(self):
        self.group.wait()


class Chain(Reduction):
    def copy(self, sent, got, src, dst, z):
        w = self.w
        return pltpu.make_async_remote_copy(
            src_ref=src, dst_ref=dst, send_sem=w.cs.at[sent], recv_sem=w.cs.at[2 + got],
            device_id=self.at.peer(dict(z=z)), device_id_type=MESH)

    def along_z(self, step, total):
        w, count = self.w, self.size["z"]
        long, alone = count == 4, count == 1
        if step == 0:
            z = self.at.place["z"]
            self.end = (z == 0) | (z == count - 1)
            self.inner = jnp.logical_not(self.end)
            self.inward = self.copy(0, 0, total, w.c0, jnp.where(z < 2, 1, 2))
            self.swap = self.copy(0, 1, w.c1, w.c2, count - 1 - z)
            self.outward = self.copy(1, 0, w.pc, w.pc, jnp.where(z < 2, 0, 3))
            if long:
                pl.when(self.end)(self.inward.start)
            else:
                w.c1[...] = total[...]
        elif step == 1:
            if long:
                @pl.when(self.inner)
                def _():
                    self.inward.wait_recv()
                    w.c1[...] = (total[...].astype(F32) + w.c0[...].astype(F32)).astype(BF)
                    self.swap.start()
            elif not alone:
                self.swap.start()
        elif step == 2:
            def join():
                self.swap.wait_recv()
                w.pc[...] = (w.c1[...].astype(F32) + w.c2[...].astype(F32)).astype(BF)

            if long:
                @pl.when(self.inner)
                def _():
                    join()
                    self.outward.start()
            elif alone:
                w.pc[...] = w.c1[...]
            else:
                join()
        else:
            if long:
                @pl.when(self.end)
                def _():
                    self.outward.wait_recv()
                    self.inward.wait_send()

                @pl.when(self.inner)
                def _():
                    self.swap.wait_send()
                    self.outward.wait_send()
            elif not alone:
                self.swap.wait_send()
            self.share(w.pc)


class Pairs(Reduction):
    def along_z(self, step, total):
        w, z = self.w, self.at.place["z"]
        partners = [z + 1 - 2 * (z % 2), (z + 2) % 4]
        partners[self.size["z"] // 2 :] = [None] * (2 - self.size["z"] // 2)
        if step == 0:
            self.held = total
        elif partners[step - 1] is not None:
            self.group.wait()
            total = self.held[...].astype(F32) + getattr(w, f"p{step - 1}")[...].astype(F32)
            self.held = getattr(w, f"t{step - 1}")
            self.held[...] = total.astype(BF)
        if step == len(partners):
            self.share(self.held)
        elif partners[step] is not None:
            self.group = self.links.group([
                (self.held, getattr(w, f"p{step}"), self.at.peer(dict(z=partners[step])))])


YX, XY = ("y", "x"), ("x", "y")
ITEMS = {
    "ga0": (4, YX, Chain),
    "gb0": (3, YX, Chain),
    "gb1": (3, YX, Chain),
    "gb2": (3, XY, Chain),
    "gc0": (3, YX, Pairs),
    "gc1": (3, YX, Pairs),
    "gc2": (3, XY, Pairs),
}
SENDS, GROUPS_OF_COPIES = 8, 72
GAINS = ("gain1", "shift1", "gain2", "shift2", "gain3", "shift3")


def mega(n_dp, names, *refs):
    r = SimpleNamespace(**dict(zip(names, refs)))
    team, teams = block_sizes(n_dp)
    dp, chan = lax.axis_index("dp"), lax.axis_index("chan")
    core, y, bit = chan % 2, chan // 2, dp % 2
    sibling, across, corner = (dp, 2 * y + 1 - core), (dp, 2 * (1 - y) + core), (dp, 2 * (1 - y) + 1 - core)
    beside, oblique = (dp + 1 - 2 * bit, chan), (dp + 1 - 2 * bit, 2 * (1 - y) + core)
    quads = (sibling, across, corner)
    rank, lead = dp % team, dp // team
    own_place = dict(y=y, x=bit, z=rank // 2)

    def peer(place):
        place = {**own_place, **place}
        return (lead * team + 2 * place["z"] + place["x"], 2 * place["y"] + core)

    at = SimpleNamespace(core=core, sibling=sibling, team=team, teams=teams, rank=rank, lead=lead, place=own_place,
                         peer=peer, device=lambda p: (p, chan))
    links = Links(r.send, r.recv, r.own, r.idle)
    at.results = links.here_all()

    def others():
        return [(lax.rem(dp + s, n_dp), chan) for s in range(1, n_dp)]

    barrier = pltpu.get_barrier_semaphore()
    for device in quads + (oblique,) + tuple(others()):
        pl.semaphore_signal(barrier, inc=1, device_id=device, device_id_type=MESH)
    load_x, load_ts, load_table = links.here(r.x, r.xl), links.here(r.ts, r.tss), links.here(r.table, r.tab)
    for i, name in enumerate(GAINS):
        pltpu.make_async_copy(getattr(r, name), r.pin.at[i], r.gains).start()
    load_we, load_dy, load_cnt = links.here(r.we, r.wel), links.here(r.dy, r.dyl), links.here(r.cnt, r.cns)
    mine = aligned(SL * chan, SL)
    fill = links.here_all([
        (r.w1, r.w1g.at[:, mine, :]), (r.w2, r.w2g.at[:, mine, :]), (r.we, r.weg.at[:, mine, :]),
        (r.wq, r.wqg.at[0:3, mine, :]), (r.wo, r.wqg.at[3:4, mine, :])])

    def pack(src, dst):
        for k in range(CHAN):
            for half in range(2):
                rows = slice(128 * half, 128 * half + 128)
                both = jnp.concatenate([src[2 * k, rows, :].astype(F32), src[2 * k + 1, rows, :].astype(F32)], axis=1)
                dst[k, rows, :] = both.astype(BF)

    load_x.wait()
    pack(r.xl, r.xp)
    pltpu.make_async_copy(r.pin, r.pin, r.gains).wait()
    r.par[...] = jnp.zeros((8, 128), F32)
    for i in range(len(GAINS)):
        r.par[i : i + 1, 0:SL] = r.pin[i].astype(F32)
    pl.semaphore_wait(barrier, CHAN + n_dp - 1)

    far = SL * (2 * (1 - y) + core)
    low = (dp // 2) % 2
    above = (dp + 2 - 4 * low, chan) if n_dp > 2 else None

    class Share:
        def __init__(self, w, g, parts, later=None):
            self.w, self.g, self.parts = w, g, parts if n_dp > 2 else min(parts, 2)
            self.from_sibling = links.group()
            self.size = SL // self.parts
            self.part = {1: 0, 2: 32 * bit, 4: 32 * low + 16 * bit}[self.parts]
            self.over = links.group()
            start = self.over.plan(
                w.at[:, aligned(self.part, self.size), :], g.at[:, aligned(SL * chan + self.part, self.size), :], across)
            if later is None:
                start()
            else:
                later.append(start)

        def own(self):
            self.from_sibling.remote(self.w, self.g.at[:, mine, :], sibling)

        def piece(self, start, size):
            return self.g.at[:, aligned(far + start, size), :]

        def to_sibling(self, start, size):
            piece = self.piece(start, size)
            self.from_sibling.remote(piece, piece, sibling)

        def relay(self):
            self.over.wait()
            piece = self.piece(self.part, self.size)
            if self.parts > 1:
                self.around = links.group([(piece, piece, beside)])
            if self.parts < 4:
                self.to_sibling(self.part, self.size)

        def relay_up(self):
            if self.parts == 4:
                self.around.wait()
                piece = self.piece(32 * low, 32)
                self.around = links.group([(piece, piece, above)])
                self.to_sibling(32 * low, 32)

        def relay_again(self):
            self.around.wait()
            self.to_sibling(32 - 32 * (low if self.parts == 4 else bit), 32)

        def landed(self):
            self.from_sibling.wait()

    def rows3(ref, row):
        return ref.at[3 * row : 3 * row + 3]

    one = [Share(rows3(r.w1, row), rows3(r.w1g, row), 2 if row == 2 else 4) for row in range(3)]
    for share in one:
        share.own()
    later = []
    two = [Share(rows3(r.w2, row), rows3(r.w2g, row), 4, later) for row in range(2)]
    for share in two:
        share.own()

    load_ts.wait()
    row8 = lax.broadcasted_iota(jnp.int32, (8, 128), 0)
    times = jnp.zeros((8, 128), F32)
    for i in range(8):
        times = jnp.where(row8 == i, r.tss[i].astype(F32), times)
    r.tl[...] = times
    r.ta[dp] = times
    steps = r.table.shape[0]
    load_table.wait()

    def embeddings(times):
        count = times.shape[0]
        wide = jnp.broadcast_to(times[:, 0:1], (count, steps))
        hot = jnp.where(wide == lax.broadcasted_iota(jnp.int32, (count, steps), 1).astype(F32), 1.0, 0.0)
        temb = dot(hot.astype(BF), r.tab[...])
        s = sigmoid(temb)
        return temb, s, (temb * s).astype(BF)

    _, _, tsil = embeddings(jnp.concatenate([times, times], axis=0))
    load_we.wait()
    r.el[...] = jnp.zeros((8, 128), F32)
    r.el[:, 0:SL] = dot_nt(tsil, r.wel[0])[0:8]
    r.eg[chan] = r.el[...]
    moves_x, moves_emb = links.group(), links.group()
    later += [moves_x.plan(r.xp.at[d[1]], r.xg.at[chan], d) for d in quads]
    later += [moves_x.plan(r.par, r.pg.at[chan], d) for d in quads]
    later += [moves_emb.plan(r.el, r.eg.at[chan], d) for d in quads]

    def start_later():
        for start in later:
            start()

    pl.when(core == 0)(start_later)
    r.xg[chan] = r.xp[chan]
    r.pg[chan] = r.par[...]
    at_row = lax.broadcasted_iota(jnp.int32, (C, C), 0) // (C // GROUPS)
    at_col = lax.broadcasted_iota(jnp.int32, (C, C), 1) // (C // GROUPS)
    r.bd[...] = jnp.where(at_row == at_col, 1.0, 0.0).astype(BF)
    for ref in (r.a1, r.a2, r.dd):
        for gap in range(3):
            ref[gap * STEP : gap * STEP + GAP, :] = jnp.zeros((GAP, 3 * C), BF)
    load_dy.wait()
    pack(r.dyl, r.dyp)
    r.dyg[chan] = r.dyp[chan]
    for share in one:
        share.relay()
    pl.when(core == 1)(start_later)
    two.append(Share(rows3(r.w2, 2), rows3(r.w2g, 2), 1))
    two[2].own()
    one[0].relay_up()
    two[0].relay()
    one[1].relay_up()
    out = [Share(r.wq, r.wqg.at[0:3], 1), Share(r.wo, r.wqg.at[3:4], 1)]
    for share in out:
        share.own()
    two[1].relay()
    one[2].relay_again()
    two[0].relay_up()
    moves_dy = links.group([(r.dyp.at[d[1]], r.dyg.at[chan], d) for d in quads])
    mix = Share(r.we, r.weg, 1)
    mix.own()
    moves_late = links.group([(r.tl, r.ta.at[dp], d) for d in others()])
    one[0].relay_again()
    two[1].relay_up()

    bd = r.bd[...]
    moves_x.wait()
    one[1].relay_again()
    for b in range(2):
        first, _ = unpack(r.pg[2 * b], r.pg[2 * b + 1])
        r.pa[:, 128 * b : 128 * b + 128] = first
    par = r.pa[...]
    gain1, shift1, gain2, shift2, gain3, shift3 = [par[i : i + 1] for i in range(6)]

    def spread_out(src, at, dst, scale=None):
        for b in range(2):
            pair = unpack(src[2 * b, pl.ds(at, CH), :].astype(F32), src[2 * b + 1, pl.ds(at, CH), :].astype(F32))
            for m in range(2):
                value = pair[m] if scale is None else pair[m] * scale[m]
                dst[pl.ds(pl.multiple_of(at + m * ROWS, CH), CH), 128 * b : 128 * b + 128] = value.astype(dst.dtype)

    def rows_of(m, at):
        return pl.ds(pl.multiple_of(at + m * ROWS, CH), CH)

    def rows_gap(m, at):
        return pl.ds(pl.multiple_of(at + m * STEP, 16), CH)

    def to_shift(dst):
        def emit(m, at, u):
            write_shift(dst, m, at, u * sigmoid(u), True)
        return emit

    def open_x(m, at):
        if m == 0:
            spread_out(r.xg, at, r.xf)
        return r.xf[rows_of(m, at), :]

    rstd1 = norm_forward(lambda m, at: r.xf[rows_of(m, at), :], r.n1, gain1, shift1, bd, to_shift(r.a1), first=open_x)
    fill.wait()

    for share in one:
        share.landed()
    conv_forward(r.a1, r.w1g, r.h, (0, 1, 2))
    two[0].relay_again()
    moves_emb.wait()
    for b in range(2):
        first, _ = unpack(r.eg[2 * b], r.eg[2 * b + 1])
        r.emb[:, 128 * b : 128 * b + 128] = first
    emb = [r.emb[pl.ds(2 * chan + m, 1), :] for m in range(2)]
    rstd2 = norm_forward(lambda m, at: r.h[rows_gap(m, at), :] + emb[m], r.n2, gain2, shift2, bd, to_shift(r.a2),
                         early=two[2].relay, midway=two[1].relay_again)
    out[0].relay()
    for share in two:
        share.landed()
    conv_forward(r.a2, r.w2g, r.h, (0, 1, 2))
    out[1].relay()

    def load_resid(m, at):
        return r.xf[rows_of(m, at), :]

    def make_resid(m, at):
        value = r.xf[rows_of(m, at), :] + r.h[rows_gap(m, at), :]
        r.xf[rows_of(m, at), :] = value
        return value

    def to_a3(m, at, u):
        r.a3[rows_of(m, at), :] = u.astype(BF)

    rstd3 = norm_forward(load_resid, r.n3, gain3, shift3, bd, to_a3, first=make_resid)
    out[0].landed()
    for j, ref in enumerate((r.q, r.k, r.v)):
        ref[...] = dot_nt(r.a3[...], r.wqg[j]).astype(BF)
    load_cnt.wait()
    count = r.cns[0]
    live = [jnp.where(2 * chan + m < count, 1.0, 0.0).astype(F32) for m in range(2)]
    scale = C ** (-0.5)
    half = [slice(0, ROWS), slice(ROWS, 2 * ROWS)]
    for m in range(2):
        s = dot_nt(r.q[half[m], :], r.k[half[m], :]) * scale
        p = jnp.exp(s - jnp.max(s, axis=1, keepdims=True))
        p = p * (1.0 / jnp.sum(p, axis=1, keepdims=True))
        r.p[half[m], :] = p
        r.pb[half[m], :] = p.astype(BF)
        r.o[half[m], :] = dot(p.astype(BF), r.v[half[m], :]).astype(BF)

    moves_dy.wait()
    out[1].landed()

    def open_dy(i, held):
        spread_out(r.dyg, chunk_at(i), r.g, live)
        return held

    lax.fori_loop(0, ROWS // CH, open_dy, 0)
    for m in range(2):
        r.turn[m] = r.g[half[m], :].T
    r.dqo[3] = (dot(r.turn[0], r.o[half[0], :]) + dot(r.turn[1], r.o[half[1], :])).astype(BF)
    r.do[...] = dot(r.g[...], r.wqg[3]).astype(BF)
    for m in range(2):
        dp_m = dot_nt(r.do[half[m], :], r.v[half[m], :])
        p = r.p[half[m], :]
        ds = (p * (dp_m - jnp.sum(p * dp_m, axis=1, keepdims=True)) * scale).astype(BF)
        r.dv[half[m], :] = dot(r.pb[half[m], :].T, r.do[half[m], :]).astype(BF)
        r.dq[half[m], :] = dot(ds, r.k[half[m], :]).astype(BF)
        r.dk[half[m], :] = dot(ds.T, r.q[half[m], :]).astype(BF)
    for j, ref in enumerate((r.dq, r.dk, r.dv)):
        parts = [dot(ref[half[m], :].T, r.a3[half[m], :]) for m in range(2)]
        r.dqo[j] = (parts[0] + parts[1]).astype(BF)

    items = []

    def reduce(letter, grad):
        start = 0
        for name, (taps, order, kind) in ITEMS.items():
            if name[1] == letter:
                work = SimpleNamespace(**{k[4:]: getattr(r, k) for k in names if k.startswith(name + "_")})
                items.append(kind(at, links, grad.at[start : start + taps], getattr(r, name), work, order))
                start += taps

    def go(*which):
        for i in which:
            items[i].advance()

    reduce("a", r.dqo)
    for m in range(2):
        total = None
        for j, ref in enumerate((r.dq, r.dk, r.dv)):
            part_j = dot(ref[half[m], :], r.wqg[j])
            total = part_j if total is None else total + part_j
        r.h[m * STEP : m * STEP + ROWS, :] = total

    def to_dres(m, at, dv, held):
        value = r.g[rows_of(m, at), :].astype(F32) + dv
        r.dres[rows_of(m, at), :] = value
        write_shift(r.dd, m, at, value, False)
        return held

    passes(norm_back(r.h, r.n3, gain3, shift3, rstd3, bd, False, r.e, 4, to_dres))
    go(0)

    def turn():
        for m in range(2):
            r.turn[m] = r.dd[GAP + STEP * m : GAP + STEP * m + ROWS, C : 2 * C].T

    turn()
    for row in range(3):
        conv_weight(r.a2, r.turn, r.dw2, row)
    reduce("b", r.dw2)
    conv_back(r.dd, r.w2g, r.h)
    mix.relay()

    def to_dh1(m, at, dv, held):
        write_shift(r.dd, m, at, dv, False)
        return held + fold(dv)

    second = norm_back(r.h, r.n2, gain2, shift2, rstd2, bd, True, r.e, 2, to_dh1)
    go(1, 2, 3)
    demb = passes(second, zero_pair())
    for m in range(2):
        r.dm[chan, m : m + 1, :] = col(demb[m]).astype(BF).astype(F32)
    moves_dm = links.group([(r.dm.at[chan], r.dm.at[chan], d) for d in quads])
    turn()
    for row in range(3):
        conv_weight(r.a1, r.turn, r.dw1, row)
    reduce("c", r.dw1)
    r.big[...] = dot_nt(r.o[...], r.wqg[3])

    def pack_out(at, pair, dst):
        for b in range(2):
            even, odd = unpack(*(v[:, 128 * b : 128 * b + 128] for v in pair))
            dst[2 * b, pl.ds(at, CH), :] = even.astype(BF)
            dst[2 * b + 1, pl.ds(at, CH), :] = odd.astype(BF)

    def to_y(i, held):
        at = chunk_at(i)
        pack_out(at, [(load_resid(m, at) + r.big[rows_of(m, at), :]) * live[m] for m in range(2)], r.yp)
        return held

    lax.fori_loop(0, ROWS // CH, to_y, 0)

    def data_one():
        conv_back(r.dd, r.w1g, r.h)

    def norm_one():
        back1 = norm_back(r.h, r.n1, gain1, shift1, rstd1, bd, True, r.e, 0,
                          lambda m, at, dv, held: r.dres[rows_of(m, at), :] + dv)

        def to_maps(i, held):
            at = chunk_at(i)
            pack_out(at, [back1(m, at, 0) for m in range(2)], r.mp)
            return held

        lax.fori_loop(0, ROWS // CH, to_maps, 0)
        moves_dm.wait()
        for j in range(CHAN):
            r.dl[2 * j : 2 * j + 2, :] = r.dm[j, 0:2, :]
        r.ra[dp] = r.dl[...]
        for d in others():
            moves_late.remote(r.dl, r.ra.at[dp], d)
        for b in range(2):
            block = r.e[:, 128 * b : 128 * b + 128]
            r.es[2 * b] = block
            r.es[2 * b + 1] = pltpu.roll(block, SL, 1)
        r.er[chan] = r.es[chan]
        for d in quads:
            moves_e.remote(r.es.at[d[1]], r.er.at[chan], d)

    def send_maps():
        for src, dst in ((r.yp, r.yo), (r.mp, r.mo)):
            at.results.copy(src.at[chan], dst.at[chan])
            for d in quads:
                moves_out.remote(src.at[d[1]], dst.at[chan], d)

    def send_gains():
        moves_e.wait()
        r.et[...] = r.er[0] + r.er[1] + r.er[2] + r.er[3]
        at.results.copy(r.et, r.ext.at[dp])
        for d in others():
            moves_out.remote(r.et, r.ext.at[dp], d)

    def embedding():
        mix.landed()
        moves_late.wait()
        maps = 8 * n_dp
        temb, s, tsil = embeddings(r.ta[...].reshape(maps, 128))
        rows = r.ra[...].reshape(maps, C)
        r.rt[...] = rows.T
        r.dew[...] = dot(r.rt[mine, :].astype(BF), tsil)
        dtemb = dot(rows.astype(BF), r.weg[0]) * (s * (1.0 + temb * (1.0 - s)))
        high = dtemb.astype(BF)
        r.bw[0:maps, :] = high
        r.bw[maps:, :] = (dtemb - high.astype(F32)).astype(BF)
        for src, dst in ((r.dew, r.de), (r.bw, r.both), (r.ta, r.tall)):
            at.results.copy(src, dst)

    moves_e, moves_out = links.group(), links.group()
    go(0)
    data_one()
    go(6, 4, 5, 3, 1)
    norm_one()
    go(2, 0, 4, 6)
    send_maps()
    go(1, 5, 0, 2, 3)
    send_gains()
    go(4, 6, 1, 5, 2, 0, 3)
    embedding()
    go(4, 6, 1, 5, 2, 0, 3, 1, 4, 2, 3, 6, 5)
    for item in items:
        item.finish()
    at.results.wait()
    moves_out.wait()
    links.close()


STORES = ["y", "dm", "de_out", "dq", "do", "d2", "d1", "dt"]


def finish(n_dp, names, *refs):
    r = SimpleNamespace(**dict(zip(names, refs)))
    maps = 8 * n_dp
    steps = r.dt.shape[0]
    links = Links(None, None, r.own, None)
    load = {name: links.here(getattr(r, name), getattr(r, name + "_v"))
            for name in ["yo", "mo", "tall", "both"] + list(ITEMS) + ["de", "ext"]}

    def out(name, src, index=slice(None)):
        dst = getattr(r, name)
        pltpu.make_async_copy(src.at[index], dst.at[index], r.stores.at[STORES.index(name)]).start()

    for name, dst, src, dst_v in (("yo", "y", r.yo_v, r.y_v), ("mo", "dm", r.mo_v, r.dm_v)):
        load[name].wait()
        for j in range(CHAN):
            block = src[j].astype(F32)
            dst_v[2 * j] = block[:, 0:SL].astype(BF)
            dst_v[2 * j + 1] = pltpu.roll(block, SL, 1)[:, 0:SL].astype(BF)
        out(dst, dst_v)
    load["tall"].wait()
    load["both"].wait()
    lanes = r.tall_v[...].reshape(maps, 128).T[0:1, :]
    lanes = jnp.concatenate([lanes, lanes], axis=1)
    for start in range(0, steps, 256):
        size = min(256, steps - start)
        ids = lax.broadcasted_iota(jnp.int32, (size, 2 * maps), 0).astype(F32) + float(start)
        hot = jnp.where(ids == lanes, 1.0, 0.0).astype(BF)
        r.dt_v[start : start + size, :] = dot(hot, r.both_v[...])
        out("dt", r.dt_v, slice(start, start + size))

    def whole(name, dst_v, base, taps):
        src = getattr(r, name + "_v")
        for i, t in enumerate(taps):
            for half in range(2):
                dst_v[base + i, :, 128 * half : 128 * half + 128] = src[0, half, SL * t : SL * t + SL, :].astype(F32)

    done = dict(b=0, c=0)
    for name, (taps, _, _) in ITEMS.items():
        load[name].wait()
        if name[1] == "a":
            whole(name, r.dq_v, 0, range(3))
            out("dq", r.dq_v)
            whole(name, r.do_v, 0, [3])
            out("do", r.do_v)
        else:
            key, start = dict(b="d2", c="d1")[name[1]], done[name[1]]
            dst_v = getattr(r, key + "_v")
            whole(name, dst_v, start, range(taps))
            out(key, dst_v, slice(start, start + taps))
            done[name[1]] += taps
    load["de"].wait()
    out("de_out", r.de_v)
    load["ext"].wait()
    total = r.ext_v[0]
    for i in range(1, n_dp):
        total = total + r.ext_v[i]
    for i in range(6):
        r.gains_v[i] = total[i : i + 1, 0:SL]
        pltpu.make_async_copy(r.gains_v.at[i], getattr(r, f"e{i}"), r.stores.at[len(STORES)]).start()
    for at, name in enumerate(STORES):
        src = r.de_v if name == "de_out" else getattr(r, name + "_v")
        pltpu.make_async_copy(src, getattr(r, name), r.stores.at[at]).wait()
    pltpu.make_async_copy(r.gains_v, r.gains_v, r.stores.at[len(STORES)]).wait()


def per_device(x_maps, timesteps, counts, emb_table, w_first, w_second, w_embed, w_qkv, w_out, gain_one, shift_one,
               gain_two, shift_two, gain_three, shift_three, cotangent, *, n_dp):
    team, teams = block_sizes(n_dp)
    slots, side, _, _ = x_maps.shape
    emb = w_embed.shape[0]
    steps = emb_table.shape[0]
    inputs = dict(
        x=x_maps.reshape(slots, side * side, SL), dy=cotangent.reshape(slots, side * side, SL),
        ts=timesteps, cnt=counts, table=emb_table,
        w1=jnp.swapaxes(w_first, 2, 3).reshape(9, SL, C), w2=jnp.swapaxes(w_second, 2, 3).reshape(9, SL, C),
        we=w_embed.T[None], wq=jnp.transpose(w_qkv, (1, 2, 0)), wo=w_out.T[None])
    gains = (gain_one, shift_one, gain_two, shift_two, gain_three, shift_three)
    inputs.update({name: v.reshape(1, SL) for name, v in zip(GAINS, gains)})
    anywhere = pl.BlockSpec(memory_space=pl.ANY)

    def of(shape, dtype):
        return jax.ShapeDtypeStruct(shape, dtype)

    maps = 8 * n_dp
    middle = dict(
        yo=of((CHAN, ROWS, 128), BF), mo=of((CHAN, ROWS, 128), BF), tall=of((n_dp, 8, 128), F32),
        ext=of((n_dp, 8, 128), F32), both=of((2 * maps, emb), BF), de=of((SL, emb), F32))
    middle.update({name: of((1, 2, SL * item[0], 128), BF) for name, item in ITEMS.items()})
    v = pltpu.VMEM
    maps2 = 2 * ROWS
    scratch = dict(
        xl=v((slots, ROWS, SL), BF), dyl=v((slots, ROWS, SL), BF), pin=v((len(GAINS), 1, SL), BF),
        tss=pltpu.SMEM((slots,), jnp.int32), cns=pltpu.SMEM((1,), jnp.int32), tab=v((steps, emb), BF),
        xp=v((CHAN, ROWS, 128), BF), dyp=v((CHAN, ROWS, 128), BF),
        xg=v((CHAN, ROWS, 128), BF), dyg=v((CHAN, ROWS, 128), BF),
        yp=v((CHAN, ROWS, 128), BF), mp=v((CHAN, ROWS, 128), BF),
        w1g=v((9, C, C), BF), w2g=v((9, C, C), BF), weg=v((1, C, emb), BF), wqg=v((4, C, C), BF),
        bd=v((C, C), BF), tl=v((8, 128), F32), ta=v((n_dp, 8, 128), F32), par=v((8, 128), F32),
        pg=v((CHAN, 8, 128), F32), pa=v((8, C), F32), emb=v((8, C), F32),
        wel=v((1, SL, emb), BF), el=v((8, 128), F32), eg=v((CHAN, 8, 128), F32),
        a1=v((TALL + 2 * GAP, 3 * C), BF), a2=v((TALL + 2 * GAP, 3 * C), BF), dd=v((TALL + 2 * GAP, 3 * C), BF),
        h=v((TALL, C), F32), xf=v((maps2, C), F32), n1=v((maps2, C), F32), n2=v((maps2, C), F32),
        n3=v((maps2, C), F32), dres=v((maps2, C), F32), big=v((maps2, C), F32), p=v((maps2, C), F32),
        e=v((8, C), F32), es=v((CHAN, 8, 128), F32), er=v((CHAN, 8, 128), F32), et=v((8, 128), F32),
        dm=v((CHAN, 8, C), F32), dl=v((8, C), F32), ra=v((n_dp, 8, C), F32), rt=v((C, maps), F32),
        dew=v((SL, emb), F32), bw=v((2 * maps, emb), BF), turn=v((2, ROWS, C), BF),
        dw1=v((9, C, C), BF), dw2=v((9, C, C), BF), dqo=v((4, C, C), BF))
    for name in ("a3", "q", "k", "v", "pb", "o", "g", "do", "dq", "dk", "dv"):
        scratch[name] = v((maps2, C), BF)
    for name, (taps, order, kind) in ITEMS.items():
        buffers = reduction_scratch(taps, order, kind, teams)
        scratch.update({name + "_" + k: b for k, b in buffers.items()})
    several = len(ITEMS) if teams > 1 else 0
    scratch.update(
        idle=v((4096, 128), BF), send=pltpu.SemaphoreType.DMA((SENDS + several,)),
        recv=pltpu.SemaphoreType.DMA((GROUPS_OF_COPIES + several,)), own=pltpu.SemaphoreType.DMA((9 + several,)),
        gains=pltpu.SemaphoreType.DMA(()))
    got = pl.pallas_call(
        functools.partial(mega, n_dp, list(inputs) + list(middle) + list(scratch)),
        out_shape=tuple(middle.values()),
        in_specs=[anywhere] * len(inputs),
        out_specs=(anywhere,) * len(middle),
        scratch_shapes=list(scratch.values()),
        compiler_params=pltpu.CompilerParams(collective_id=0, has_side_effects=True, vmem_limit_bytes=60 << 20),
        name="blocks",
    )(*inputs.values())
    results = dict(
        y=of((slots, ROWS, SL), BF), dm=of((slots, ROWS, SL), BF), dt=of((steps, emb), F32), d1=of((9, SL, C), F32),
        d2=of((9, SL, C), F32), de_out=of((SL, emb), F32), dq=of((3, SL, C), F32), do=of((1, SL, C), F32))
    results.update({f"e{i}": of((1, SL), F32) for i in range(6)})
    scratch = {name + "_v": v(o.shape, o.dtype) for name, o in middle.items()}
    scratch.update({name + "_v": v(o.shape, o.dtype) for name, o in results.items() if name[0] != "e"})
    scratch.update(
        gains_v=v((6, 1, SL), F32), own=pltpu.SemaphoreType.DMA((len(middle),)),
        stores=pltpu.SemaphoreType.DMA((len(STORES) + 1,)))
    got = pl.pallas_call(
        functools.partial(finish, n_dp, list(middle) + list(results) + list(scratch)),
        out_shape=tuple(results.values()),
        in_specs=[anywhere] * len(middle),
        out_specs=(anywhere,) * len(results),
        scratch_shapes=list(scratch.values()),
        compiler_params=pltpu.CompilerParams(vmem_limit_bytes=60 << 20),
        name="finish",
    )(*got)
    got = dict(zip(results, got))
    return (
        got["y"].reshape(x_maps.shape), got["dm"].reshape(x_maps.shape), got["dt"],
        jnp.swapaxes(got["d1"].reshape(3, 3, SL, C), 2, 3), jnp.swapaxes(got["d2"].reshape(3, 3, SL, C), 2, 3),
        got["de_out"].T, jnp.transpose(got["dq"], (2, 0, 1)), got["do"].reshape(SL, C).T,
    ) + tuple(got[f"e{i}"].reshape(SL) for i in range(6))


def solution(mesh):
    weights = (P(None, None, None, "chan"), P(None, None, None, "chan"), P(None, "chan"), P(None, None, "chan"),
               P(None, "chan")) + (P("chan"),) * 6
    maps = P("dp", None, None, "chan")
    return jax.shard_map(
        functools.partial(per_device, n_dp=mesh.shape["dp"]), mesh=mesh,
        in_specs=(maps, P("dp"), P("dp"), P()) + weights + (maps,),
        out_specs=(maps, maps, P()) + weights, check_vma=False)
```

```python
import functools
from types import SimpleNamespace

import jax
import jax.numpy as jnp
from jax import lax
from jax.experimental import pallas as pl
from jax.experimental.pallas import tpu as pltpu
from jax.sharding import PartitionSpec as P

F32 = jnp.float32
BF = jnp.bfloat16
MESH = pl.DeviceIdType.MESH
EPS = 1e-06
GROUPS = 32
CHAN = 4
ROWS = 256
C = 256
SL = C // CHAN
GAP = 16
STEP = ROWS + GAP
TALL = 2 * ROWS + GAP
CH = 128
COUNT = ROWS * (C // GROUPS)


def dot(a, b):
    return jnp.dot(a, b, preferred_element_type=F32)


def dot_nt(a, b):
    return lax.dot_general(a, b, (((1,), (1,)), ((), ())), preferred_element_type=F32)


def sigmoid(u):
    return 0.5 * jnp.tanh(0.5 * u) + 0.5


def fold(v):
    return v.reshape(v.shape[0] // 8, 8, v.shape[1]).sum(axis=0)


def group_total(rows, bd):
    at = lax.broadcasted_iota(jnp.int32, (8, C), 0)
    stack = jnp.zeros((8, C), F32)
    for i, row in enumerate(rows):
        stack = jnp.where(at == i, row, stack)
    high = stack.astype(BF).astype(F32)
    rest = stack - high
    mid = rest.astype(BF).astype(F32)
    parts = jnp.concatenate([high, mid, rest - mid, jnp.zeros((8, C), F32)], axis=0)
    total = dot(parts.astype(BF), bd)
    total = total[0:8] + total[8:16] + total[16:24]
    return [total[i : i + 1] for i in range(len(rows))]


def chunk_at(i):
    return pl.multiple_of(i * CH, CH)


def passes(body, carry=None):
    carry = (0, 0) if carry is None else carry

    def step(i, held):
        return tuple(body(m, chunk_at(i), held[m]) for m in range(2))

    return lax.fori_loop(0, ROWS // CH, step, carry)


def zero_pair():
    return (jnp.zeros((8, C), F32), jnp.zeros((8, C), F32))


def col(v):
    return jnp.sum(v, axis=0, keepdims=True)


def write_shift(dst, m, at, value, forward):
    place = lax.broadcasted_iota(jnp.int32, (CH, C), 0) % 16
    before = jnp.where(place == 0, 0.0, pltpu.roll(value, 1, 0))
    after = jnp.where(place == 15, 0.0, pltpu.roll(value, CH - 1, 0))
    first, last = (before, after) if forward else (after, before)
    rows = pl.ds(pl.multiple_of(at + (GAP + m * STEP), 16), CH)
    dst[rows, 0:C] = first.astype(BF)
    dst[rows, C : 2 * C] = value.astype(BF)
    dst[rows, 2 * C : 3 * C] = last.astype(BF)


def norm_forward(load, n_ref, gain, shift, bd, emit, first=None, early=None, midway=None):
    sums = []
    for at in range(0, ROWS, CH):
        for m in range(2):
            value = (first or load)(m, at)
            if at == 0:
                near = col(value[0:32]) * (1.0 / 32)
                sums.append([near, zero_pair()[0], zero_pair()[0]])
            d = value - sums[m][0]
            sums[m][1] = sums[m][1] + fold(d)
            sums[m][2] = sums[m][2] + fold(d * d)
    if early is not None:
        early()
    ones = [col(t[1]) for t in sums]
    middle = [t[0] + one * (1.0 / ROWS) for t, one in zip(sums, ones)]
    mean = [v * (GROUPS / C) for v in group_total(middle, bd)]
    spread = [
        col(t[2]) - one * one * (1.0 / ROWS) + ROWS * (mid - mu) * (mid - mu)
        for t, one, mid, mu in zip(sums, ones, middle, mean)]
    rstd = [lax.rsqrt(v * (1.0 / COUNT) + EPS) for v in group_total(spread, bd)]
    if midway is not None:
        midway()

    def last(m, at, held):
        n = (load(m, at) - mean[m]) * rstd[m]
        n_ref[pl.ds(pl.multiple_of(at + m * ROWS, CH), CH), :] = n
        emit(m, at, n * gain + shift)
        return held

    passes(last)
    return rstd


def norm_back(d_ref, n_ref, gain, shift, rstd, bd, active, e_ref, e_at, emit):
    def rows(m, at):
        return pl.ds(pl.multiple_of(at + m * STEP, 16), CH)

    def first(m, at, held):
        d = d_ref[rows(m, at), :]
        n = n_ref[pl.ds(pl.multiple_of(at + m * ROWS, CH), CH), :]
        if active:
            u = n * gain + shift
            s = sigmoid(u)
            d = d * (s * (1.0 + u * (1.0 - s)))
            d_ref[rows(m, at), :] = d
        return (held[0] + fold(d), held[1] + fold(d * n))

    total = passes(first, (zero_pair(), zero_pair()))
    ones = [col(t[0]) for t in total]
    twos = [col(t[1]) for t in total]
    e_ref[e_at : e_at + 1, :] = twos[0] + twos[1]
    e_ref[e_at + 1 : e_at + 2, :] = ones[0] + ones[1]
    means = group_total([gain * v for v in ones + twos], bd)
    means = [v * (1.0 / COUNT) for v in means]

    def second(m, at, held):
        d = d_ref[rows(m, at), :]
        n = n_ref[pl.ds(pl.multiple_of(at + m * ROWS, CH), CH), :]
        return emit(m, at, rstd[m] * (d * gain - means[m] - n * means[2 + m]), held)

    return second


def unpack(low, high):
    lane = lax.broadcasted_iota(jnp.int32, low.shape, 1)
    first = jnp.where(lane < SL, low, pltpu.roll(high, SL, 1))
    second = jnp.where(lane < SL, pltpu.roll(low, SL, 1), high)
    return first, second


BLOCKS = ((0, STEP), (STEP, ROWS))


def conv_forward(a_ref, w_ref, h_ref, rows):
    for start, size in BLOCKS:
        total = None
        for row in rows:
            for c in range(3):
                at = 16 * row + start
                part = dot_nt(a_ref[at : at + size, C * c : C * c + C], w_ref[3 * row + c])
                total = part if total is None else total + part
        h_ref[start : start + size, :] = total


def conv_back(d_ref, w_ref, h_ref):
    for start, size in BLOCKS:
        total = None
        for row in range(3):
            at = 16 * (2 - row) + start
            part = dot(d_ref[at : at + size, :], w_ref[3 * row : 3 * row + 3].reshape(3 * C, C))
            total = part if total is None else total + part
        h_ref[start : start + size, :] = total


def conv_weight(a_ref, turned, dw_ref, row):
    for c in range(3):
        total = None
        for m in range(2):
            at = 16 * row + STEP * m
            part = dot(turned[m], a_ref[at : at + ROWS, C * c : C * c + C])
            total = part if total is None else total + part
        dw_ref[3 * row + c] = total.astype(BF)


class Group:
    def __init__(self, links):
        self.links, self.at, self.rows = links, links.used, 0
        links.used += 1

    def remote(self, src, dst, device):
        self.plan(src, dst, device)()

    def plan(self, src, dst, device):
        links, rows = self.links, rows_in(src)
        if links.sending + rows > links.idle.shape[0]:
            links.ended.append((links.senders, links.sending))
            links.senders, links.sending = links.senders + 1, 0
        links.sending += rows
        self.rows += rows
        sender = links.send.at[links.senders]
        return lambda: pltpu.make_async_remote_copy(
            src_ref=src, dst_ref=dst, send_sem=sender, recv_sem=links.recv.at[self.at],
            device_id=device, device_id_type=MESH).start()

    def wait(self):
        self.links.wait_rows(self.links.recv.at[self.at], self.rows)


class LocalGroup:
    def __init__(self, links):
        self.links, self.at, self.rows = links, links.local, 0
        links.local += 1

    def copy(self, src, dst):
        self.rows += rows_in(src)
        pltpu.make_async_copy(src, dst, self.links.own.at[self.at]).start()

    def wait(self):
        self.links.wait_rows(self.links.own.at[self.at], self.rows)


def rows_in(ref):
    size = ref.dtype.itemsize
    for n in ref.shape:
        size *= n
    return size // 256


class Links:
    def __init__(self, send, recv, own, idle):
        self.send, self.recv, self.own, self.idle = send, recv, own, idle
        self.used, self.local, self.senders, self.sending = 0, 0, 0, 0
        self.ended = []

    def wait_rows(self, semaphore, rows):
        view = self.idle.at[0:rows]
        pltpu.make_async_copy(view, view, semaphore).wait()

    def group(self, copies=()):
        group = Group(self)
        for src, dst, device in copies:
            group.remote(src, dst, device)
        return group

    def here(self, src, dst):
        copy = pltpu.make_async_copy(src, dst, self.own.at[self.local])
        self.local += 1
        copy.start()
        return copy

    def here_all(self, copies=()):
        group = LocalGroup(self)
        for src, dst in copies:
            group.copy(src, dst)
        return group

    def close(self):
        for at, rows in self.ended + [(self.senders, self.sending)]:
            self.wait_rows(self.send.at[at], rows)


def block_sizes(n_dp):
    team = min(8, n_dp)
    return team, n_dp // team


def aligned(start, size):
    return pl.ds(pl.multiple_of(start, size), size)


def reduction_scratch(taps, order, kind, teams):
    rows = SL * taps
    part = (1, 1, rows, 128)
    shapes = dict(rc=(2, taps, SL, C), s0=(2, 2, rows, 128), pc=part, sum=part, rt=(teams,) + part)
    shapes.update({name: part for name in ("c0", "c1", "c2", "p0", "p1", "t0", "t1")})
    size = dict(y=2, x=2)
    for k, axis in enumerate(order):
        size[axis] = 1
        shapes[f"r{k}"] = shapes[f"s{k + 1}"] = (size["y"], size["x"], rows, 128)
    buffers = {name: pltpu.VMEM(shape, BF) for name, shape in shapes.items()}
    if kind is Chain:
        buffers.update(cs=pltpu.SemaphoreType.DMA((4,)))
    return buffers


class Reduction:
    def __init__(self, at, links, grad, out, work, order):
        self.at, self.links, self.grad, self.out, self.w, self.order = at, links, grad, out, work, order
        self.taps = grad.shape[0]
        self.size = dict(y=2, x=2, z=at.team // 2)
        self.stage = -1
        self.whole = dict(y=True, x=True)
        self.group = links.group([
            (grad.at[:, aligned(SL * (2 * y + 1 - at.core), SL), :], self.w.rc.at[y], at.sibling) for y in range(2)])

    def view(self, ref, axis, index):
        return ref.at[pl.ds(index, 1)] if axis == "y" else ref.at[:, pl.ds(index, 1)]

    def send(self):
        axis = self.order[self.stage]
        other = 1 - self.at.place[axis]
        current, arriving = getattr(self.w, f"s{self.stage}"), getattr(self.w, f"r{self.stage}")
        self.group = self.links.group([(self.view(current, axis, other), arriving, self.at.peer({axis: other}))])

    def collect(self):
        at, w = self.at, self.w
        self.group.wait()
        if self.stage < 0:
            for y in range(2):
                for t in range(self.taps):
                    mine = self.grad[t, aligned(SL * (2 * y + at.core), SL), :].astype(F32)
                    total = (mine + w.rc[y, t].astype(F32)).astype(BF)
                    for half in range(2):
                        w.s0[y, half, SL * t : SL * t + SL, :] = total[:, 128 * half : 128 * half + 128]
            return
        axis = self.order[self.stage]
        mine = self.view(getattr(w, f"s{self.stage}"), axis, at.place[axis])[...].astype(F32)
        total = mine + getattr(w, f"r{self.stage}")[...].astype(F32)
        getattr(w, f"s{self.stage + 1}")[...] = total.astype(BF)

    def across_teams(self, piece):
        at, w = self.at, self.w
        own = self.links.here(piece, w.rt.at[at.lead])
        group = self.links.group([
            (piece, w.rt.at[at.lead], at.device((at.lead + s) % at.teams * at.team + at.rank))
            for s in range(1, at.teams)])
        own.wait()
        group.wait()
        total = w.rt[0].astype(F32)
        for s in range(1, at.teams):
            total = total + w.rt[s].astype(F32)
        w.sum[...] = total.astype(BF)
        return w.sum

    def share(self, source):
        source = self.across_teams(source) if self.at.teams > 1 else source
        target = self.out.at[:, pl.ds(self.at.place["x"], 1)]
        self.at.results.copy(source, target)
        self.group = self.links.group([(source, target, self.at.peer(dict(x=1 - self.at.place["x"])))])

    def advance(self):
        last = len(self.order) - 1
        if self.stage <= last:
            self.collect()
        if self.stage < last:
            self.stage += 1
            self.send()
        else:
            self.along_z(self.stage - last, getattr(self.w, f"s{last + 1}"))
            self.stage += 1

    def finish(self):
        self.group.wait()


class Chain(Reduction):
    def copy(self, sent, got, src, dst, z):
        w = self.w
        return pltpu.make_async_remote_copy(
            src_ref=src, dst_ref=dst, send_sem=w.cs.at[sent], recv_sem=w.cs.at[2 + got],
            device_id=self.at.peer(dict(z=z)), device_id_type=MESH)

    def along_z(self, step, total):
        w, count = self.w, self.size["z"]
        long, alone = count == 4, count == 1
        if step == 0:
            z = self.at.place["z"]
            self.end = (z == 0) | (z == count - 1)
            self.inner = jnp.logical_not(self.end)
            self.inward = self.copy(0, 0, total, w.c0, jnp.where(z < 2, 1, 2))
            self.swap = self.copy(0, 1, w.c1, w.c2, count - 1 - z)
            self.outward = self.copy(1, 0, w.pc, w.pc, jnp.where(z < 2, 0, 3))
            if long:
                pl.when(self.end)(self.inward.start)
            else:
                w.c1[...] = total[...]
        elif step == 1:
            if long:
                @pl.when(self.inner)
                def _():
                    self.inward.wait_recv()
                    w.c1[...] = (total[...].astype(F32) + w.c0[...].astype(F32)).astype(BF)
                    self.swap.start()
            elif not alone:
                self.swap.start()
        elif step == 2:
            def join():
                self.swap.wait_recv()
                w.pc[...] = (w.c1[...].astype(F32) + w.c2[...].astype(F32)).astype(BF)

            if long:
                @pl.when(self.inner)
                def _():
                    join()
                    self.outward.start()
            elif alone:
                w.pc[...] = w.c1[...]
            else:
                join()
        else:
            if long:
                @pl.when(self.end)
                def _():
                    self.outward.wait_recv()
                    self.inward.wait_send()

                @pl.when(self.inner)
                def _():
                    self.swap.wait_send()
                    self.outward.wait_send()
            elif not alone:
                self.swap.wait_send()
            self.share(w.pc)


class Pairs(Reduction):
    def along_z(self, step, total):
        w, z = self.w, self.at.place["z"]
        partners = [z + 1 - 2 * (z % 2), (z + 2) % 4]
        partners[self.size["z"] // 2 :] = [None] * (2 - self.size["z"] // 2)
        if step == 0:
            self.held = total
        elif partners[step - 1] is not None:
            self.group.wait()
            total = self.held[...].astype(F32) + getattr(w, f"p{step - 1}")[...].astype(F32)
            self.held = getattr(w, f"t{step - 1}")
            self.held[...] = total.astype(BF)
        if step == len(partners):
            self.share(self.held)
        elif partners[step] is not None:
            self.group = self.links.group([
                (self.held, getattr(w, f"p{step}"), self.at.peer(dict(z=partners[step])))])


YX, XY = ("y", "x"), ("x", "y")
ITEMS = {
    "ga0": (4, YX, Chain),
    "gb0": (3, YX, Chain),
    "gb1": (3, YX, Chain),
    "gb2": (3, XY, Chain),
    "gc0": (3, YX, Pairs),
    "gc1": (3, YX, Pairs),
    "gc2": (3, XY, Pairs),
}
SENDS, GROUPS_OF_COPIES = 8, 72
GAINS = ("gain1", "shift1", "gain2", "shift2", "gain3", "shift3")


def mega(n_dp, names, *refs):
    r = SimpleNamespace(**dict(zip(names, refs)))
    team, teams = block_sizes(n_dp)
    dp, chan = lax.axis_index("dp"), lax.axis_index("chan")
    core, y, bit = chan % 2, chan // 2, dp % 2
    sibling, across, corner = (dp, 2 * y + 1 - core), (dp, 2 * (1 - y) + core), (dp, 2 * (1 - y) + 1 - core)
    beside, oblique = (dp + 1 - 2 * bit, chan), (dp + 1 - 2 * bit, 2 * (1 - y) + core)
    quads = (sibling, across, corner)
    rank, lead = dp % team, dp // team
    own_place = dict(y=y, x=bit, z=rank // 2)

    def peer(place):
        place = {**own_place, **place}
        return (lead * team + 2 * place["z"] + place["x"], 2 * place["y"] + core)

    at = SimpleNamespace(core=core, sibling=sibling, team=team, teams=teams, rank=rank, lead=lead, place=own_place,
                         peer=peer, device=lambda p: (p, chan))
    links = Links(r.send, r.recv, r.own, r.idle)
    at.results = links.here_all()

    def others():
        return [(lax.rem(dp + s, n_dp), chan) for s in range(1, n_dp)]

    barrier = pltpu.get_barrier_semaphore()
    for device in quads + (oblique,) + tuple(others()):
        pl.semaphore_signal(barrier, inc=1, device_id=device, device_id_type=MESH)
    load_x, load_ts, load_table = links.here(r.x, r.xl), links.here(r.ts, r.tss), links.here(r.table, r.tab)
    for i, name in enumerate(GAINS):
        pltpu.make_async_copy(getattr(r, name), r.pin.at[i], r.gains).start()
    load_we, load_dy, load_cnt = links.here(r.we, r.wel), links.here(r.dy, r.dyl), links.here(r.cnt, r.cns)
    mine = aligned(SL * chan, SL)
    fill = links.here_all([
        (r.w1, r.w1g.at[:, mine, :]), (r.w2, r.w2g.at[:, mine, :]), (r.we, r.weg.at[:, mine, :]),
        (r.wq, r.wqg.at[0:3, mine, :]), (r.wo, r.wqg.at[3:4, mine, :])])

    def pack(src, dst):
        for k in range(CHAN):
            for half in range(2):
                rows = slice(128 * half, 128 * half + 128)
                both = jnp.concatenate([src[2 * k, rows, :].astype(F32), src[2 * k + 1, rows, :].astype(F32)], axis=1)
                dst[k, rows, :] = both.astype(BF)

    load_x.wait()
    pack(r.xl, r.xp)
    pltpu.make_async_copy(r.pin, r.pin, r.gains).wait()
    r.par[...] = jnp.zeros((8, 128), F32)
    for i in range(len(GAINS)):
        r.par[i : i + 1, 0:SL] = r.pin[i].astype(F32)
    pl.semaphore_wait(barrier, CHAN + n_dp - 1)

    far = SL * (2 * (1 - y) + core)
    low = (dp // 2) % 2
    above = (dp + 2 - 4 * low, chan) if n_dp > 2 else None

    class Share:
        def __init__(self, w, g, parts, later=None):
            self.w, self.g, self.parts = w, g, parts if n_dp > 2 else min(parts, 2)
            self.from_sibling = links.group()
            self.size = SL // self.parts
            self.part = {1: 0, 2: 32 * bit, 4: 32 * low + 16 * bit}[self.parts]
            self.over = links.group()
            start = self.over.plan(
                w.at[:, aligned(self.part, self.size), :], g.at[:, aligned(SL * chan + self.part, self.size), :], across)
            if later is None:
                start()
            else:
                later.append(start)

        def own(self):
            self.from_sibling.remote(self.w, self.g.at[:, mine, :], sibling)

        def piece(self, start, size):
            return self.g.at[:, aligned(far + start, size), :]

        def to_sibling(self, start, size):
            piece = self.piece(start, size)
            self.from_sibling.remote(piece, piece, sibling)

        def relay(self):
            self.over.wait()
            piece = self.piece(self.part, self.size)
            if self.parts > 1:
                self.around = links.group([(piece, piece, beside)])
            if self.parts < 4:
                self.to_sibling(self.part, self.size)

        def relay_up(self):
            if self.parts == 4:
                self.around.wait()
                piece = self.piece(32 * low, 32)
                self.around = links.group([(piece, piece, above)])
                self.to_sibling(32 * low, 32)

        def relay_again(self):
            self.around.wait()
            self.to_sibling(32 - 32 * (low if self.parts == 4 else bit), 32)

        def landed(self):
            self.from_sibling.wait()

    def rows3(ref, row):
        return ref.at[3 * row : 3 * row + 3]

    one = [Share(rows3(r.w1, row), rows3(r.w1g, row), 2 if row == 2 else 4) for row in range(3)]
    for share in one:
        share.own()
    later = []
    two = [Share(rows3(r.w2, row), rows3(r.w2g, row), 4, later) for row in range(2)]
    for share in two:
        share.own()

    load_ts.wait()
    row8 = lax.broadcasted_iota(jnp.int32, (8, 128), 0)
    times = jnp.zeros((8, 128), F32)
    for i in range(8):
        times = jnp.where(row8 == i, r.tss[i].astype(F32), times)
    r.tl[...] = times
    r.ta[dp] = times
    steps = r.table.shape[0]
    load_table.wait()

    def embeddings(times):
        count = times.shape[0]
        wide = jnp.broadcast_to(times[:, 0:1], (count, steps))
        hot = jnp.where(wide == lax.broadcasted_iota(jnp.int32, (count, steps), 1).astype(F32), 1.0, 0.0)
        temb = dot(hot.astype(BF), r.tab[...])
        s = sigmoid(temb)
        return temb, s, (temb * s).astype(BF)

    _, _, tsil = embeddings(jnp.concatenate([times, times], axis=0))
    load_we.wait()
    r.el[...] = jnp.zeros((8, 128), F32)
    r.el[:, 0:SL] = dot_nt(tsil, r.wel[0])[0:8]
    r.eg[chan] = r.el[...]
    moves_x, moves_emb = links.group(), links.group()
    later += [moves_x.plan(r.xp.at[d[1]], r.xg.at[chan], d) for d in quads]
    later += [moves_x.plan(r.par, r.pg.at[chan], d) for d in quads]
    later += [moves_emb.plan(r.el, r.eg.at[chan], d) for d in quads]

    def start_later():
        for start in later:
            start()

    pl.when(core == 0)(start_later)
    r.xg[chan] = r.xp[chan]
    r.pg[chan] = r.par[...]
    at_row = lax.broadcasted_iota(jnp.int32, (C, C), 0) // (C // GROUPS)
    at_col = lax.broadcasted_iota(jnp.int32, (C, C), 1) // (C // GROUPS)
    r.bd[...] = jnp.where(at_row == at_col, 1.0, 0.0).astype(BF)
    for ref in (r.a1, r.a2, r.dd):
        for gap in range(3):
            ref[gap * STEP : gap * STEP + GAP, :] = jnp.zeros((GAP, 3 * C), BF)
    load_dy.wait()
    pack(r.dyl, r.dyp)
    r.dyg[chan] = r.dyp[chan]
    for share in one:
        share.relay()
    pl.when(core == 1)(start_later)
    two.append(Share(rows3(r.w2, 2), rows3(r.w2g, 2), 1))
    two[2].own()
    one[0].relay_up()
    two[0].relay()
    one[1].relay_up()
    out = [Share(r.wq, r.wqg.at[0:3], 1), Share(r.wo, r.wqg.at[3:4], 1)]
    for share in out:
        share.own()
    two[1].relay()
    one[2].relay_again()
    two[0].relay_up()
    moves_dy = links.group([(r.dyp.at[d[1]], r.dyg.at[chan], d) for d in quads])
    mix = Share(r.we, r.weg, 1)
    mix.own()
    moves_late = links.group([(r.tl, r.ta.at[dp], d) for d in others()])
    one[0].relay_again()
    two[1].relay_up()

    bd = r.bd[...]
    moves_x.wait()
    one[1].relay_again()
    for b in range(2):
        first, _ = unpack(r.pg[2 * b], r.pg[2 * b + 1])
        r.pa[:, 128 * b : 128 * b + 128] = first
    par = r.pa[...]
    gain1, shift1, gain2, shift2, gain3, shift3 = [par[i : i + 1] for i in range(6)]

    def spread_out(src, at, dst, scale=None):
        for b in range(2):
            pair = unpack(src[2 * b, pl.ds(at, CH), :].astype(F32), src[2 * b + 1, pl.ds(at, CH), :].astype(F32))
            for m in range(2):
                value = pair[m] if scale is None else pair[m] * scale[m]
                dst[pl.ds(pl.multiple_of(at + m * ROWS, CH), CH), 128 * b : 128 * b + 128] = value.astype(dst.dtype)

    def rows_of(m, at):
        return pl.ds(pl.multiple_of(at + m * ROWS, CH), CH)

    def rows_gap(m, at):
        return pl.ds(pl.multiple_of(at + m * STEP, 16), CH)

    def to_shift(dst):
        def emit(m, at, u):
            write_shift(dst, m, at, u * sigmoid(u), True)
        return emit

    def open_x(m, at):
        if m == 0:
            spread_out(r.xg, at, r.xf)
        return r.xf[rows_of(m, at), :]

    rstd1 = norm_forward(lambda m, at: r.xf[rows_of(m, at), :], r.n1, gain1, shift1, bd, to_shift(r.a1), first=open_x)
    fill.wait()

    for share in one:
        share.landed()
    conv_forward(r.a1, r.w1g, r.h, (0, 1, 2))
    two[0].relay_again()
    moves_emb.wait()
    for b in range(2):
        first, _ = unpack(r.eg[2 * b], r.eg[2 * b + 1])
        r.emb[:, 128 * b : 128 * b + 128] = first
    emb = [r.emb[pl.ds(2 * chan + m, 1), :] for m in range(2)]
    rstd2 = norm_forward(lambda m, at: r.h[rows_gap(m, at), :] + emb[m], r.n2, gain2, shift2, bd, to_shift(r.a2),
                         early=two[2].relay, midway=two[1].relay_again)
    out[0].relay()
    for share in two:
        share.landed()
    conv_forward(r.a2, r.w2g, r.h, (0, 1, 2))
    out[1].relay()

    def load_resid(m, at):
        return r.xf[rows_of(m, at), :]

    def make_resid(m, at):
        value = r.xf[rows_of(m, at), :] + r.h[rows_gap(m, at), :]
        r.xf[rows_of(m, at), :] = value
        return value

    def to_a3(m, at, u):
        r.a3[rows_of(m, at), :] = u.astype(BF)

    rstd3 = norm_forward(load_resid, r.n3, gain3, shift3, bd, to_a3, first=make_resid)
    out[0].landed()
    for j, ref in enumerate((r.q, r.k, r.v)):
        ref[...] = dot_nt(r.a3[...], r.wqg[j]).astype(BF)
    load_cnt.wait()
    count = r.cns[0]
    live = [jnp.where(2 * chan + m < count, 1.0, 0.0).astype(F32) for m in range(2)]
    scale = C ** (-0.5)
    half = [slice(0, ROWS), slice(ROWS, 2 * ROWS)]
    for m in range(2):
        s = dot_nt(r.q[half[m], :], r.k[half[m], :]) * scale
        p = jnp.exp(s - jnp.max(s, axis=1, keepdims=True))
        p = p * (1.0 / jnp.sum(p, axis=1, keepdims=True))
        r.p[half[m], :] = p
        r.pb[half[m], :] = p.astype(BF)
        r.o[half[m], :] = dot(p.astype(BF), r.v[half[m], :]).astype(BF)

    moves_dy.wait()
    out[1].landed()

    def open_dy(i, held):
        spread_out(r.dyg, chunk_at(i), r.g, live)
        return held

    lax.fori_loop(0, ROWS // CH, open_dy, 0)
    for m in range(2):
        r.turn[m] = r.g[half[m], :].T
    r.dqo[3] = (dot(r.turn[0], r.o[half[0], :]) + dot(r.turn[1], r.o[half[1], :])).astype(BF)
    r.do[...] = dot(r.g[...], r.wqg[3]).astype(BF)
    for m in range(2):
        dp_m = dot_nt(r.do[half[m], :], r.v[half[m], :])
        p = r.p[half[m], :]
        ds = (p * (dp_m - jnp.sum(p * dp_m, axis=1, keepdims=True)) * scale).astype(BF)
        r.dv[half[m], :] = dot(r.pb[half[m], :].T, r.do[half[m], :]).astype(BF)
        r.dq[half[m], :] = dot(ds, r.k[half[m], :]).astype(BF)
        r.dk[half[m], :] = dot(ds.T, r.q[half[m], :]).astype(BF)
    for j, ref in enumerate((r.dq, r.dk, r.dv)):
        parts = [dot(ref[half[m], :].T, r.a3[half[m], :]) for m in range(2)]
        r.dqo[j] = (parts[0] + parts[1]).astype(BF)

    items = []

    def reduce(letter, grad):
        start = 0
        for name, (taps, order, kind) in ITEMS.items():
            if name[1] == letter:
                work = SimpleNamespace(**{k[4:]: getattr(r, k) for k in names if k.startswith(name + "_")})
                items.append(kind(at, links, grad.at[start : start + taps], getattr(r, name), work, order))
                start += taps

    def go(*which):
        for i in which:
            items[i].advance()

    reduce("a", r.dqo)
    for m in range(2):
        total = None
        for j, ref in enumerate((r.dq, r.dk, r.dv)):
            part_j = dot(ref[half[m], :], r.wqg[j])
            total = part_j if total is None else total + part_j
        r.h[m * STEP : m * STEP + ROWS, :] = total

    def to_dres(m, at, dv, held):
        value = r.g[rows_of(m, at), :].astype(F32) + dv
        r.dres[rows_of(m, at), :] = value
        write_shift(r.dd, m, at, value, False)
        return held

    passes(norm_back(r.h, r.n3, gain3, shift3, rstd3, bd, False, r.e, 4, to_dres))
    go(0)

    def turn():
        for m in range(2):
            r.turn[m] = r.dd[GAP + STEP * m : GAP + STEP * m + ROWS, C : 2 * C].T

    turn()
    for row in range(3):
        conv_weight(r.a2, r.turn, r.dw2, row)
    reduce("b", r.dw2)
    conv_back(r.dd, r.w2g, r.h)
    mix.relay()

    def to_dh1(m, at, dv, held):
        write_shift(r.dd, m, at, dv, False)
        return held + fold(dv)

    second = norm_back(r.h, r.n2, gain2, shift2, rstd2, bd, True, r.e, 2, to_dh1)
    go(1, 2, 3)
    demb = passes(second, zero_pair())
    for m in range(2):
        r.dm[chan, m : m + 1, :] = col(demb[m]).astype(BF).astype(F32)
    moves_dm = links.group([(r.dm.at[chan], r.dm.at[chan], d) for d in quads])
    turn()
    for row in range(3):
        conv_weight(r.a1, r.turn, r.dw1, row)
    reduce("c", r.dw1)
    r.big[...] = dot_nt(r.o[...], r.wqg[3])

    def pack_out(at, pair, dst):
        for b in range(2):
            even, odd = unpack(*(v[:, 128 * b : 128 * b + 128] for v in pair))
            dst[2 * b, pl.ds(at, CH), :] = even.astype(BF)
            dst[2 * b + 1, pl.ds(at, CH), :] = odd.astype(BF)

    def to_y(i, held):
        at = chunk_at(i)
        pack_out(at, [(load_resid(m, at) + r.big[rows_of(m, at), :]) * live[m] for m in range(2)], r.yp)
        return held

    lax.fori_loop(0, ROWS // CH, to_y, 0)

    def data_one():
        conv_back(r.dd, r.w1g, r.h)

    def norm_one():
        back1 = norm_back(r.h, r.n1, gain1, shift1, rstd1, bd, True, r.e, 0,
                          lambda m, at, dv, held: r.dres[rows_of(m, at), :] + dv)

        def to_maps(i, held):
            at = chunk_at(i)
            pack_out(at, [back1(m, at, 0) for m in range(2)], r.mp)
            return held

        lax.fori_loop(0, ROWS // CH, to_maps, 0)
        moves_dm.wait()
        for j in range(CHAN):
            r.dl[2 * j : 2 * j + 2, :] = r.dm[j, 0:2, :]
        r.ra[dp] = r.dl[...]
        for d in others():
            moves_late.remote(r.dl, r.ra.at[dp], d)
        for b in range(2):
            block = r.e[:, 128 * b : 128 * b + 128]
            r.es[2 * b] = block
            r.es[2 * b + 1] = pltpu.roll(block, SL, 1)
        r.er[chan] = r.es[chan]
        for d in quads:
            moves_e.remote(r.es.at[d[1]], r.er.at[chan], d)

    def send_maps():
        for src, dst in ((r.yp, r.yo), (r.mp, r.mo)):
            at.results.copy(src.at[chan], dst.at[chan])
            for d in quads:
                moves_out.remote(src.at[d[1]], dst.at[chan], d)

    def send_gains():
        moves_e.wait()
        r.et[...] = r.er[0] + r.er[1] + r.er[2] + r.er[3]
        at.results.copy(r.et, r.ext.at[dp])
        for d in others():
            moves_out.remote(r.et, r.ext.at[dp], d)

    def embedding():
        mix.landed()
        moves_late.wait()
        maps = 8 * n_dp
        temb, s, tsil = embeddings(r.ta[...].reshape(maps, 128))
        rows = r.ra[...].reshape(maps, C)
        r.rt[...] = rows.T
        r.dew[...] = dot(r.rt[mine, :].astype(BF), tsil)
        dtemb = dot(rows.astype(BF), r.weg[0]) * (s * (1.0 + temb * (1.0 - s)))
        high = dtemb.astype(BF)
        r.bw[0:maps, :] = high
        r.bw[maps:, :] = (dtemb - high.astype(F32)).astype(BF)
        for src, dst in ((r.dew, r.de), (r.bw, r.both), (r.ta, r.tall)):
            at.results.copy(src, dst)

    moves_e, moves_out = links.group(), links.group()
    go(0)
    data_one()
    go(6, 4, 5, 3, 1)
    norm_one()
    go(2, 0, 4, 6)
    send_maps()
    go(1, 5, 0, 2, 3)
    send_gains()
    go(4, 6, 1, 5, 2, 0, 3)
    embedding()
    go(4, 6, 1, 5, 2, 0, 3, 1, 4, 2, 3, 6, 5)
    for item in items:
        item.finish()
    at.results.wait()
    moves_out.wait()
    links.close()


STORES = ["y", "dm", "de_out", "dq", "do", "d2", "d1", "dt"]


def finish(n_dp, names, *refs):
    r = SimpleNamespace(**dict(zip(names, refs)))
    maps = 8 * n_dp
    steps = r.dt.shape[0]
    links = Links(None, None, r.own, None)
    load = {name: links.here(getattr(r, name), getattr(r, name + "_v"))
            for name in ["yo", "mo", "tall", "both"] + list(ITEMS) + ["de", "ext"]}

    def out(name, src, index=slice(None)):
        dst = getattr(r, name)
        pltpu.make_async_copy(src.at[index], dst.at[index], r.stores.at[STORES.index(name)]).start()

    for name, dst, src, dst_v in (("yo", "y", r.yo_v, r.y_v), ("mo", "dm", r.mo_v, r.dm_v)):
        load[name].wait()
        for j in range(CHAN):
            block = src[j].astype(F32)
            dst_v[2 * j] = block[:, 0:SL].astype(BF)
            dst_v[2 * j + 1] = pltpu.roll(block, SL, 1)[:, 0:SL].astype(BF)
        out(dst, dst_v)
    load["tall"].wait()
    load["both"].wait()
    lanes = r.tall_v[...].reshape(maps, 128).T[0:1, :]
    lanes = jnp.concatenate([lanes, lanes], axis=1)
    for start in range(0, steps, 256):
        size = min(256, steps - start)
        ids = lax.broadcasted_iota(jnp.int32, (size, 2 * maps), 0).astype(F32) + float(start)
        hot = jnp.where(ids == lanes, 1.0, 0.0).astype(BF)
        r.dt_v[start : start + size, :] = dot(hot, r.both_v[...])
        out("dt", r.dt_v, slice(start, start + size))

    def whole(name, dst_v, base, taps):
        src = getattr(r, name + "_v")
        for i, t in enumerate(taps):
            for half in range(2):
                dst_v[base + i, :, 128 * half : 128 * half + 128] = src[0, half, SL * t : SL * t + SL, :].astype(F32)

    done = dict(b=0, c=0)
    for name, (taps, _, _) in ITEMS.items():
        load[name].wait()
        if name[1] == "a":
            whole(name, r.dq_v, 0, range(3))
            out("dq", r.dq_v)
            whole(name, r.do_v, 0, [3])
            out("do", r.do_v)
        else:
            key, start = dict(b="d2", c="d1")[name[1]], done[name[1]]
            dst_v = getattr(r, key + "_v")
            whole(name, dst_v, start, range(taps))
            out(key, dst_v, slice(start, start + taps))
            done[name[1]] += taps
    load["de"].wait()
    out("de_out", r.de_v)
    load["ext"].wait()
    total = r.ext_v[0]
    for i in range(1, n_dp):
        total = total + r.ext_v[i]
    for i in range(6):
        r.gains_v[i] = total[i : i + 1, 0:SL]
        pltpu.make_async_copy(r.gains_v.at[i], getattr(r, f"e{i}"), r.stores.at[len(STORES)]).start()
    for at, name in enumerate(STORES):
        src = r.de_v if name == "de_out" else getattr(r, name + "_v")
        pltpu.make_async_copy(src, getattr(r, name), r.stores.at[at]).wait()
    pltpu.make_async_copy(r.gains_v, r.gains_v, r.stores.at[len(STORES)]).wait()


def per_device(x_maps, timesteps, counts, emb_table, w_first, w_second, w_embed, w_qkv, w_out, gain_one, shift_one,
               gain_two, shift_two, gain_three, shift_three, cotangent, *, n_dp):
    team, teams = block_sizes(n_dp)
    slots, side, _, _ = x_maps.shape
    emb = w_embed.shape[0]
    steps = emb_table.shape[0]
    inputs = dict(
        x=x_maps.reshape(slots, side * side, SL), dy=cotangent.reshape(slots, side * side, SL),
        ts=timesteps, cnt=counts, table=emb_table,
        w1=jnp.swapaxes(w_first, 2, 3).reshape(9, SL, C), w2=jnp.swapaxes(w_second, 2, 3).reshape(9, SL, C),
        we=w_embed.T[None], wq=jnp.transpose(w_qkv, (1, 2, 0)), wo=w_out.T[None])
    gains = (gain_one, shift_one, gain_two, shift_two, gain_three, shift_three)
    inputs.update({name: v.reshape(1, SL) for name, v in zip(GAINS, gains)})
    anywhere = pl.BlockSpec(memory_space=pl.ANY)

    def of(shape, dtype):
        return jax.ShapeDtypeStruct(shape, dtype)

    maps = 8 * n_dp
    middle = dict(
        yo=of((CHAN, ROWS, 128), BF), mo=of((CHAN, ROWS, 128), BF), tall=of((n_dp, 8, 128), F32),
        ext=of((n_dp, 8, 128), F32), both=of((2 * maps, emb), BF), de=of((SL, emb), F32))
    middle.update({name: of((1, 2, SL * item[0], 128), BF) for name, item in ITEMS.items()})
    v = pltpu.VMEM
    maps2 = 2 * ROWS
    scratch = dict(
        xl=v((slots, ROWS, SL), BF), dyl=v((slots, ROWS, SL), BF), pin=v((len(GAINS), 1, SL), BF),
        tss=pltpu.SMEM((slots,), jnp.int32), cns=pltpu.SMEM((1,), jnp.int32), tab=v((steps, emb), BF),
        xp=v((CHAN, ROWS, 128), BF), dyp=v((CHAN, ROWS, 128), BF),
        xg=v((CHAN, ROWS, 128), BF), dyg=v((CHAN, ROWS, 128), BF),
        yp=v((CHAN, ROWS, 128), BF), mp=v((CHAN, ROWS, 128), BF),
        w1g=v((9, C, C), BF), w2g=v((9, C, C), BF), weg=v((1, C, emb), BF), wqg=v((4, C, C), BF),
        bd=v((C, C), BF), tl=v((8, 128), F32), ta=v((n_dp, 8, 128), F32), par=v((8, 128), F32),
        pg=v((CHAN, 8, 128), F32), pa=v((8, C), F32), emb=v((8, C), F32),
        wel=v((1, SL, emb), BF), el=v((8, 128), F32), eg=v((CHAN, 8, 128), F32),
        a1=v((TALL + 2 * GAP, 3 * C), BF), a2=v((TALL + 2 * GAP, 3 * C), BF), dd=v((TALL + 2 * GAP, 3 * C), BF),
        h=v((TALL, C), F32), xf=v((maps2, C), F32), n1=v((maps2, C), F32), n2=v((maps2, C), F32),
        n3=v((maps2, C), F32), dres=v((maps2, C), F32), big=v((maps2, C), F32), p=v((maps2, C), F32),
        e=v((8, C), F32), es=v((CHAN, 8, 128), F32), er=v((CHAN, 8, 128), F32), et=v((8, 128), F32),
        dm=v((CHAN, 8, C), F32), dl=v((8, C), F32), ra=v((n_dp, 8, C), F32), rt=v((C, maps), F32),
        dew=v((SL, emb), F32), bw=v((2 * maps, emb), BF), turn=v((2, ROWS, C), BF),
        dw1=v((9, C, C), BF), dw2=v((9, C, C), BF), dqo=v((4, C, C), BF))
    for name in ("a3", "q", "k", "v", "pb", "o", "g", "do", "dq", "dk", "dv"):
        scratch[name] = v((maps2, C), BF)
    for name, (taps, order, kind) in ITEMS.items():
        buffers = reduction_scratch(taps, order, kind, teams)
        scratch.update({name + "_" + k: b for k, b in buffers.items()})
    several = len(ITEMS) if teams > 1 else 0
    scratch.update(
        idle=v((4096, 128), BF), send=pltpu.SemaphoreType.DMA((SENDS + several,)),
        recv=pltpu.SemaphoreType.DMA((GROUPS_OF_COPIES + several,)), own=pltpu.SemaphoreType.DMA((9 + several,)),
        gains=pltpu.SemaphoreType.DMA(()))
    got = pl.pallas_call(
        functools.partial(mega, n_dp, list(inputs) + list(middle) + list(scratch)),
        out_shape=tuple(middle.values()),
        in_specs=[anywhere] * len(inputs),
        out_specs=(anywhere,) * len(middle),
        scratch_shapes=list(scratch.values()),
        compiler_params=pltpu.CompilerParams(collective_id=0, has_side_effects=True, vmem_limit_bytes=60 << 20),
        name="blocks",
    )(*inputs.values())
    results = dict(
        y=of((slots, ROWS, SL), BF), dm=of((slots, ROWS, SL), BF), dt=of((steps, emb), F32), d1=of((9, SL, C), F32),
        d2=of((9, SL, C), F32), de_out=of((SL, emb), F32), dq=of((3, SL, C), F32), do=of((1, SL, C), F32))
    results.update({f"e{i}": of((1, SL), F32) for i in range(6)})
    scratch = {name + "_v": v(o.shape, o.dtype) for name, o in middle.items()}
    scratch.update({name + "_v": v(o.shape, o.dtype) for name, o in results.items() if name[0] != "e"})
    scratch.update(
        gains_v=v((6, 1, SL), F32), own=pltpu.SemaphoreType.DMA((len(middle),)),
        stores=pltpu.SemaphoreType.DMA((len(STORES) + 1,)))
    got = pl.pallas_call(
        functools.partial(finish, n_dp, list(middle) + list(results) + list(scratch)),
        out_shape=tuple(results.values()),
        in_specs=[anywhere] * len(middle),
        out_specs=(anywhere,) * len(results),
        scratch_shapes=list(scratch.values()),
        compiler_params=pltpu.CompilerParams(vmem_limit_bytes=60 << 20),
        name="finish",
    )(*got)
    got = dict(zip(results, got))
    return (
        got["y"].reshape(x_maps.shape), got["dm"].reshape(x_maps.shape), got["dt"],
        jnp.swapaxes(got["d1"].reshape(3, 3, SL, C), 2, 3), jnp.swapaxes(got["d2"].reshape(3, 3, SL, C), 2, 3),
        got["de_out"].T, jnp.transpose(got["dq"], (2, 0, 1)), got["do"].reshape(SL, C).T,
    ) + tuple(got[f"e{i}"].reshape(SL) for i in range(6))


def solution(mesh):
    weights = (P(None, None, None, "chan"), P(None, None, None, "chan"), P(None, "chan"), P(None, None, "chan"),
               P(None, "chan")) + (P("chan"),) * 6
    maps = P("dp", None, None, "chan")
    return jax.shard_map(
        functools.partial(per_device, n_dp=mesh.shape["dp"]), mesh=mesh,
        in_specs=(maps, P("dp"), P("dp"), P()) + weights + (maps,),
        out_specs=(maps, maps, P()) + weights, check_vma=False)
```

```python
import functools
from types import SimpleNamespace

import jax
import jax.numpy as jnp
from jax import lax
from jax.experimental import pallas as pl
from jax.experimental.pallas import tpu as pltpu
from jax.sharding import PartitionSpec as P

F32 = jnp.float32
BF = jnp.bfloat16
MESH = pl.DeviceIdType.MESH
EPS = 1e-06
GROUPS = 32
CHAN = 4
ROWS = 256
C = 256
SL = C // CHAN
GAP = 16
STEP = ROWS + GAP
TALL = 2 * ROWS + GAP
CH = 256
COUNT = ROWS * (C // GROUPS)


def dot(a, b):
    return jnp.dot(a, b, preferred_element_type=F32)


def dot_nt(a, b):
    return lax.dot_general(a, b, (((1,), (1,)), ((), ())), preferred_element_type=F32)


def sigmoid(u):
    return 0.5 * jnp.tanh(0.5 * u) + 0.5


def fold(v):
    return v.reshape(v.shape[0] // 8, 8, v.shape[1]).sum(axis=0)


def group_total(rows, bd):
    at = lax.broadcasted_iota(jnp.int32, (8, C), 0)
    stack = jnp.zeros((8, C), F32)
    for i, row in enumerate(rows):
        stack = jnp.where(at == i, row, stack)
    high = stack.astype(BF).astype(F32)
    rest = stack - high
    mid = rest.astype(BF).astype(F32)
    parts = jnp.concatenate([high, mid, rest - mid, jnp.zeros((8, C), F32)], axis=0)
    total = dot(parts.astype(BF), bd)
    total = total[0:8] + total[8:16] + total[16:24]
    return [total[i : i + 1] for i in range(len(rows))]


def chunk_at(i):
    return pl.multiple_of(i * CH, CH)


def passes(body, carry=None):
    carry = (0, 0) if carry is None else carry

    def step(i, held):
        return tuple(body(m, chunk_at(i), held[m]) for m in range(2))

    return lax.fori_loop(0, ROWS // CH, step, carry)


def zero_pair():
    return (jnp.zeros((8, C), F32), jnp.zeros((8, C), F32))


def col(v):
    return jnp.sum(v, axis=0, keepdims=True)


def write_shift(dst, m, at, value, forward):
    place = lax.broadcasted_iota(jnp.int32, (CH, C), 0) % 16
    before = jnp.where(place == 0, 0.0, pltpu.roll(value, 1, 0))
    after = jnp.where(place == 15, 0.0, pltpu.roll(value, CH - 1, 0))
    first, last = (before, after) if forward else (after, before)
    rows = pl.ds(pl.multiple_of(at + (GAP + m * STEP), 16), CH)
    dst[rows, 0:C] = first.astype(BF)
    dst[rows, C : 2 * C] = value.astype(BF)
    dst[rows, 2 * C : 3 * C] = last.astype(BF)


def norm_forward(load, n_ref, gain, shift, bd, emit, first=None, early=None, midway=None):
    sums = []
    for at in range(0, ROWS, CH):
        for m in range(2):
            value = (first or load)(m, at)
            if at == 0:
                near = col(value[0:32]) * (1.0 / 32)
                sums.append([near, zero_pair()[0], zero_pair()[0]])
            d = value - sums[m][0]
            sums[m][1] = sums[m][1] + fold(d)
            sums[m][2] = sums[m][2] + fold(d * d)
    if early is not None:
        early()
    ones = [col(t[1]) for t in sums]
    middle = [t[0] + one * (1.0 / ROWS) for t, one in zip(sums, ones)]
    mean = [v * (GROUPS / C) for v in group_total(middle, bd)]
    spread = [
        col(t[2]) - one * one * (1.0 / ROWS) + ROWS * (mid - mu) * (mid - mu)
        for t, one, mid, mu in zip(sums, ones, middle, mean)]
    rstd = [lax.rsqrt(v * (1.0 / COUNT) + EPS) for v in group_total(spread, bd)]
    if midway is not None:
        midway()

    def last(m, at, held):
        n = (load(m, at) - mean[m]) * rstd[m]
        n_ref[pl.ds(pl.multiple_of(at + m * ROWS, CH), CH), :] = n
        emit(m, at, n * gain + shift)
        return held

    passes(last)
    return rstd


def norm_back(d_ref, n_ref, gain, shift, rstd, bd, active, e_ref, e_at, emit):
    def rows(m, at):
        return pl.ds(pl.multiple_of(at + m * STEP, 16), CH)

    def first(m, at, held):
        d = d_ref[rows(m, at), :]
        n = n_ref[pl.ds(pl.multiple_of(at + m * ROWS, CH), CH), :]
        if active:
            u = n * gain + shift
            s = sigmoid(u)
            d = d * (s * (1.0 + u * (1.0 - s)))
            d_ref[rows(m, at), :] = d
        return (held[0] + fold(d), held[1] + fold(d * n))

    total = passes(first, (zero_pair(), zero_pair()))
    ones = [col(t[0]) for t in total]
    twos = [col(t[1]) for t in total]
    e_ref[e_at : e_at + 1, :] = twos[0] + twos[1]
    e_ref[e_at + 1 : e_at + 2, :] = ones[0] + ones[1]
    means = group_total([gain * v for v in ones + twos], bd)
    means = [v * (1.0 / COUNT) for v in means]

    def second(m, at, held):
        d = d_ref[rows(m, at), :]
        n = n_ref[pl.ds(pl.multiple_of(at + m * ROWS, CH), CH), :]
        return emit(m, at, rstd[m] * (d * gain - means[m] - n * means[2 + m]), held)

    return second


def unpack(low, high):
    lane = lax.broadcasted_iota(jnp.int32, low.shape, 1)
    first = jnp.where(lane < SL, low, pltpu.roll(high, SL, 1))
    second = jnp.where(lane < SL, pltpu.roll(low, SL, 1), high)
    return first, second


BLOCKS = ((0, STEP), (STEP, ROWS))


def conv_forward(a_ref, w_ref, h_ref, rows):
    for start, size in BLOCKS:
        total = None
        for row in rows:
            for c in range(3):
                at = 16 * row + start
                part = dot_nt(a_ref[at : at + size, C * c : C * c + C], w_ref[3 * row + c])
                total = part if total is None else total + part
        h_ref[start : start + size, :] = total


def conv_back(d_ref, w_ref, h_ref):
    for start, size in BLOCKS:
        total = None
        for row in range(3):
            at = 16 * (2 - row) + start
            part = dot(d_ref[at : at + size, :], w_ref[3 * row : 3 * row + 3].reshape(3 * C, C))
            total = part if total is None else total + part
        h_ref[start : start + size, :] = total


def conv_weight(a_ref, turned, dw_ref, row):
    for c in range(3):
        total = None
        for m in range(2):
            at = 16 * row + STEP * m
            part = dot(turned[m], a_ref[at : at + ROWS, C * c : C * c + C])
            total = part if total is None else total + part
        dw_ref[3 * row + c] = total.astype(BF)


class Group:
    def __init__(self, links):
        self.links, self.at, self.rows = links, links.used, 0
        links.used += 1

    def remote(self, src, dst, device):
        self.plan(src, dst, device)()

    def plan(self, src, dst, device):
        links, rows = self.links, rows_in(src)
        if links.sending + rows > links.idle.shape[0]:
            links.ended.append((links.senders, links.sending))
            links.senders, links.sending = links.senders + 1, 0
        links.sending += rows
        self.rows += rows
        sender = links.send.at[links.senders]
        return lambda: pltpu.make_async_remote_copy(
            src_ref=src, dst_ref=dst, send_sem=sender, recv_sem=links.recv.at[self.at],
            device_id=device, device_id_type=MESH).start()

    def wait(self):
        self.links.wait_rows(self.links.recv.at[self.at], self.rows)


class LocalGroup:
    def __init__(self, links):
        self.links, self.at, self.rows = links, links.local, 0
        links.local += 1

    def copy(self, src, dst):
        self.rows += rows_in(src)
        pltpu.make_async_copy(src, dst, self.links.own.at[self.at]).start()

    def wait(self):
        self.links.wait_rows(self.links.own.at[self.at], self.rows)


def rows_in(ref):
    size = ref.dtype.itemsize
    for n in ref.shape:
        size *= n
    return size // 256


class Links:
    def __init__(self, send, recv, own, idle):
        self.send, self.recv, self.own, self.idle = send, recv, own, idle
        self.used, self.local, self.senders, self.sending = 0, 0, 0, 0
        self.ended = []

    def wait_rows(self, semaphore, rows):
        view = self.idle.at[0:rows]
        pltpu.make_async_copy(view, view, semaphore).wait()

    def group(self, copies=()):
        group = Group(self)
        for src, dst, device in copies:
            group.remote(src, dst, device)
        return group

    def here(self, src, dst):
        copy = pltpu.make_async_copy(src, dst, self.own.at[self.local])
        self.local += 1
        copy.start()
        return copy

    def here_all(self, copies=()):
        group = LocalGroup(self)
        for src, dst in copies:
            group.copy(src, dst)
        return group

    def close(self):
        for at, rows in self.ended + [(self.senders, self.sending)]:
            self.wait_rows(self.send.at[at], rows)


def block_sizes(n_dp):
    team = min(8, n_dp)
    return team, n_dp // team


def aligned(start, size):
    return pl.ds(pl.multiple_of(start, size), size)


def reduction_scratch(taps, order, kind, teams):
    rows = SL * taps
    part = (1, 1, rows, 128)
    shapes = dict(rc=(2, taps, SL, C), s0=(2, 2, rows, 128), pc=part, sum=part, rt=(teams,) + part)
    shapes.update({name: part for name in ("c0", "c1", "c2", "p0", "p1", "t0", "t1")})
    size = dict(y=2, x=2)
    for k, axis in enumerate(order):
        size[axis] = 1
        shapes[f"r{k}"] = shapes[f"s{k + 1}"] = (size["y"], size["x"], rows, 128)
    buffers = {name: pltpu.VMEM(shape, BF) for name, shape in shapes.items()}
    if kind is Chain:
        buffers.update(cs=pltpu.SemaphoreType.DMA((4,)))
    return buffers


class Reduction:
    def __init__(self, at, links, grad, out, work, order):
        self.at, self.links, self.grad, self.out, self.w, self.order = at, links, grad, out, work, order
        self.taps = grad.shape[0]
        self.size = dict(y=2, x=2, z=at.team // 2)
        self.stage = -1
        self.whole = dict(y=True, x=True)
        self.group = links.group([
            (grad.at[:, aligned(SL * (2 * y + 1 - at.core), SL), :], self.w.rc.at[y], at.sibling) for y in range(2)])

    def view(self, ref, axis, index):
        return ref.at[pl.ds(index, 1)] if axis == "y" else ref.at[:, pl.ds(index, 1)]

    def send(self):
        axis = self.order[self.stage]
        other = 1 - self.at.place[axis]
        current, arriving = getattr(self.w, f"s{self.stage}"), getattr(self.w, f"r{self.stage}")
        self.group = self.links.group([(self.view(current, axis, other), arriving, self.at.peer({axis: other}))])

    def collect(self):
        at, w = self.at, self.w
        self.group.wait()
        if self.stage < 0:
            for y in range(2):
                for t in range(self.taps):
                    mine = self.grad[t, aligned(SL * (2 * y + at.core), SL), :].astype(F32)
                    total = (mine + w.rc[y, t].astype(F32)).astype(BF)
                    for half in range(2):
                        w.s0[y, half, SL * t : SL * t + SL, :] = total[:, 128 * half : 128 * half + 128]
            return
        axis = self.order[self.stage]
        mine = self.view(getattr(w, f"s{self.stage}"), axis, at.place[axis])[...].astype(F32)
        total = mine + getattr(w, f"r{self.stage}")[...].astype(F32)
        getattr(w, f"s{self.stage + 1}")[...] = total.astype(BF)

    def across_teams(self, piece):
        at, w = self.at, self.w
        own = self.links.here(piece, w.rt.at[at.lead])
        group = self.links.group([
            (piece, w.rt.at[at.lead], at.device((at.lead + s) % at.teams * at.team + at.rank))
            for s in range(1, at.teams)])
        own.wait()
        group.wait()
        total = w.rt[0].astype(F32)
        for s in range(1, at.teams):
            total = total + w.rt[s].astype(F32)
        w.sum[...] = total.astype(BF)
        return w.sum

    def share(self, source):
        source = self.across_teams(source) if self.at.teams > 1 else source
        target = self.out.at[:, pl.ds(self.at.place["x"], 1)]
        self.at.results.copy(source, target)
        self.group = self.links.group([(source, target, self.at.peer(dict(x=1 - self.at.place["x"])))])

    def advance(self):
        last = len(self.order) - 1
        if self.stage <= last:
            self.collect()
        if self.stage < last:
            self.stage += 1
            self.send()
        else:
            self.along_z(self.stage - last, getattr(self.w, f"s{last + 1}"))
            self.stage += 1

    def finish(self):
        self.group.wait()


class Chain(Reduction):
    def copy(self, sent, got, src, dst, z):
        w = self.w
        return pltpu.make_async_remote_copy(
            src_ref=src, dst_ref=dst, send_sem=w.cs.at[sent], recv_sem=w.cs.at[2 + got],
            device_id=self.at.peer(dict(z=z)), device_id_type=MESH)

    def along_z(self, step, total):
        w, count = self.w, self.size["z"]
        long, alone = count == 4, count == 1
        if step == 0:
            z = self.at.place["z"]
            self.end = (z == 0) | (z == count - 1)
            self.inner = jnp.logical_not(self.end)
            self.inward = self.copy(0, 0, total, w.c0, jnp.where(z < 2, 1, 2))
            self.swap = self.copy(0, 1, w.c1, w.c2, count - 1 - z)
            self.outward = self.copy(1, 0, w.pc, w.pc, jnp.where(z < 2, 0, 3))
            if long:
                pl.when(self.end)(self.inward.start)
            else:
                w.c1[...] = total[...]
        elif step == 1:
            if long:
                @pl.when(self.inner)
                def _():
                    self.inward.wait_recv()
                    w.c1[...] = (total[...].astype(F32) + w.c0[...].astype(F32)).astype(BF)
                    self.swap.start()
            elif not alone:
                self.swap.start()
        elif step == 2:
            def join():
                self.swap.wait_recv()
                w.pc[...] = (w.c1[...].astype(F32) + w.c2[...].astype(F32)).astype(BF)

            if long:
                @pl.when(self.inner)
                def _():
                    join()
                    self.outward.start()
            elif alone:
                w.pc[...] = w.c1[...]
            else:
                join()
        else:
            if long:
                @pl.when(self.end)
                def _():
                    self.outward.wait_recv()
                    self.inward.wait_send()

                @pl.when(self.inner)
                def _():
                    self.swap.wait_send()
                    self.outward.wait_send()
            elif not alone:
                self.swap.wait_send()
            self.share(w.pc)


class Pairs(Reduction):
    def along_z(self, step, total):
        w, z = self.w, self.at.place["z"]
        partners = [z + 1 - 2 * (z % 2), (z + 2) % 4]
        partners[self.size["z"] // 2 :] = [None] * (2 - self.size["z"] // 2)
        if step == 0:
            self.held = total
        elif partners[step - 1] is not None:
            self.group.wait()
            total = self.held[...].astype(F32) + getattr(w, f"p{step - 1}")[...].astype(F32)
            self.held = getattr(w, f"t{step - 1}")
            self.held[...] = total.astype(BF)
        if step == len(partners):
            self.share(self.held)
        elif partners[step] is not None:
            self.group = self.links.group([
                (self.held, getattr(w, f"p{step}"), self.at.peer(dict(z=partners[step])))])


YX, XY = ("y", "x"), ("x", "y")
ITEMS = {
    "ga0": (4, YX, Chain),
    "gb0": (3, YX, Chain),
    "gb1": (3, YX, Chain),
    "gb2": (3, XY, Chain),
    "gc0": (3, YX, Pairs),
    "gc1": (3, YX, Pairs),
    "gc2": (3, XY, Pairs),
}
SENDS, GROUPS_OF_COPIES = 8, 72
GAINS = ("gain1", "shift1", "gain2", "shift2", "gain3", "shift3")


def mega(n_dp, names, *refs):
    r = SimpleNamespace(**dict(zip(names, refs)))
    team, teams = block_sizes(n_dp)
    dp, chan = lax.axis_index("dp"), lax.axis_index("chan")
    core, y, bit = chan % 2, chan // 2, dp % 2
    sibling, across, corner = (dp, 2 * y + 1 - core), (dp, 2 * (1 - y) + core), (dp, 2 * (1 - y) + 1 - core)
    beside, oblique = (dp + 1 - 2 * bit, chan), (dp + 1 - 2 * bit, 2 * (1 - y) + core)
    quads = (sibling, across, corner)
    rank, lead = dp % team, dp // team
    own_place = dict(y=y, x=bit, z=rank // 2)

    def peer(place):
        place = {**own_place, **place}
        return (lead * team + 2 * place["z"] + place["x"], 2 * place["y"] + core)

    at = SimpleNamespace(core=core, sibling=sibling, team=team, teams=teams, rank=rank, lead=lead, place=own_place,
                         peer=peer, device=lambda p: (p, chan))
    links = Links(r.send, r.recv, r.own, r.idle)
    at.results = links.here_all()

    def others():
        return [(lax.rem(dp + s, n_dp), chan) for s in range(1, n_dp)]

    barrier = pltpu.get_barrier_semaphore()
    for device in quads + (oblique,) + tuple(others()):
        pl.semaphore_signal(barrier, inc=1, device_id=device, device_id_type=MESH)
    load_x, load_ts, load_table = links.here(r.x, r.xl), links.here(r.ts, r.tss), links.here(r.table, r.tab)
    for i, name in enumerate(GAINS):
        pltpu.make_async_copy(getattr(r, name), r.pin.at[i], r.gains).start()
    load_we, load_dy, load_cnt = links.here(r.we, r.wel), links.here(r.dy, r.dyl), links.here(r.cnt, r.cns)
    mine = aligned(SL * chan, SL)
    fill = links.here_all([
        (r.w1, r.w1g.at[:, mine, :]), (r.w2, r.w2g.at[:, mine, :]), (r.we, r.weg.at[:, mine, :]),
        (r.wq, r.wqg.at[0:3, mine, :]), (r.wo, r.wqg.at[3:4, mine, :])])

    def pack(src, dst):
        for k in range(CHAN):
            for half in range(2):
                rows = slice(128 * half, 128 * half + 128)
                both = jnp.concatenate([src[2 * k, rows, :].astype(F32), src[2 * k + 1, rows, :].astype(F32)], axis=1)
                dst[k, rows, :] = both.astype(BF)

    load_x.wait()
    pack(r.xl, r.xp)
    pltpu.make_async_copy(r.pin, r.pin, r.gains).wait()
    r.par[...] = jnp.zeros((8, 128), F32)
    for i in range(len(GAINS)):
        r.par[i : i + 1, 0:SL] = r.pin[i].astype(F32)
    pl.semaphore_wait(barrier, CHAN + n_dp - 1)

    far = SL * (2 * (1 - y) + core)
    low = (dp // 2) % 2
    above = (dp + 2 - 4 * low, chan) if n_dp > 2 else None

    class Share:
        def __init__(self, w, g, parts, later=None):
            self.w, self.g, self.parts = w, g, parts if n_dp > 2 else min(parts, 2)
            self.from_sibling = links.group()
            self.size = SL // self.parts
            self.part = {1: 0, 2: 32 * bit, 4: 32 * low + 16 * bit}[self.parts]
            self.over = links.group()
            start = self.over.plan(
                w.at[:, aligned(self.part, self.size), :], g.at[:, aligned(SL * chan + self.part, self.size), :], across)
            if later is None:
                start()
            else:
                later.append(start)

        def own(self):
            self.from_sibling.remote(self.w, self.g.at[:, mine, :], sibling)

        def piece(self, start, size):
            return self.g.at[:, aligned(far + start, size), :]

        def to_sibling(self, start, size):
            piece = self.piece(start, size)
            self.from_sibling.remote(piece, piece, sibling)

        def relay(self):
            self.over.wait()
            piece = self.piece(self.part, self.size)
            if self.parts > 1:
                self.around = links.group([(piece, piece, beside)])
            if self.parts < 4:
                self.to_sibling(self.part, self.size)

        def relay_up(self):
            if self.parts == 4:
                self.around.wait()
                piece = self.piece(32 * low, 32)
                self.around = links.group([(piece, piece, above)])
                self.to_sibling(32 * low, 32)

        def relay_again(self):
            self.around.wait()
            self.to_sibling(32 - 32 * (low if self.parts == 4 else bit), 32)

        def landed(self):
            self.from_sibling.wait()

    def rows3(ref, row):
        return ref.at[3 * row : 3 * row + 3]

    one = [Share(rows3(r.w1, row), rows3(r.w1g, row), 2 if row == 2 else 4) for row in range(3)]
    for share in one:
        share.own()
    later = []
    two = [Share(rows3(r.w2, row), rows3(r.w2g, row), 4, later) for row in range(2)]
    for share in two:
        share.own()

    load_ts.wait()
    row8 = lax.broadcasted_iota(jnp.int32, (8, 128), 0)
    times = jnp.zeros((8, 128), F32)
    for i in range(8):
        times = jnp.where(row8 == i, r.tss[i].astype(F32), times)
    r.tl[...] = times
    r.ta[dp] = times
    steps = r.table.shape[0]
    load_table.wait()

    def embeddings(times):
        count = times.shape[0]
        wide = jnp.broadcast_to(times[:, 0:1], (count, steps))
        hot = jnp.where(wide == lax.broadcasted_iota(jnp.int32, (count, steps), 1).astype(F32), 1.0, 0.0)
        temb = dot(hot.astype(BF), r.tab[...])
        s = sigmoid(temb)
        return temb, s, (temb * s).astype(BF)

    _, _, tsil = embeddings(jnp.concatenate([times, times], axis=0))
    load_we.wait()
    r.el[...] = jnp.zeros((8, 128), F32)
    r.el[:, 0:SL] = dot_nt(tsil, r.wel[0])[0:8]
    r.eg[chan] = r.el[...]
    moves_x, moves_emb = links.group(), links.group()
    later += [moves_x.plan(r.xp.at[d[1]], r.xg.at[chan], d) for d in quads]
    later += [moves_x.plan(r.par, r.pg.at[chan], d) for d in quads]
    later += [moves_emb.plan(r.el, r.eg.at[chan], d) for d in quads]

    def start_later():
        for start in later:
            start()

    pl.when(core == 0)(start_later)
    r.xg[chan] = r.xp[chan]
    r.pg[chan] = r.par[...]
    at_row = lax.broadcasted_iota(jnp.int32, (C, C), 0) // (C // GROUPS)
    at_col = lax.broadcasted_iota(jnp.int32, (C, C), 1) // (C // GROUPS)
    r.bd[...] = jnp.where(at_row == at_col, 1.0, 0.0).astype(BF)
    for ref in (r.a1, r.a2, r.dd):
        for gap in range(3):
            ref[gap * STEP : gap * STEP + GAP, :] = jnp.zeros((GAP, 3 * C), BF)
    load_dy.wait()
    pack(r.dyl, r.dyp)
    r.dyg[chan] = r.dyp[chan]
    for share in one:
        share.relay()
    pl.when(core == 1)(start_later)
    two.append(Share(rows3(r.w2, 2), rows3(r.w2g, 2), 1))
    two[2].own()
    one[0].relay_up()
    two[0].relay()
    one[1].relay_up()
    out = [Share(r.wq, r.wqg.at[0:3], 1), Share(r.wo, r.wqg.at[3:4], 1)]
    for share in out:
        share.own()
    two[1].relay()
    one[2].relay_again()
    two[0].relay_up()
    moves_dy = links.group([(r.dyp.at[d[1]], r.dyg.at[chan], d) for d in quads])
    mix = Share(r.we, r.weg, 1)
    mix.own()
    moves_late = links.group([(r.tl, r.ta.at[dp], d) for d in others()])
    one[0].relay_again()
    two[1].relay_up()

    bd = r.bd[...]
    moves_x.wait()
    one[1].relay_again()
    for b in range(2):
        first, _ = unpack(r.pg[2 * b], r.pg[2 * b + 1])
        r.pa[:, 128 * b : 128 * b + 128] = first
    par = r.pa[...]
    gain1, shift1, gain2, shift2, gain3, shift3 = [par[i : i + 1] for i in range(6)]

    def spread_out(src, at, dst, scale=None):
        for b in range(2):
            pair = unpack(src[2 * b, pl.ds(at, CH), :].astype(F32), src[2 * b + 1, pl.ds(at, CH), :].astype(F32))
            for m in range(2):
                value = pair[m] if scale is None else pair[m] * scale[m]
                dst[pl.ds(pl.multiple_of(at + m * ROWS, CH), CH), 128 * b : 128 * b + 128] = value.astype(dst.dtype)

    def rows_of(m, at):
        return pl.ds(pl.multiple_of(at + m * ROWS, CH), CH)

    def rows_gap(m, at):
        return pl.ds(pl.multiple_of(at + m * STEP, 16), CH)

    def to_shift(dst):
        def emit(m, at, u):
            write_shift(dst, m, at, u * sigmoid(u), True)
        return emit

    def open_x(m, at):
        if m == 0:
            spread_out(r.xg, at, r.xf)
        return r.xf[rows_of(m, at), :]

    rstd1 = norm_forward(lambda m, at: r.xf[rows_of(m, at), :], r.n1, gain1, shift1, bd, to_shift(r.a1), first=open_x)
    fill.wait()

    for share in one:
        share.landed()
    conv_forward(r.a1, r.w1g, r.h, (0, 1, 2))
    two[0].relay_again()
    moves_emb.wait()
    for b in range(2):
        first, _ = unpack(r.eg[2 * b], r.eg[2 * b + 1])
        r.emb[:, 128 * b : 128 * b + 128] = first
    emb = [r.emb[pl.ds(2 * chan + m, 1), :] for m in range(2)]
    rstd2 = norm_forward(lambda m, at: r.h[rows_gap(m, at), :] + emb[m], r.n2, gain2, shift2, bd, to_shift(r.a2),
                         early=two[2].relay, midway=two[1].relay_again)
    out[0].relay()
    for share in two:
        share.landed()
    conv_forward(r.a2, r.w2g, r.h, (0, 1, 2))
    out[1].relay()

    def load_resid(m, at):
        return r.xf[rows_of(m, at), :]

    def make_resid(m, at):
        value = r.xf[rows_of(m, at), :] + r.h[rows_gap(m, at), :]
        r.xf[rows_of(m, at), :] = value
        return value

    def to_a3(m, at, u):
        r.a3[rows_of(m, at), :] = u.astype(BF)

    rstd3 = norm_forward(load_resid, r.n3, gain3, shift3, bd, to_a3, first=make_resid)
    out[0].landed()
    for j, ref in enumerate((r.q, r.k, r.v)):
        ref[...] = dot_nt(r.a3[...], r.wqg[j]).astype(BF)
    load_cnt.wait()
    count = r.cns[0]
    live = [jnp.where(2 * chan + m < count, 1.0, 0.0).astype(F32) for m in range(2)]
    scale = C ** (-0.5)
    half = [slice(0, ROWS), slice(ROWS, 2 * ROWS)]
    for m in range(2):
        s = dot_nt(r.q[half[m], :], r.k[half[m], :]) * scale
        p = jnp.exp(s - jnp.max(s, axis=1, keepdims=True))
        p = p * (1.0 / jnp.sum(p, axis=1, keepdims=True))
        r.p[half[m], :] = p
        r.pb[half[m], :] = p.astype(BF)
        r.o[half[m], :] = dot(p.astype(BF), r.v[half[m], :]).astype(BF)

    moves_dy.wait()
    out[1].landed()

    def open_dy(i, held):
        spread_out(r.dyg, chunk_at(i), r.g, live)
        return held

    lax.fori_loop(0, ROWS // CH, open_dy, 0)
    for m in range(2):
        r.turn[m] = r.g[half[m], :].T
    r.dqo[3] = (dot(r.turn[0], r.o[half[0], :]) + dot(r.turn[1], r.o[half[1], :])).astype(BF)
    r.do[...] = dot(r.g[...], r.wqg[3]).astype(BF)
    for m in range(2):
        dp_m = dot_nt(r.do[half[m], :], r.v[half[m], :])
        p = r.p[half[m], :]
        ds = (p * (dp_m - jnp.sum(p * dp_m, axis=1, keepdims=True)) * scale).astype(BF)
        r.dv[half[m], :] = dot(r.pb[half[m], :].T, r.do[half[m], :]).astype(BF)
        r.dq[half[m], :] = dot(ds, r.k[half[m], :]).astype(BF)
        r.dk[half[m], :] = dot(ds.T, r.q[half[m], :]).astype(BF)
    for j, ref in enumerate((r.dq, r.dk, r.dv)):
        parts = [dot(ref[half[m], :].T, r.a3[half[m], :]) for m in range(2)]
        r.dqo[j] = (parts[0] + parts[1]).astype(BF)

    items = []

    def reduce(letter, grad):
        start = 0
        for name, (taps, order, kind) in ITEMS.items():
            if name[1] == letter:
                work = SimpleNamespace(**{k[4:]: getattr(r, k) for k in names if k.startswith(name + "_")})
                items.append(kind(at, links, grad.at[start : start + taps], getattr(r, name), work, order))
                start += taps

    def go(*which):
        for i in which:
            items[i].advance()

    reduce("a", r.dqo)
    for m in range(2):
        total = None
        for j, ref in enumerate((r.dq, r.dk, r.dv)):
            part_j = dot(ref[half[m], :], r.wqg[j])
            total = part_j if total is None else total + part_j
        r.h[m * STEP : m * STEP + ROWS, :] = total

    def to_dres(m, at, dv, held):
        value = r.g[rows_of(m, at), :].astype(F32) + dv
        r.dres[rows_of(m, at), :] = value
        write_shift(r.dd, m, at, value, False)
        return held

    passes(norm_back(r.h, r.n3, gain3, shift3, rstd3, bd, False, r.e, 4, to_dres))

    def turn():
        for m in range(2):
            r.turn[m] = r.dd[GAP + STEP * m : GAP + STEP * m + ROWS, C : 2 * C].T

    turn()
    go(0)
    for row in range(3):
        conv_weight(r.a2, r.turn, r.dw2, row)
    reduce("b", r.dw2)
    conv_back(r.dd, r.w2g, r.h)
    mix.relay()

    def to_dh1(m, at, dv, held):
        write_shift(r.dd, m, at, dv, False)
        return held + fold(dv)

    second = norm_back(r.h, r.n2, gain2, shift2, rstd2, bd, True, r.e, 2, to_dh1)
    go(1, 2, 3)
    demb = passes(second, zero_pair())
    for m in range(2):
        r.dm[chan, m : m + 1, :] = col(demb[m]).astype(BF).astype(F32)
    moves_dm = links.group([(r.dm.at[chan], r.dm.at[chan], d) for d in quads])
    turn()
    for row in range(3):
        conv_weight(r.a1, r.turn, r.dw1, row)
    reduce("c", r.dw1)
    r.big[...] = dot_nt(r.o[...], r.wqg[3])

    def pack_out(at, pair, dst):
        for b in range(2):
            even, odd = unpack(*(v[:, 128 * b : 128 * b + 128] for v in pair))
            dst[2 * b, pl.ds(at, CH), :] = even.astype(BF)
            dst[2 * b + 1, pl.ds(at, CH), :] = odd.astype(BF)

    def to_y(i, held):
        at = chunk_at(i)
        pack_out(at, [(load_resid(m, at) + r.big[rows_of(m, at), :]) * live[m] for m in range(2)], r.yp)
        return held

    lax.fori_loop(0, ROWS // CH, to_y, 0)

    def data_one():
        conv_back(r.dd, r.w1g, r.h)

    def norm_one():
        back1 = norm_back(r.h, r.n1, gain1, shift1, rstd1, bd, True, r.e, 0,
                          lambda m, at, dv, held: r.dres[rows_of(m, at), :] + dv)

        def to_maps(i, held):
            at = chunk_at(i)
            pack_out(at, [back1(m, at, 0) for m in range(2)], r.mp)
            return held

        lax.fori_loop(0, ROWS // CH, to_maps, 0)
        moves_dm.wait()
        for j in range(CHAN):
            r.dl[2 * j : 2 * j + 2, :] = r.dm[j, 0:2, :]
        r.ra[dp] = r.dl[...]
        for d in others():
            moves_late.remote(r.dl, r.ra.at[dp], d)
        for b in range(2):
            block = r.e[:, 128 * b : 128 * b + 128]
            r.es[2 * b] = block
            r.es[2 * b + 1] = pltpu.roll(block, SL, 1)
        r.er[chan] = r.es[chan]
        for d in quads:
            moves_e.remote(r.es.at[d[1]], r.er.at[chan], d)

    def send_maps():
        for src, dst in ((r.yp, r.yo), (r.mp, r.mo)):
            at.results.copy(src.at[chan], dst.at[chan])
            for d in quads:
                moves_out.remote(src.at[d[1]], dst.at[chan], d)

    def send_gains():
        moves_e.wait()
        r.et[...] = r.er[0] + r.er[1] + r.er[2] + r.er[3]
        at.results.copy(r.et, r.ext.at[dp])
        for d in others():
            moves_out.remote(r.et, r.ext.at[dp], d)

    def embedding():
        mix.landed()
        moves_late.wait()
        maps = 8 * n_dp
        temb, s, tsil = embeddings(r.ta[...].reshape(maps, 128))
        rows = r.ra[...].reshape(maps, C)
        r.rt[...] = rows.T
        r.dew[...] = dot(r.rt[mine, :].astype(BF), tsil)
        dtemb = dot(rows.astype(BF), r.weg[0]) * (s * (1.0 + temb * (1.0 - s)))
        high = dtemb.astype(BF)
        r.bw[0:maps, :] = high
        r.bw[maps:, :] = (dtemb - high.astype(F32)).astype(BF)
        for src, dst in ((r.dew, r.de), (r.bw, r.both), (r.ta, r.tall)):
            at.results.copy(src, dst)

    moves_e, moves_out = links.group(), links.group()
    go(0)
    data_one()
    go(6, 4, 5, 3, 1)
    norm_one()
    go(2, 0, 4, 6)
    send_maps()
    go(1, 5, 0, 2, 3)
    send_gains()
    go(4, 6, 1, 5, 2, 0, 3)
    embedding()
    go(4, 6, 1, 5, 2, 0, 3, 1, 4, 2, 3, 6, 5)
    for item in items:
        item.finish()
    at.results.wait()
    moves_out.wait()
    links.close()


STORES = ["y", "dm", "de_out", "dq", "do", "d2", "d1", "dt"]


def finish(n_dp, names, *refs):
    r = SimpleNamespace(**dict(zip(names, refs)))
    maps = 8 * n_dp
    steps = r.dt.shape[0]
    links = Links(None, None, r.own, None)
    load = {name: links.here(getattr(r, name), getattr(r, name + "_v"))
            for name in ["yo", "mo", "tall", "both"] + list(ITEMS) + ["de", "ext"]}

    def out(name, src, index=slice(None)):
        dst = getattr(r, name)
        pltpu.make_async_copy(src.at[index], dst.at[index], r.stores.at[STORES.index(name)]).start()

    for name, dst, src, dst_v in (("yo", "y", r.yo_v, r.y_v), ("mo", "dm", r.mo_v, r.dm_v)):
        load[name].wait()
        for j in range(CHAN):
            block = src[j].astype(F32)
            dst_v[2 * j] = block[:, 0:SL].astype(BF)
            dst_v[2 * j + 1] = pltpu.roll(block, SL, 1)[:, 0:SL].astype(BF)
        out(dst, dst_v)
    load["tall"].wait()
    load["both"].wait()
    lanes = r.tall_v[...].reshape(maps, 128).T[0:1, :]
    lanes = jnp.concatenate([lanes, lanes], axis=1)
    for start in range(0, steps, 256):
        size = min(256, steps - start)
        ids = lax.broadcasted_iota(jnp.int32, (size, 2 * maps), 0).astype(F32) + float(start)
        hot = jnp.where(ids == lanes, 1.0, 0.0).astype(BF)
        r.dt_v[start : start + size, :] = dot(hot, r.both_v[...])
        out("dt", r.dt_v, slice(start, start + size))

    def whole(name, dst_v, base, taps):
        src = getattr(r, name + "_v")
        for i, t in enumerate(taps):
            for half in range(2):
                dst_v[base + i, :, 128 * half : 128 * half + 128] = src[0, half, SL * t : SL * t + SL, :].astype(F32)

    done = dict(b=0, c=0)
    for name, (taps, _, _) in ITEMS.items():
        load[name].wait()
        if name[1] == "a":
            whole(name, r.dq_v, 0, range(3))
            out("dq", r.dq_v)
            whole(name, r.do_v, 0, [3])
            out("do", r.do_v)
        else:
            key, start = dict(b="d2", c="d1")[name[1]], done[name[1]]
            dst_v = getattr(r, key + "_v")
            whole(name, dst_v, start, range(taps))
            out(key, dst_v, slice(start, start + taps))
            done[name[1]] += taps
    load["de"].wait()
    out("de_out", r.de_v)
    load["ext"].wait()
    total = r.ext_v[0]
    for i in range(1, n_dp):
        total = total + r.ext_v[i]
    for i in range(6):
        r.gains_v[i] = total[i : i + 1, 0:SL]
        pltpu.make_async_copy(r.gains_v.at[i], getattr(r, f"e{i}"), r.stores.at[len(STORES)]).start()
    for at, name in enumerate(STORES):
        src = r.de_v if name == "de_out" else getattr(r, name + "_v")
        pltpu.make_async_copy(src, getattr(r, name), r.stores.at[at]).wait()
    pltpu.make_async_copy(r.gains_v, r.gains_v, r.stores.at[len(STORES)]).wait()


def per_device(x_maps, timesteps, counts, emb_table, w_first, w_second, w_embed, w_qkv, w_out, gain_one, shift_one,
               gain_two, shift_two, gain_three, shift_three, cotangent, *, n_dp):
    team, teams = block_sizes(n_dp)
    slots, side, _, _ = x_maps.shape
    emb = w_embed.shape[0]
    steps = emb_table.shape[0]
    inputs = dict(
        x=x_maps.reshape(slots, side * side, SL), dy=cotangent.reshape(slots, side * side, SL),
        ts=timesteps, cnt=counts, table=emb_table,
        w1=jnp.swapaxes(w_first, 2, 3).reshape(9, SL, C), w2=jnp.swapaxes(w_second, 2, 3).reshape(9, SL, C),
        we=w_embed.T[None], wq=jnp.transpose(w_qkv, (1, 2, 0)), wo=w_out.T[None])
    gains = (gain_one, shift_one, gain_two, shift_two, gain_three, shift_three)
    inputs.update({name: v.reshape(1, SL) for name, v in zip(GAINS, gains)})
    anywhere = pl.BlockSpec(memory_space=pl.ANY)

    def of(shape, dtype):
        return jax.ShapeDtypeStruct(shape, dtype)

    maps = 8 * n_dp
    middle = dict(
        yo=of((CHAN, ROWS, 128), BF), mo=of((CHAN, ROWS, 128), BF), tall=of((n_dp, 8, 128), F32),
        ext=of((n_dp, 8, 128), F32), both=of((2 * maps, emb), BF), de=of((SL, emb), F32))
    middle.update({name: of((1, 2, SL * item[0], 128), BF) for name, item in ITEMS.items()})
    v = pltpu.VMEM
    maps2 = 2 * ROWS
    scratch = dict(
        xl=v((slots, ROWS, SL), BF), dyl=v((slots, ROWS, SL), BF), pin=v((len(GAINS), 1, SL), BF),
        tss=pltpu.SMEM((slots,), jnp.int32), cns=pltpu.SMEM((1,), jnp.int32), tab=v((steps, emb), BF),
        xp=v((CHAN, ROWS, 128), BF), dyp=v((CHAN, ROWS, 128), BF),
        xg=v((CHAN, ROWS, 128), BF), dyg=v((CHAN, ROWS, 128), BF),
        yp=v((CHAN, ROWS, 128), BF), mp=v((CHAN, ROWS, 128), BF),
        w1g=v((9, C, C), BF), w2g=v((9, C, C), BF), weg=v((1, C, emb), BF), wqg=v((4, C, C), BF),
        bd=v((C, C), BF), tl=v((8, 128), F32), ta=v((n_dp, 8, 128), F32), par=v((8, 128), F32),
        pg=v((CHAN, 8, 128), F32), pa=v((8, C), F32), emb=v((8, C), F32),
        wel=v((1, SL, emb), BF), el=v((8, 128), F32), eg=v((CHAN, 8, 128), F32),
        a1=v((TALL + 2 * GAP, 3 * C), BF), a2=v((TALL + 2 * GAP, 3 * C), BF), dd=v((TALL + 2 * GAP, 3 * C), BF),
        h=v((TALL, C), F32), xf=v((maps2, C), F32), n1=v((maps2, C), F32), n2=v((maps2, C), F32),
        n3=v((maps2, C), F32), dres=v((maps2, C), F32), big=v((maps2, C), F32), p=v((maps2, C), F32),
        e=v((8, C), F32), es=v((CHAN, 8, 128), F32), er=v((CHAN, 8, 128), F32), et=v((8, 128), F32),
        dm=v((CHAN, 8, C), F32), dl=v((8, C), F32), ra=v((n_dp, 8, C), F32), rt=v((C, maps), F32),
        dew=v((SL, emb), F32), bw=v((2 * maps, emb), BF), turn=v((2, ROWS, C), BF),
        dw1=v((9, C, C), BF), dw2=v((9, C, C), BF), dqo=v((4, C, C), BF))
    for name in ("a3", "q", "k", "v", "pb", "o", "g", "do", "dq", "dk", "dv"):
        scratch[name] = v((maps2, C), BF)
    for name, (taps, order, kind) in ITEMS.items():
        buffers = reduction_scratch(taps, order, kind, teams)
        scratch.update({name + "_" + k: b for k, b in buffers.items()})
    several = len(ITEMS) if teams > 1 else 0
    scratch.update(
        idle=v((4096, 128), BF), send=pltpu.SemaphoreType.DMA((SENDS + several,)),
        recv=pltpu.SemaphoreType.DMA((GROUPS_OF_COPIES + several,)), own=pltpu.SemaphoreType.DMA((9 + several,)),
        gains=pltpu.SemaphoreType.DMA(()))
    got = pl.pallas_call(
        functools.partial(mega, n_dp, list(inputs) + list(middle) + list(scratch)),
        out_shape=tuple(middle.values()),
        in_specs=[anywhere] * len(inputs),
        out_specs=(anywhere,) * len(middle),
        scratch_shapes=list(scratch.values()),
        compiler_params=pltpu.CompilerParams(collective_id=0, has_side_effects=True, vmem_limit_bytes=60 << 20),
        name="blocks",
    )(*inputs.values())
    results = dict(
        y=of((slots, ROWS, SL), BF), dm=of((slots, ROWS, SL), BF), dt=of((steps, emb), F32), d1=of((9, SL, C), F32),
        d2=of((9, SL, C), F32), de_out=of((SL, emb), F32), dq=of((3, SL, C), F32), do=of((1, SL, C), F32))
    results.update({f"e{i}": of((1, SL), F32) for i in range(6)})
    scratch = {name + "_v": v(o.shape, o.dtype) for name, o in middle.items()}
    scratch.update({name + "_v": v(o.shape, o.dtype) for name, o in results.items() if name[0] != "e"})
    scratch.update(
        gains_v=v((6, 1, SL), F32), own=pltpu.SemaphoreType.DMA((len(middle),)),
        stores=pltpu.SemaphoreType.DMA((len(STORES) + 1,)))
    got = pl.pallas_call(
        functools.partial(finish, n_dp, list(middle) + list(results) + list(scratch)),
        out_shape=tuple(results.values()),
        in_specs=[anywhere] * len(middle),
        out_specs=(anywhere,) * len(results),
        scratch_shapes=list(scratch.values()),
        compiler_params=pltpu.CompilerParams(vmem_limit_bytes=60 << 20),
        name="finish",
    )(*got)
    got = dict(zip(results, got))
    return (
        got["y"].reshape(x_maps.shape), got["dm"].reshape(x_maps.shape), got["dt"],
        jnp.swapaxes(got["d1"].reshape(3, 3, SL, C), 2, 3), jnp.swapaxes(got["d2"].reshape(3, 3, SL, C), 2, 3),
        got["de_out"].T, jnp.transpose(got["dq"], (2, 0, 1)), got["do"].reshape(SL, C).T,
    ) + tuple(got[f"e{i}"].reshape(SL) for i in range(6))


def solution(mesh):
    weights = (P(None, None, None, "chan"), P(None, None, None, "chan"), P(None, "chan"), P(None, None, "chan"),
               P(None, "chan")) + (P("chan"),) * 6
    maps = P("dp", None, None, "chan")
    return jax.shard_map(
        functools.partial(per_device, n_dp=mesh.shape["dp"]), mesh=mesh,
        in_specs=(maps, P("dp"), P("dp"), P()) + weights + (maps,),
        out_specs=(maps, maps, P()) + weights, check_vma=False)
```
